128 devices in a mesh: dp: 16 (over y_lo, z, core), fsdp: 8 (over y_hi, x).
Axes of the slice: x: 4, y: 4 (y_hi: 2, y_lo: 2; y = y_hi * 2 + y_lo), z: 4, core: 2. Of those that a mesh axis runs over, the one named last changes fastest.
Arguments:
- context: bfloat16 [65536, 1024], P(('dp', 'fsdp')), may hold values from -6 to 6
- residual: bfloat16 [65536, 2048], P(('dp', 'fsdp')), may hold values from -6 to 6
- out_weight: bfloat16 [1024, 2048], P('fsdp'), may hold values from -0.1875 to 0.1875
- norm_gain: float32 [2048], replicated, may hold values from 0.5 to 1.5
- user_vectors: bfloat16 [1024, 2048], P(('dp', 'fsdp')), may hold values from -12 to 12
- positive: int32 [1024], P(('dp', 'fsdp')), may hold values from 0 to 255
- item_ids: int32 [256], P(('dp', 'fsdp')), may hold values from 0 to 127
- item_counts: int32 [256], P(('dp', 'fsdp')), may hold values from 1 to 5000
- lengths: int32 [256], P(('dp', 'fsdp')), may hold values from 64 to 256
Outputs:
- mean_loss: float32 [], replicated
- residual_grad: bfloat16 [65536, 2048], P(('dp', 'fsdp'))
- context_grad: bfloat16 [65536, 1024], P(('dp', 'fsdp'))
- weight_grad: bfloat16 [1024, 2048], P('fsdp')
- norm_gain_grad: float32 [2048], replicated
- user_grad: bfloat16 [1024, 2048], P(('dp', 'fsdp'))
The draws below stay inside these ranges and needn't reach their ends.
All inputs are finite; a program needn't handle non-finite values.
Results may differ from the reference program's by a relative error of at most 0.015.
Values may be sent and summed in bfloat16 or wider, within the bound.
No kernel may reach another device: no remote copies, remote signals or barrier semaphores. Data moves between devices by JAX's collectives and lax.ppermute only.
A program may use at most 128 MiB of HBM per device.

```python
import math
import jax
import jax.numpy as jnp
import numpy as np
from jax import lax

D = 2048
H = 1024
LENGTH = 256
ITEMS = 256
USER_COUNT = 1024
TOKENS = 65536


def draw_user_vectors(key, part):
    key_normal = jax.random.fold_in(key, 11)
    row_index = jnp.arange(USER_COUNT, dtype=jnp.float32)
    row_factor = 0.05 * (1.0 + 2.0 * row_index / max(USER_COUNT - 1, 1))
    normed_share = jax.random.normal(key_normal, (USER_COUNT, D), jnp.float32)
    value_rows = normed_share * row_factor[:, None]
    return jnp.clip(value_rows, -12.0, 12.0).astype(jnp.bfloat16)


def plant(entries, key, smallest, largest):
    longest = entries.shape.index(max(entries.shape))
    spots = []
    for shift in (0, 1):
        where = [jax.random.randint(jax.random.fold_in(key, axis), (), 0, length) for axis, length in enumerate(entries.shape)]
        where[longest] = (where[longest] + shift) % entries.shape[longest]
        spots.append(tuple(where))
    return entries.at[spots[0]].set(smallest).at[spots[1]].set(largest)


def shard_levels(stream_key, extent, split, low, high):
    loudness = 1.0
    for axis_at, blocks in split:
        draws = jax.random.uniform(jax.random.fold_in(jax.random.fold_in(stream_key, 6), axis_at), (blocks,), jnp.float32, low / len(split), high / len(split))
        loudness = loudness * jnp.repeat(jnp.exp(draws), extent[axis_at] // blocks).reshape((-1,) + (1,) * (len(extent) - 1 - axis_at))
    return loudness


def rank_table(count, slope):
    loads = [(1 << 20) // math.isqrt(rank ** slope) + 1 for rank in range(1, count + 1)]
    spread = 1 + sum(loads) // (1 << 30)
    return np.cumsum(np.array([max(1, weight // spread) for weight in loads]))


def ranked_ids(own_key, shape, number_of, skew):
    listing = rank_table(number_of, skew)
    pick = jax.random.randint(jax.random.fold_in(own_key, 1), shape, 0, int(listing[number_of - 1]))
    grade = jnp.searchsorted(jnp.asarray(listing, jnp.int32), pick, side="right")
    return jax.random.permutation(jax.random.fold_in(own_key, 2), number_of)[grade].astype(jnp.int32)


def gaussian(stream_key, dims, scale, limit, cuts=(), kind=jnp.bfloat16):
    entries = jax.random.normal(stream_key, dims, jnp.float32) * scale
    if len(cuts) > 0:
        entries = shard_levels(stream_key, dims, cuts, -0.22, 0.18) * entries
    return jnp.clip(entries, min=-limit, max=limit).astype(kind)


def setup_inputs(seed: int = 0) -> dict:
    splits = jax.random.split(jax.random.key(seed), 10)
    context = gaussian(splits[0], (TOKENS, H), 1.0, 6.0, ((0, 128),))
    residual = gaussian(splits[1], (TOKENS, D), 1.0, 6.0, ((0, 128),))
    out_weight = gaussian(splits[2], (H, D), H ** -0.5, 0.1875, ((0, 8),))
    norm_gain = jnp.clip(1.0 + 0.1 * jax.random.normal(splits[3], (D,), jnp.float32), 0.5, 1.5)
    user_vectors = draw_user_vectors(jax.random.fold_in(splits[9], 71), 0)
    positive = plant(jax.random.randint(splits[5], (USER_COUNT,), 0, ITEMS), jax.random.fold_in(splits[5], 1), 0, ITEMS - 1).astype(jnp.int32)
    item_ids = plant(ranked_ids(splits[6], (ITEMS,), ITEMS // 2, 2), jax.random.fold_in(splits[6], 3), 0, (ITEMS // 2) - 1).astype(jnp.int32)
    item_counts = plant(jax.random.randint(splits[7], (ITEMS,), 1, 5001), jax.random.fold_in(splits[7], 1), 1, 5000).astype(jnp.int32)
    lengths = plant(jax.random.randint(splits[8], (ITEMS,), LENGTH // 4, LENGTH + 1), jax.random.fold_in(splits[8], 1), LENGTH // 4, LENGTH).astype(jnp.int32)
    return dict(context=context, residual=residual, out_weight=out_weight, norm_gain=norm_gain, user_vectors=user_vectors, positive=positive, item_ids=item_ids, item_counts=item_counts, lengths=lengths)


EPSILON = 1e-06
MASKED_FILL = -1e+30

def stream_of(context_rows, residual_rows, out_weight, norm_gain):
    attended = jnp.dot(context_rows, out_weight, preferred_element_type=jnp.float32)
    stream = residual_rows.astype(jnp.float32) + attended
    inverse_root_mean = lax.rsqrt(lax.optimization_barrier(jnp.mean(stream * stream, axis=-1, keepdims=True)) + EPSILON)
    return (stream, inverse_root_mean, stream * inverse_root_mean * norm_gain)

def reference(context, residual, out_weight, norm_gain, user_vectors, positive, item_ids, item_counts, lengths):
    context_items = context.reshape(ITEMS, LENGTH, H)
    residual_items = residual.reshape(ITEMS, LENGTH, D)
    positions = jnp.arange(LENGTH, dtype=jnp.int32)

    def pool_item(packed):
        context_rows, residual_rows, length_here = packed
        stream, inverse_root_mean, normed = stream_of(context_rows, residual_rows, out_weight, norm_gain)
        inside = (positions < length_here)[:, None]
        return lax.optimization_barrier(jnp.sum(jnp.where(inside, normed, 0.0), axis=0)) / length_here.astype(jnp.float32)
    pooled = lax.map(pool_item, (context_items, residual_items, lengths))
    emb_scale = lax.rsqrt(lax.optimization_barrier(jnp.mean(pooled * pooled, axis=-1, keepdims=True)) + EPSILON)
    embedding = (pooled * emb_scale).astype(jnp.bfloat16)
    scores = jnp.dot(user_vectors, embedding.T, preferred_element_type=jnp.float32)
    columns = jnp.arange(ITEMS, dtype=jnp.int32)
    onehot = columns[None, :] == positive[:, None]
    positive_id = lax.optimization_barrier(jnp.sum(jnp.where(onehot, item_ids[None, :], 0), axis=1))
    excluded = (item_ids[None, :] == positive_id[:, None]) & jnp.logical_not(onehot)
    log_counts = jnp.log(item_counts.astype(jnp.float32))
    logits = jnp.where(excluded, MASKED_FILL, scores - log_counts[None, :])
    row_max = lax.optimization_barrier(jnp.max(logits, axis=1, keepdims=True))
    weights = jnp.where(excluded, 0.0, jnp.exp(logits - row_max))
    row_total = lax.optimization_barrier(jnp.sum(weights, axis=1, keepdims=True))
    log_total = row_max[:, 0] + jnp.log(row_total[:, 0])
    picked = lax.optimization_barrier(jnp.sum(jnp.where(onehot, logits, 0.0), axis=1))
    mean_loss = jnp.mean(log_total - picked)
    logit_grad = (weights / row_total - onehot.astype(jnp.float32)).astype(jnp.bfloat16)
    user_grad = jnp.dot(logit_grad, embedding, preferred_element_type=jnp.float32).astype(jnp.bfloat16)
    emb_grad = jnp.dot(logit_grad.T, user_vectors, preferred_element_type=jnp.float32)
    pooled_grad = emb_scale * emb_grad - pooled * emb_scale ** 3 * lax.optimization_barrier(jnp.mean(pooled * emb_grad, axis=-1, keepdims=True))

    def backward_item(carried, packed):
        weight_sum, gain_sum = carried
        context_rows, residual_rows, length_here, grad_row = packed
        stream, inverse_root_mean, normed = stream_of(context_rows, residual_rows, out_weight, norm_gain)
        inside = (positions < length_here)[:, None]
        normed_grad = jnp.where(inside, grad_row[None, :] / length_here.astype(jnp.float32), 0.0)
        gain_sum = gain_sum + lax.optimization_barrier(jnp.sum(normed_grad * stream * inverse_root_mean, axis=0))
        scaled = norm_gain * normed_grad
        stream_grad = inverse_root_mean * scaled - stream * inverse_root_mean ** 3 * lax.optimization_barrier(jnp.mean(scaled * stream, axis=-1, keepdims=True))
        residual_grad = stream_grad.astype(jnp.bfloat16)
        context_grad = jnp.dot(residual_grad, out_weight.T, preferred_element_type=jnp.float32).astype(jnp.bfloat16)
        weight_sum = weight_sum + jnp.dot(context_rows.T, residual_grad, preferred_element_type=jnp.float32)
        return ((weight_sum, gain_sum), (residual_grad, context_grad))
    start_sums = (jnp.zeros((H, D), jnp.float32), jnp.zeros((D,), jnp.float32))
    final_sums, outputs = lax.scan(backward_item, start_sums, (context_items, residual_items, lengths, pooled_grad))
    weight_sum, gain_sum = final_sums
    residual_grad = outputs[0].reshape(TOKENS, D)
    context_grad = outputs[1].reshape(TOKENS, H)
    return (mean_loss, residual_grad, context_grad, weight_sum.astype(jnp.bfloat16), gain_sum, user_grad)
```

```python
import jax
import jax.numpy as jnp
from jax import lax
from jax.sharding import PartitionSpec as P

EPSILON = 1e-06
MASKED_FILL = -1e30
AXES = ("dp", "fsdp")
F32 = jnp.float32
BF16 = jnp.bfloat16


def linear(x, y, z, c):
    return ((((y % 2) * 4 + z) * 2 + c) * 2 + y // 2) * 4 + x


def move(value, where):
    perm = []
    for x in range(4):
        for y in range(4):
            for z in range(4):
                for c in range(2):
                    perm.append((linear(x, y, z, c), linear(*where(x, y, z, c))))
    return lax.ppermute(value, AXES, perm)


def shift(value, axis, k):
    if axis == "x":
        return move(value, lambda x, y, z, c: ((x + k) % 4, y, z, c))
    if axis == "y":
        return move(value, lambda x, y, z, c: (x, (y + k) % 4, z, c))
    return move(value, lambda x, y, z, c: (x, y, (z + k) % 4, c))


def swap_core(value):
    return move(value, lambda x, y, z, c: (x, y, z, 1 - c))


def swap_y_hi(value):
    return move(value, lambda x, y, z, c: (x, 3 - y, z, c))


def swap_y_lo(value):
    return move(value, lambda x, y, z, c: (x, y ^ 1, z, c))


def put(pieces, indices):
    out = jnp.zeros((len(pieces),) + pieces[0].shape, pieces[0].dtype)
    for piece, index in zip(pieces, indices):
        out = lax.dynamic_update_index_in_dim(out, piece, index, 0)
    return out


def gather_ring(value, axis, at):
    pieces = [value] + [shift(value, axis, k) for k in (1, 2, 3)]
    return put(pieces, [(at - k) % 4 for k in range(4)])


def gather_pair(value, other, at):
    return put([value, other], [at, 1 - at])


def scatter_ring(blocks, axis, at):
    def block(j):
        return lax.dynamic_index_in_dim(blocks, j % 4, 0, keepdims=False)

    arrived = [shift(block(at + k).astype(BF16), axis, k) for k in (1, 2, 3)]
    total = block(at).astype(F32)
    for piece in arrived:
        total = total + piece.astype(F32)
    return total


def scatter_pair(blocks, swap, at):
    arrived = swap(lax.dynamic_index_in_dim(blocks, 1 - at, 0, keepdims=False).astype(BF16))
    return lax.dynamic_index_in_dim(blocks, at, 0, keepdims=False).astype(F32) + arrived.astype(F32)


def contract_rows(left, right):
    return lax.dot_general(left, right, (((0,), (0,)), ((), ())), preferred_element_type=F32)


def contract_last(left, right):
    return lax.dot_general(left, right, (((1,), (1,)), ((), ())), preferred_element_type=F32)


def on_device(
    context, residual, out_weight, norm_gain, user_vectors, positive, item_ids, item_counts, lengths
):
    tok_rows, head_width = context.shape
    width = residual.shape[1]
    items_here = lengths.shape[0]
    item_length = tok_rows // items_here
    users_here = user_vectors.shape[0]
    dp, fsdp = lax.axis_index("dp"), lax.axis_index("fsdp")
    y_lo, z, core = dp // 8, (dp // 2) % 4, dp % 2
    y_hi, x = fsdp // 4, fsdp % 4
    y = y_hi * 2 + y_lo
    half = width // 2
    part = half // 2
    rows = out_weight.shape[0]

    mine = lax.dynamic_slice(out_weight, (0, core * half), (rows, half))
    first = gather_ring(mine[:, :part], "x", x)
    second = gather_pair(mine[:, part:], swap_y_hi(mine[:, part:]), y_hi)
    first = gather_pair(first, swap_y_hi(first), y_hi).reshape(head_width, part)
    second = gather_ring(second, "x", x)
    second = jnp.transpose(second, (1, 0, 2, 3)).reshape(head_width, part)
    first_other, second_other = swap_core(first), swap_core(second)
    is_zero = core == 0
    weight = jnp.concatenate(
        [
            jnp.where(is_zero, first, first_other),
            jnp.where(is_zero, second, second_other),
            jnp.where(is_zero, first_other, first),
            jnp.where(is_zero, second_other, second),
        ],
        axis=1,
    )

    labels = jnp.stack([item_ids, item_counts // 128, item_counts % 128], axis=1)
    labels = jnp.pad(labels, ((0, users_here - items_here), (0, 0)))
    labels = jnp.concatenate([positive[:, None], labels], axis=1)
    labels = jnp.pad(labels, ((0, 0), (0, 124))).astype(BF16)
    users = jnp.concatenate([user_vectors, labels], axis=1)
    users = gather_ring(users, "x", x)
    users = gather_ring(users, "y", y)
    users = gather_ring(users, "z", z)
    users = gather_pair(users, swap_core(users), core)
    users = users.reshape(128, users_here, width + 128)
    items_labels = users[:, :items_here, width + 1 : width + 4].reshape(128 * items_here, 3)
    ids_all = items_labels[:, 0]
    counts_all = items_labels[:, 1].astype(F32) * 128.0 + items_labels[:, 2].astype(F32)
    users = users.reshape(128 * users_here, width + 128)
    positive_all = users[:, width].astype(jnp.int32)
    users_all = users[:, :width]

    attended = jnp.dot(context, weight, preferred_element_type=F32)
    stream = residual.astype(F32) + attended
    inverse = lax.rsqrt(jnp.mean(stream * stream, axis=-1, keepdims=True) + EPSILON)
    positions = jnp.arange(item_length, dtype=jnp.int32)
    inside = (positions[None, :] < lengths[:, None])[:, :, None]
    length_float = lengths.astype(F32)[:, None]
    normed = (stream * inverse).reshape(items_here, item_length, width)
    pooled = jnp.sum(jnp.where(inside, normed, 0.0), axis=1) * norm_gain / length_float
    emb_scale = lax.rsqrt(jnp.mean(pooled * pooled, axis=-1, keepdims=True) + EPSILON)
    embedding = (pooled * emb_scale).astype(BF16)

    emb = gather_ring(embedding, "x", x)
    emb = gather_ring(emb, "y", y)
    emb = gather_ring(emb, "z", z)
    emb = gather_pair(emb, swap_core(emb), core)
    emb_all = emb.reshape(128 * items_here, width)

    place = jnp.arange(128 * items_here, dtype=jnp.int32)
    chip = place // items_here
    px, py, pz, pc = chip % 4, (chip // 4) % 4, (chip // 16) % 4, chip // 64
    item_index = linear(px, py, pz, pc) * items_here + place % items_here
    onehot = item_index[None, :] == positive_all[:, None]
    positive_id = jnp.sum(jnp.where(onehot, ids_all[None, :].astype(F32), 0.0), axis=1)
    excluded = (ids_all[None, :].astype(F32) == positive_id[:, None]) & jnp.logical_not(onehot)
    scores = contract_last(users_all, emb_all)
    logits = jnp.where(excluded, MASKED_FILL, scores - jnp.log(counts_all)[None, :])
    row_max = jnp.max(logits, axis=1, keepdims=True)
    weights = jnp.where(excluded, 0.0, jnp.exp(logits - row_max))
    row_total = jnp.sum(weights, axis=1, keepdims=True)
    log_total = row_max[:, 0] + jnp.log(row_total[:, 0])
    mean_loss = jnp.mean(log_total - jnp.sum(jnp.where(onehot, logits, 0.0), axis=1))
    logit_grad = (weights / row_total - onehot.astype(F32)).astype(BF16)
    here = ((core * 4 + z) * 4 + y) * 4 + x
    user_grad = jnp.dot(
        lax.dynamic_slice_in_dim(logit_grad, here * users_here, users_here, 0),
        emb_all,
        preferred_element_type=F32,
    ).astype(BF16)
    emb_grad_all = contract_rows(logit_grad, users_all)
    emb_float = emb_all.astype(F32)
    emb_dot = jnp.mean(emb_float * emb_grad_all, axis=-1, keepdims=True)
    gain_grad = jnp.sum(emb_float * emb_grad_all - emb_float * emb_float * emb_dot, axis=0) / norm_gain
    emb_grad = lax.dynamic_slice_in_dim(emb_grad_all, here * items_here, items_here, 0)
    pooled_grad = emb_scale * emb_grad - pooled * emb_scale**3 * jnp.mean(
        pooled * emb_grad, axis=-1, keepdims=True
    )

    item_grad = norm_gain * pooled_grad / length_float
    scaled = jnp.where(inside, item_grad[:, None, :], 0.0).reshape(tok_rows, width)
    stream_grad = inverse * scaled - stream * inverse**3 * jnp.mean(
        scaled * stream, axis=-1, keepdims=True
    )
    residual_grad = stream_grad.astype(BF16)

    def product(which):
        return contract_rows(
            context, lax.dynamic_slice(residual_grad, (0, which * half), (tok_rows, half))
        )

    other_half = swap_core(product(1 - core).astype(BF16))
    context_grad = contract_last(residual_grad, weight).astype(BF16)
    total = product(core) + other_half.astype(F32)
    blocks = total.reshape(2, 4, rows, half)
    first, second = blocks[..., :part], blocks[..., part:]
    first = scatter_pair(first, swap_y_hi, y_hi)
    second = scatter_ring(jnp.transpose(second, (1, 0, 2, 3)), "x", x)
    first = scatter_ring(first, "x", x)
    second = scatter_pair(second, swap_y_hi, y_hi)
    quarter = half // 4
    own = jnp.concatenate([first, second], axis=1).reshape(rows, 4, quarter)
    own = scatter_ring(jnp.transpose(own, (1, 0, 2)), "z", z)
    own = lax.reduce_precision(own, 8, 7)
    own = (own + swap_y_lo(own.astype(BF16)).astype(F32)).astype(BF16)
    own = gather_ring(own, "z", z)
    own = gather_pair(own, swap_core(own), core)
    weight_grad = jnp.transpose(own.reshape(8, rows, quarter), (1, 0, 2)).reshape(rows, width)
    return (mean_loss, residual_grad, context_grad, weight_grad, gain_grad, user_grad)


def solution(mesh):
    placed = (
        P(AXES, None),
        P(AXES, None),
        P("fsdp", None),
        P(),
        P(AXES, None),
        P(AXES),
        P(AXES),
        P(AXES),
        P(AXES),
    )
    return jax.shard_map(
        on_device,
        mesh=mesh,
        in_specs=placed,
        out_specs=(P(), P(AXES, None), P(AXES, None), P("fsdp", None), P(), P(AXES, None)),
        check_vma=False,
    )
```

```python
import functools

import jax
import jax.numpy as jnp
from jax import lax
from jax.experimental import pallas as pl
from jax.experimental.pallas import tpu as pltpu
from jax.sharding import PartitionSpec as P

EPSILON = 1e-06
MASKED_FILL = -1e30
AXES = ("dp", "fsdp")
F32 = jnp.float32
BF16 = jnp.bfloat16
VMEM = pl.BlockSpec(memory_space=pltpu.VMEM)
SMEM = pl.BlockSpec(memory_space=pltpu.SMEM)
ANY = pl.BlockSpec(memory_space=pl.ANY)
PARAMS = pltpu.CompilerParams(vmem_limit_bytes=56 * 1024 * 1024)
DEVICES = 128
LABELS = 128


def linear(x, y, z, c):
    return ((((y % 2) * 4 + z) * 2 + c) * 2 + y // 2) * 4 + x


def move(value, where):
    perm = []
    for x in range(4):
        for y in range(4):
            for z in range(4):
                for c in range(2):
                    perm.append((linear(x, y, z, c), linear(*where(x, y, z, c))))
    return lax.ppermute(value, AXES, perm)


def shift(value, axis, k):
    if axis == "x":
        return move(value, lambda x, y, z, c: ((x + k) % 4, y, z, c))
    if axis == "y":
        return move(value, lambda x, y, z, c: (x, (y + k) % 4, z, c))
    return move(value, lambda x, y, z, c: (x, y, (z + k) % 4, c))


def swap_core(value):
    return move(value, lambda x, y, z, c: (x, y, z, 1 - c))


def swap_y_hi(value):
    return move(value, lambda x, y, z, c: (x, 3 - y, z, c))


def swap_y_lo(value):
    return move(value, lambda x, y, z, c: (x, y ^ 1, z, c))


def swap_z(value, bits):
    return move(value, lambda x, y, z, c: (x, y, z ^ bits, c))


def ring(value, axis):
    return [value] + [shift(value, axis, k) for k in (1, 2, 3)]


def put(pieces, at):
    out = jnp.zeros((4,) + pieces[0].shape, pieces[0].dtype)
    for k, piece in enumerate(pieces):
        out = lax.dynamic_update_index_in_dim(out, piece, (at - k) % 4, 0)
    return out


def dot(left, right):
    return jnp.dot(left, right, preferred_element_type=F32)


def contract_rows(left, right):
    return lax.dot_general(left, right, (((0,), (0,)), ((), ())), preferred_element_type=F32)


def contract_last(left, right):
    return lax.dot_general(left, right, (((1,), (1,)), ((), ())), preferred_element_type=F32)


def column_offsets(core, width):
    half, part = width // 2, width // 4
    mine = pl.multiple_of(core * half, half)
    other = pl.multiple_of((1 - core) * half, half)
    return (
        (mine, pl.multiple_of(mine + part, part)),
        (other, pl.multiple_of(other + part, part)),
    )


def forward_kernel(where, lengths, context, residual, gain, *refs):
    a_refs, b_refs = (refs[0:2], refs[2:4]), (refs[4:8], refs[8:12])
    stream, inverse, pooled, embedding = refs[12:]
    tokens, width = residual.shape
    part = width // 4
    head = context.shape[1]
    block = head // 8
    items = lengths.shape[0]
    length = tokens // items
    for side, (first_at, second_at) in enumerate(column_offsets(where[3], width)):
        acc = residual[:, pl.ds(first_at, part)].astype(F32)
        for yrel in range(2):
            acc = acc + dot(
                context[:, yrel * 4 * block : (yrel + 1) * 4 * block],
                a_refs[side][yrel][...].reshape(4 * block, part),
            )
        stream[:, pl.ds(first_at, part)] = acc
        acc = residual[:, pl.ds(second_at, part)].astype(F32)
        for k in range(4):
            columns = jnp.concatenate(
                [
                    context[:, k * block : (k + 1) * block],
                    context[:, (4 + k) * block : (5 + k) * block],
                ],
                axis=1,
            )
            acc = acc + dot(columns, b_refs[side][k][...].reshape(2 * block, part))
        stream[:, pl.ds(second_at, part)] = acc
    for i in range(items):
        rows = stream[i * length : (i + 1) * length, :]
        inv = lax.rsqrt(jnp.mean(rows * rows, axis=-1, keepdims=True) + EPSILON)
        inverse[i * length : (i + 1) * length, :] = inv
        position = lax.broadcasted_iota(jnp.int32, (length, 1), 0)
        kept = jnp.where(position < lengths[i], inv, 0.0)
        total = jnp.sum(rows * kept, axis=0, keepdims=True)
        pool = total * gain[...] / lengths[i].astype(F32)
        pooled[i : i + 1, :] = pool
    pool = pooled[...]
    scale = lax.rsqrt(jnp.mean(pool * pool, axis=-1, keepdims=True) + EPSILON)
    embedding[...] = (pool * scale).astype(BF16)


def loss_kernel(users_here, where, lengths, gain, pooled, *refs):
    user_refs, emb_refs = refs[:8], refs[8:16]
    loss, gain_grad, item_grad, user_grad = refs[16:20]
    users, placed, grads, emb_grads, user_sem, emb_sem = refs[20:]
    x, y, z, core = where[0], where[1], where[2], where[3]
    group, width = emb_refs[0].shape
    chunk = user_refs[0].shape[0]
    items = 8 * group
    items_here = lengths.shape[0]
    people = users.shape[0]
    copies = []
    for n in range(8):
        side, k = n // 4, n % 4
        c = core if side == 0 else 1 - core
        at = c * 4 + (z - k + 4) % 4
        copies.append(
            pltpu.make_async_copy(
                emb_refs[n], placed.at[pl.ds(pl.multiple_of(at * group, group), group)], emb_sem.at[n]
            )
        )
        copies.append(
            pltpu.make_async_copy(
                user_refs[n], users.at[pl.ds(pl.multiple_of(at * chunk, chunk), chunk)], user_sem.at[n]
            )
        )
    for copy in copies:
        copy.start()
    to = lax.broadcasted_iota(jnp.int32, (items, items), 0)
    of = lax.broadcasted_iota(jnp.int32, (items, items), 1)
    per = group // items_here
    to_chip, of_chip = (to // items_here) % per, (of // items_here) % per
    turned = (
        ((y - of_chip // 4 + 4) % 4 == to_chip // 4)
        & ((x - of_chip % 4 + 4) % 4 == to_chip % 4)
        & (to // group == of // group)
        & (to % items_here == of % items_here)
    )
    turn = jnp.where(turned, 1.0, 0.0).astype(BF16)
    for copy in copies:
        copy.wait()
    emb = dot(turn, placed[...]).astype(BF16)
    labels = users[:, width : width + LABELS]
    person = lax.broadcasted_iota(jnp.int32, (people, items), 0)
    item = lax.broadcasted_iota(jnp.int32, (people, items), 1)
    holder = jnp.where(
        person == (item // items_here) * users_here + item % items_here, 1.0, 0.0
    ).astype(BF16)
    item_labels = contract_rows(labels, holder)
    ids = item_labels[1:2, :]
    log_counts = jnp.log(item_labels[2:3, :] * 128.0 + item_labels[3:4, :])
    chip = lax.broadcasted_iota(jnp.int32, (1, items), 1) // items_here
    which = lax.broadcasted_iota(jnp.int32, (1, items), 1) % items_here
    index = linear(chip % 4, (chip // 4) % 4, (chip // 16) % 4, chip // 64) * items_here + which
    index = index.astype(F32)
    positive = labels[:, 0:1].astype(F32)
    onehot = index == positive
    positive_id = jnp.sum(jnp.where(onehot, ids, 0.0), axis=1, keepdims=True)
    excluded = (ids == positive_id) & jnp.logical_not(onehot)
    scores = contract_last(users[:, :width], emb)
    logits = jnp.where(excluded, MASKED_FILL, scores - log_counts)
    row_max = jnp.max(logits, axis=1, keepdims=True)
    weights = jnp.where(excluded, 0.0, jnp.exp(logits - row_max))
    row_total = jnp.sum(weights, axis=1, keepdims=True)
    picked = jnp.sum(jnp.where(onehot, logits, 0.0), axis=1, keepdims=True)
    losses = row_max + jnp.log(row_total) - picked
    loss[...] = jnp.sum(losses, axis=0, keepdims=True) / people
    grad = (weights / row_total - jnp.where(onehot, 1.0, 0.0)).astype(BF16)
    grads[...] = grad.astype(F32)
    here = ((core * 4 + z) * 4 + y) * 4 + x
    own = grads[pl.ds(pl.multiple_of(here * users_here, users_here), users_here), :].astype(BF16)
    user_grad[...] = dot(own, emb).astype(BF16)
    all_grads = contract_rows(grad, users[:, :width])
    emb_grads[...] = all_grads
    emb_float = emb.astype(F32)
    product = emb_float * all_grads
    mean = jnp.mean(product, axis=-1, keepdims=True)
    gain_sum = jnp.sum(product - emb_float * emb_float * mean, axis=0, keepdims=True)
    gain_grad[...] = gain_sum / gain[...]
    first = here * items_here
    near = emb_grads[pl.ds(pl.multiple_of((first // 8) * 8, 8), 8), :]
    line = lax.broadcasted_iota(jnp.int32, (8, 1), 0)
    for i in range(items_here):
        mine = jnp.sum(jnp.where(line == first % 8 + i, near, 0.0), axis=0, keepdims=True)
        pool = pooled[i : i + 1, :]
        scale = lax.rsqrt(jnp.mean(pool * pool, axis=-1, keepdims=True) + EPSILON)
        pool_grad = scale * mine - pool * scale * scale * scale * jnp.mean(
            pool * mine, axis=-1, keepdims=True
        )
        item_grad[i : i + 1, :] = gain[...] * pool_grad / lengths[i].astype(F32)


def residual_kernel(where, lengths, stream, inverse, item_grad, residual_grad, send):
    tokens, width = stream.shape
    half = width // 2
    items = lengths.shape[0]
    length = tokens // items
    for i in range(items):
        span = slice(i * length, (i + 1) * length)
        rows = stream[span, :]
        inv = inverse[span, :]
        position = lax.broadcasted_iota(jnp.int32, (length, 1), 0)
        kept = jnp.where(position < lengths[i], inv, 0.0)
        row = item_grad[i : i + 1, :]
        mean = jnp.mean(rows * row, axis=-1, keepdims=True)
        residual_grad[span, :] = (kept * row - rows * (kept * inv * inv * mean)).astype(BF16)
    send[...] = residual_grad[:, pl.ds(pl.multiple_of((1 - where[3]) * half, half), half)]


def context_kernel(where, residual_grad, *refs):
    a_refs, b_refs = (refs[0:2], refs[2:4]), (refs[4:8], refs[8:12])
    context_grad = refs[12]
    tokens, width = residual_grad.shape
    part = width // 4
    block = context_grad.shape[1] // 8
    offsets = column_offsets(where[3], width)
    firsts = [residual_grad[:, pl.ds(first, part)] for first, _ in offsets]
    seconds = [residual_grad[:, pl.ds(second, part)] for _, second in offsets]
    from_a = []
    for yrel in range(2):
        from_a.append(
            sum(
                contract_last(firsts[side], a_refs[side][yrel][...].reshape(4 * block, part))
                for side in range(2)
            )
        )
    x, y_hi = where[0], where[1] // 2
    for k in range(4):
        from_b = sum(
            contract_last(seconds[side], b_refs[side][k][...].reshape(2 * block, part))
            for side in range(2)
        )
        for yrel in range(2):
            value = (
                from_a[yrel][:, k * block : (k + 1) * block]
                + from_b[:, yrel * block : (yrel + 1) * block]
            )
            y_to = y_hi if yrel == 0 else 1 - y_hi
            at = pl.multiple_of((y_to * 4 + (x - k + 4) % 4) * block, block)
            context_grad[:, pl.ds(at, block)] = value.astype(BF16)


def blocks_kernel(where, own_context, peer_context, residual_grad, peer_grad, *refs):
    tokens, width = residual_grad.shape
    half, part = width // 2, width // 4
    block = own_context.shape[0] // 8
    first_at, second_at = column_offsets(where[3], width)[0]

    def product(yrel, at, peer_at):
        span = slice(yrel * 4 * block, (yrel + 1) * 4 * block)
        return dot(own_context[span, :], residual_grad[:, pl.ds(at, part)]) + dot(
            peer_context[span, :], peer_grad[:, peer_at : peer_at + part]
        )

    if len(refs) == 1:
        refs[0][...] = product(0, first_at, 0)
        return
    first_send, kept = refs[0], refs[1]
    first_send[...] = product(1, first_at, 0).astype(BF16)
    for yrel in range(2):
        both = product(yrel, second_at, part)
        kept[yrel] = both[:block]
        for k in (1, 2, 3):
            refs[1 + k][yrel] = both[k * block : (k + 1) * block].astype(BF16)


def shaped(shape, dtype=F32):
    return jax.ShapeDtypeStruct(shape, dtype)


def on_device(
    context, residual, out_weight, norm_gain, user_vectors, positive, item_ids, item_counts, lengths
):
    tokens, head = context.shape
    width = residual.shape[1]
    items_here = lengths.shape[0]
    users_here = user_vectors.shape[0]
    dp, fsdp = lax.axis_index("dp"), lax.axis_index("fsdp")
    y_lo, z, core = dp // 8, (dp // 2) % 4, dp % 2
    y_hi, x = fsdp // 4, fsdp % 4
    y = y_hi * 2 + y_lo
    where = jnp.stack([x, y, z, core]).astype(jnp.int32)
    half, part = width // 2, width // 4
    rows = out_weight.shape[0]
    gain = norm_gain[None, :]

    mine = lax.dynamic_slice(out_weight, (0, core * half), (rows, half))
    b_own, a_own = mine[:, part:], mine[:, :part]
    b_first = jnp.stack([b_own, swap_y_hi(b_own)])
    a_near = jnp.stack(ring(a_own, "x"))
    b_pieces = ring(b_first, "x")
    a_pieces = [a_near, swap_y_hi(a_near)]
    pieces = a_pieces + [swap_core(p) for p in a_pieces] + b_pieces + [swap_core(p) for p in b_pieces]

    order = [((y_hi + yrel) % 2) * 4 + (x - k) % 4 for yrel in range(2) for k in range(4)]
    turned = jnp.concatenate(
        [lax.dynamic_slice(context, (0, at * rows), (tokens, rows)) for at in order], axis=1
    )
    own_context = turned.T
    peer_context = swap_core(own_context)

    labels = jnp.stack([item_ids, item_counts // 128, item_counts % 128], axis=1)
    labels = jnp.pad(labels, ((0, users_here - items_here), (0, 0)))
    labels = jnp.concatenate([positive[:, None], labels], axis=1)
    labels = jnp.pad(labels, ((0, 0), (0, LABELS - 4))).astype(BF16)
    users = jnp.concatenate([user_vectors, labels], axis=1)
    users = put(ring(users, "x"), x)
    users = put(ring(users, "y"), y)
    users = ring(users.reshape(16 * users_here, width + LABELS), "z")

    stream, inverse, pooled, embedding = pl.pallas_call(
        forward_kernel,
        out_shape=(
            shaped((tokens, width)),
            shaped((tokens, 1)),
            shaped((items_here, width)),
            shaped((items_here, width), BF16),
        ),
        in_specs=[SMEM, SMEM] + [VMEM] * 15,
        out_specs=(VMEM,) * 4,
        compiler_params=PARAMS,
        name="forward",
    )(where, lengths, turned, residual, gain, *pieces)

    *users, embedding = lax.optimization_barrier((*users, embedding))
    users = users + [swap_core(p) for p in users]
    emb = jnp.stack(ring(embedding, "x"))
    emb = jnp.stack(ring(emb, "y")).reshape(16 * items_here, width)
    emb = ring(emb, "z")
    emb = emb + [swap_core(p) for p in emb]

    people = DEVICES * users_here
    items = DEVICES * items_here
    loss, gain_grad, item_grad, user_grad = pl.pallas_call(
        functools.partial(loss_kernel, users_here),
        out_shape=(
            shaped((1, 1)),
            shaped((1, width)),
            shaped((items_here, width)),
            shaped((users_here, width), BF16),
        ),
        in_specs=[SMEM, SMEM, VMEM, VMEM] + [ANY] * 16,
        out_specs=(VMEM,) * 4,
        scratch_shapes=[
            pltpu.VMEM((people, width + LABELS), BF16),
            pltpu.VMEM((items, width), BF16),
            pltpu.VMEM((people, items), F32),
            pltpu.VMEM((items, width), F32),
            pltpu.SemaphoreType.DMA((8,)),
            pltpu.SemaphoreType.DMA((8,)),
        ],
        compiler_params=PARAMS,
        name="loss",
    )(where, lengths, gain, pooled, *users, *emb)

    residual_grad, send = pl.pallas_call(
        residual_kernel,
        out_shape=(shaped((tokens, width), BF16), shaped((tokens, half), BF16)),
        in_specs=[SMEM, SMEM, VMEM, VMEM, VMEM],
        out_specs=(VMEM,) * 2,
        compiler_params=PARAMS,
        name="residual",
    )(where, lengths, stream, inverse, item_grad)
    peer_grad = swap_core(send)
    context_grad = pl.pallas_call(
        context_kernel,
        out_shape=shaped((tokens, head), BF16),
        in_specs=[SMEM] + [VMEM] * 13,
        out_specs=VMEM,
        compiler_params=PARAMS,
        name="context",
    )(where, residual_grad, *pieces)

    operands = (where, own_context, peer_context, residual_grad, peer_grad)
    first_send, second, *second_send = pl.pallas_call(
        blocks_kernel,
        out_shape=(shaped((4 * rows, part), BF16), shaped((2, rows, part)))
        + (shaped((2, rows, part), BF16),) * 3,
        in_specs=[SMEM] + [VMEM] * 4,
        out_specs=(VMEM,) * 5,
        compiler_params=PARAMS,
        name="blocks_sent",
    )(*operands)
    first = pl.pallas_call(
        blocks_kernel,
        out_shape=shaped((4 * rows, part)),
        in_specs=[SMEM] + [VMEM] * 4,
        out_specs=VMEM,
        compiler_params=PARAMS,
        name="blocks_kept",
    )(*operands)

    first = (first + swap_y_hi(first_send).astype(F32)).reshape(4, rows, part)
    for k in (1, 2, 3):
        second = second + shift(second_send[k - 1], "x", 4 - k).astype(F32)
    arrived = [shift(first[k].astype(BF16), "x", 4 - k) for k in (1, 2, 3)]
    second = second[0] + swap_y_hi(second[1].astype(BF16)).astype(F32)
    first = first[0]
    for piece in arrived:
        first = first + piece.astype(F32)
    own = jnp.concatenate([first, second], axis=1)
    for swap in (swap_y_lo, lambda v: swap_z(v, 1), lambda v: swap_z(v, 3)):
        own = lax.reduce_precision(own, 8, 7)
        own = own + swap(own.astype(BF16)).astype(F32)
    own = own.astype(BF16)
    other = swap_core(own)
    weight_grad = jnp.where(
        core == 0, jnp.concatenate([own, other], axis=1), jnp.concatenate([other, own], axis=1)
    )
    return (loss[0, 0], residual_grad, context_grad, weight_grad, gain_grad[0], user_grad)


def solution(mesh):
    placed = (
        P(AXES, None),
        P(AXES, None),
        P("fsdp", None),
        P(),
        P(AXES, None),
        P(AXES),
        P(AXES),
        P(AXES),
        P(AXES),
    )
    return jax.shard_map(
        on_device,
        mesh=mesh,
        in_specs=placed,
        out_specs=(P(), P(AXES, None), P(AXES, None), P("fsdp", None), P(), P(AXES, None)),
        check_vma=False,
    )
```

```python
import functools

import jax
import jax.numpy as jnp
from jax import lax
from jax.experimental import pallas as pl
from jax.experimental.pallas import tpu as pltpu
from jax.sharding import PartitionSpec as P

EPSILON = 1e-06
MASKED_FILL = -1e30
AXES = ("dp", "fsdp")
F32 = jnp.float32
BF16 = jnp.bfloat16
VMEM = pl.BlockSpec(memory_space=pltpu.VMEM)
SMEM = pl.BlockSpec(memory_space=pltpu.SMEM)
ANY = pl.BlockSpec(memory_space=pl.ANY)


def params(mebibytes):
    return pltpu.CompilerParams(vmem_limit_bytes=mebibytes * 1024 * 1024)


def after(value, other):
    return lax.optimization_barrier((value, other))[0]

DEVICES = 128
LABELS = 128


def linear(x, y, z, c):
    return ((((y % 2) * 4 + z) * 2 + c) * 2 + y // 2) * 4 + x


def move(value, where):
    perm = []
    for x in range(4):
        for y in range(4):
            for z in range(4):
                for c in range(2):
                    perm.append((linear(x, y, z, c), linear(*where(x, y, z, c))))
    return lax.ppermute(value, AXES, perm)


def shift(value, axis, k):
    if axis == "x":
        return move(value, lambda x, y, z, c: ((x + k) % 4, y, z, c))
    if axis == "y":
        return move(value, lambda x, y, z, c: (x, (y + k) % 4, z, c))
    return move(value, lambda x, y, z, c: (x, y, (z + k) % 4, c))


def swap_core(value):
    return move(value, lambda x, y, z, c: (x, y, z, 1 - c))


def swap_y_hi(value):
    return move(value, lambda x, y, z, c: (x, 3 - y, z, c))


def swap_y_lo(value):
    return move(value, lambda x, y, z, c: (x, y ^ 1, z, c))


def swap_z(value, bits):
    return move(value, lambda x, y, z, c: (x, y, z ^ bits, c))


def ring(value, axis):
    return [value] + [shift(value, axis, k) for k in (1, 2, 3)]


def put(pieces, at):
    out = jnp.zeros((4,) + pieces[0].shape, pieces[0].dtype)
    for k, piece in enumerate(pieces):
        out = lax.dynamic_update_index_in_dim(out, piece, (at - k) % 4, 0)
    return out


def dot(left, right):
    return jnp.dot(left, right, preferred_element_type=F32)


def contract_rows(left, right):
    return lax.dot_general(left, right, (((0,), (0,)), ((), ())), preferred_element_type=F32)


def contract_last(left, right):
    return lax.dot_general(left, right, (((1,), (1,)), ((), ())), preferred_element_type=F32)


def column_offsets(core, width):
    half, part = width // 2, width // 4
    mine = pl.multiple_of(core * half, half)
    other = pl.multiple_of((1 - core) * half, half)
    return (
        (mine, pl.multiple_of(mine + part, part)),
        (other, pl.multiple_of(other + part, part)),
    )


def forward_kernel(where, lengths, context, residual, gain, *refs):
    a_refs, b_refs = (refs[0:2], refs[2:4]), (refs[4:8], refs[8:12])
    stream, inverse, pooled, embedding = refs[12:]
    tokens, width = residual.shape
    part = width // 4
    head = context.shape[1]
    block = head // 8
    items = lengths.shape[0]
    length = tokens // items
    for side, (first_at, second_at) in enumerate(column_offsets(where[3], width)):
        acc = residual[:, pl.ds(first_at, part)].astype(F32)
        for yrel in range(2):
            acc = acc + dot(
                context[:, yrel * 4 * block : (yrel + 1) * 4 * block],
                a_refs[side][yrel][...].reshape(4 * block, part),
            )
        stream[:, pl.ds(first_at, part)] = acc
        acc = residual[:, pl.ds(second_at, part)].astype(F32)
        for k in range(4):
            columns = jnp.concatenate(
                [
                    context[:, k * block : (k + 1) * block],
                    context[:, (4 + k) * block : (5 + k) * block],
                ],
                axis=1,
            )
            acc = acc + dot(columns, b_refs[side][k][...].reshape(2 * block, part))
        stream[:, pl.ds(second_at, part)] = acc
    for i in range(items):
        rows = stream[i * length : (i + 1) * length, :]
        inv = lax.rsqrt(jnp.mean(rows * rows, axis=-1, keepdims=True) + EPSILON)
        inverse[i * length : (i + 1) * length, :] = inv
        position = lax.broadcasted_iota(jnp.int32, (length, 1), 0)
        kept = jnp.where(position < lengths[i], inv, 0.0)
        total = jnp.sum(rows * kept, axis=0, keepdims=True)
        pool = total * gain[...] / lengths[i].astype(F32)
        pooled[i : i + 1, :] = pool
    pool = pooled[...]
    scale = lax.rsqrt(jnp.mean(pool * pool, axis=-1, keepdims=True) + EPSILON)
    embedding[...] = (pool * scale).astype(BF16)


def loss_kernel(users_here, where, lengths, gain, pooled, *refs):
    user_refs, emb_refs = refs[:8], refs[8:16]
    loss, gain_grad, item_grad, user_grad = refs[16:20]
    users, placed, grads, emb_grads, user_sem, emb_sem = refs[20:]
    x, y, z, core = where[0], where[1], where[2], where[3]
    group, width = emb_refs[0].shape
    chunk = user_refs[0].shape[0]
    items = 8 * group
    items_here = lengths.shape[0]
    people = users.shape[0]
    copies = []
    for n in range(8):
        side, k = n // 4, n % 4
        c = core if side == 0 else 1 - core
        at = c * 4 + (z - k + 4) % 4
        copies.append(
            pltpu.make_async_copy(
                emb_refs[n], placed.at[pl.ds(pl.multiple_of(at * group, group), group)], emb_sem.at[n]
            )
        )
        copies.append(
            pltpu.make_async_copy(
                user_refs[n], users.at[pl.ds(pl.multiple_of(at * chunk, chunk), chunk)], user_sem.at[n]
            )
        )
    for copy in copies:
        copy.start()
    to = lax.broadcasted_iota(jnp.int32, (items, items), 0)
    of = lax.broadcasted_iota(jnp.int32, (items, items), 1)
    per = group // items_here
    to_chip, of_chip = (to // items_here) % per, (of // items_here) % per
    turned = (
        ((y - of_chip // 4 + 4) % 4 == to_chip // 4)
        & ((x - of_chip % 4 + 4) % 4 == to_chip % 4)
        & (to // group == of // group)
        & (to % items_here == of % items_here)
    )
    turn = jnp.where(turned, 1.0, 0.0).astype(BF16)
    for copy in copies:
        copy.wait()
    emb = dot(turn, placed[...]).astype(BF16)
    labels = users[:, width : width + LABELS]
    person = lax.broadcasted_iota(jnp.int32, (people, items), 0)
    item = lax.broadcasted_iota(jnp.int32, (people, items), 1)
    holder = jnp.where(
        person == (item // items_here) * users_here + item % items_here, 1.0, 0.0
    ).astype(BF16)
    item_labels = contract_rows(labels, holder)
    ids = item_labels[1:2, :]
    log_counts = jnp.log(item_labels[2:3, :] * 128.0 + item_labels[3:4, :])
    chip = lax.broadcasted_iota(jnp.int32, (1, items), 1) // items_here
    which = lax.broadcasted_iota(jnp.int32, (1, items), 1) % items_here
    index = linear(chip % 4, (chip // 4) % 4, (chip // 16) % 4, chip // 64) * items_here + which
    index = index.astype(F32)
    positive = labels[:, 0:1].astype(F32)
    onehot = index == positive
    positive_id = jnp.sum(jnp.where(onehot, ids, 0.0), axis=1, keepdims=True)
    excluded = (ids == positive_id) & jnp.logical_not(onehot)
    scores = contract_last(users[:, :width], emb)
    logits = jnp.where(excluded, MASKED_FILL, scores - log_counts)
    row_max = jnp.max(logits, axis=1, keepdims=True)
    weights = jnp.where(excluded, 0.0, jnp.exp(logits - row_max))
    row_total = jnp.sum(weights, axis=1, keepdims=True)
    picked = jnp.sum(jnp.where(onehot, logits, 0.0), axis=1, keepdims=True)
    losses = row_max + jnp.log(row_total) - picked
    loss[...] = jnp.sum(losses, axis=0, keepdims=True) / people
    grad = (weights / row_total - jnp.where(onehot, 1.0, 0.0)).astype(BF16)
    grads[...] = grad.astype(F32)
    here = ((core * 4 + z) * 4 + y) * 4 + x
    own = grads[pl.ds(pl.multiple_of(here * users_here, users_here), users_here), :].astype(BF16)
    user_grad[...] = dot(own, emb).astype(BF16)
    all_grads = contract_rows(grad, users[:, :width])
    emb_grads[...] = all_grads
    emb_float = emb.astype(F32)
    product = emb_float * all_grads
    mean = jnp.mean(product, axis=-1, keepdims=True)
    gain_sum = jnp.sum(product - emb_float * emb_float * mean, axis=0, keepdims=True)
    gain_grad[...] = gain_sum / gain[...]
    first = here * items_here
    near = emb_grads[pl.ds(pl.multiple_of((first // 8) * 8, 8), 8), :]
    line = lax.broadcasted_iota(jnp.int32, (8, 1), 0)
    for i in range(items_here):
        mine = jnp.sum(jnp.where(line == first % 8 + i, near, 0.0), axis=0, keepdims=True)
        pool = pooled[i : i + 1, :]
        scale = lax.rsqrt(jnp.mean(pool * pool, axis=-1, keepdims=True) + EPSILON)
        pool_grad = scale * mine - pool * scale * scale * scale * jnp.mean(
            pool * mine, axis=-1, keepdims=True
        )
        item_grad[i : i + 1, :] = gain[...] * pool_grad / lengths[i].astype(F32)


def residual_kernel(where, lengths, stream, inverse, item_grad, residual_grad, send):
    tokens, width = stream.shape
    half = width // 2
    items = lengths.shape[0]
    length = tokens // items
    for i in range(items):
        span = slice(i * length, (i + 1) * length)
        rows = stream[span, :]
        inv = inverse[span, :]
        position = lax.broadcasted_iota(jnp.int32, (length, 1), 0)
        kept = jnp.where(position < lengths[i], inv, 0.0)
        row = item_grad[i : i + 1, :]
        mean = jnp.mean(rows * row, axis=-1, keepdims=True)
        residual_grad[span, :] = (kept * row - rows * (kept * inv * inv * mean)).astype(BF16)
    send[...] = residual_grad[:, pl.ds(pl.multiple_of((1 - where[3]) * half, half), half)]


def context_kernel(where, residual_grad, *refs):
    a_refs, b_refs = (refs[0:2], refs[2:4]), (refs[4:8], refs[8:12])
    context_grad = refs[12]
    tokens, width = residual_grad.shape
    part = width // 4
    block = context_grad.shape[1] // 8
    offsets = column_offsets(where[3], width)
    firsts = [residual_grad[:, pl.ds(first, part)] for first, _ in offsets]
    seconds = [residual_grad[:, pl.ds(second, part)] for _, second in offsets]
    from_a = []
    for yrel in range(2):
        from_a.append(
            sum(
                contract_last(firsts[side], a_refs[side][yrel][...].reshape(4 * block, part))
                for side in range(2)
            )
        )
    x, y_hi = where[0], where[1] // 2
    for k in range(4):
        from_b = sum(
            contract_last(seconds[side], b_refs[side][k][...].reshape(2 * block, part))
            for side in range(2)
        )
        for yrel in range(2):
            value = (
                from_a[yrel][:, k * block : (k + 1) * block]
                + from_b[:, yrel * block : (yrel + 1) * block]
            )
            y_to = y_hi if yrel == 0 else 1 - y_hi
            at = pl.multiple_of((y_to * 4 + (x - k + 4) % 4) * block, block)
            context_grad[:, pl.ds(at, block)] = value.astype(BF16)


def blocks_kernel(where, own_context, peer_context, residual_grad, peer_grad, *refs):
    tokens, width = residual_grad.shape
    half, part = width // 2, width // 4
    block = own_context.shape[0] // 8
    first_at, second_at = column_offsets(where[3], width)[0]

    def product(yrel, at, peer_at):
        span = slice(yrel * 4 * block, (yrel + 1) * 4 * block)
        return dot(own_context[span, :], residual_grad[:, pl.ds(at, part)]) + dot(
            peer_context[span, :], peer_grad[:, peer_at : peer_at + part]
        )

    if len(refs) == 1:
        refs[0][...] = product(0, first_at, 0)
        return
    first_send, kept = refs[0], refs[1]
    first_send[...] = product(1, first_at, 0).astype(BF16)
    for yrel in range(2):
        both = product(yrel, second_at, part)
        kept[yrel] = both[:block]
        for k in (1, 2, 3):
            refs[1 + k][yrel] = both[k * block : (k + 1) * block].astype(BF16)


def shaped(shape, dtype=F32):
    return jax.ShapeDtypeStruct(shape, dtype)


def on_device(
    context, residual, out_weight, norm_gain, user_vectors, positive, item_ids, item_counts, lengths
):
    tokens, head = context.shape
    width = residual.shape[1]
    items_here = lengths.shape[0]
    users_here = user_vectors.shape[0]
    dp, fsdp = lax.axis_index("dp"), lax.axis_index("fsdp")
    y_lo, z, core = dp // 8, (dp // 2) % 4, dp % 2
    y_hi, x = fsdp // 4, fsdp % 4
    y = y_hi * 2 + y_lo
    where = jnp.stack([x, y, z, core]).astype(jnp.int32)
    half, part = width // 2, width // 4
    rows = out_weight.shape[0]
    gain = norm_gain[None, :]

    mine = lax.dynamic_slice(out_weight, (0, core * half), (rows, half))
    b_own, a_own = mine[:, part:], mine[:, :part]
    b_other = swap_y_hi(b_own)
    b_first = jnp.stack([b_own, b_other])
    a_near = jnp.stack(ring(a_own, "x"))
    b_pieces = ring(b_first, "x")
    a_pieces = [a_near, swap_y_hi(a_near)]
    pieces = a_pieces + [swap_core(p) for p in a_pieces] + b_pieces + [swap_core(p) for p in b_pieces]

    order = [((y_hi + yrel) % 2) * 4 + (x - k) % 4 for yrel in range(2) for k in range(4)]
    later = after(context, b_other)
    turned = jnp.concatenate(
        [lax.dynamic_slice(later, (0, at * rows), (tokens, rows)) for at in order], axis=1
    )
    own_context = turned.T
    peer_context = swap_core(own_context)

    labels = jnp.stack([item_ids, item_counts // 128, item_counts % 128], axis=1)
    labels = jnp.pad(labels, ((0, users_here - items_here), (0, 0)))
    labels = jnp.concatenate([positive[:, None], labels], axis=1)
    labels = jnp.pad(labels, ((0, 0), (0, LABELS - 4))).astype(BF16)
    users = after(jnp.concatenate([user_vectors, labels], axis=1), b_other)
    users = put(ring(users, "x"), x)
    users = put(ring(users, "y"), y)
    users = ring(users.reshape(16 * users_here, width + LABELS), "z")

    stream, inverse, pooled, embedding = pl.pallas_call(
        forward_kernel,
        out_shape=(
            shaped((tokens, width)),
            shaped((tokens, 1)),
            shaped((items_here, width)),
            shaped((items_here, width), BF16),
        ),
        in_specs=[SMEM, SMEM] + [VMEM] * 15,
        out_specs=(VMEM,) * 4,
        compiler_params=params(20),
        name="forward",
    )(where, lengths, turned, residual, gain, *pieces)

    emb = jnp.stack(ring(embedding, "x"))
    emb = jnp.stack(ring(emb, "y")).reshape(16 * items_here, width)
    users = after(users, emb)
    users = users + [swap_core(p) for p in users]
    emb = ring(emb, "z")
    emb = emb + [swap_core(p) for p in emb]

    people = DEVICES * users_here
    items = DEVICES * items_here
    loss, gain_grad, item_grad, user_grad = pl.pallas_call(
        functools.partial(loss_kernel, users_here),
        out_shape=(
            shaped((1, 1)),
            shaped((1, width)),
            shaped((items_here, width)),
            shaped((users_here, width), BF16),
        ),
        in_specs=[SMEM, SMEM, VMEM, VMEM] + [ANY] * 16,
        out_specs=(VMEM,) * 4,
        scratch_shapes=[
            pltpu.VMEM((people, width + LABELS), BF16),
            pltpu.VMEM((items, width), BF16),
            pltpu.VMEM((people, items), F32),
            pltpu.VMEM((items, width), F32),
            pltpu.SemaphoreType.DMA((8,)),
            pltpu.SemaphoreType.DMA((8,)),
        ],
        compiler_params=params(32),
        name="loss",
    )(where, lengths, gain, pooled, *users, *emb)

    residual_grad, send = pl.pallas_call(
        residual_kernel,
        out_shape=(shaped((tokens, width), BF16), shaped((tokens, half), BF16)),
        in_specs=[SMEM, SMEM, VMEM, VMEM, VMEM],
        out_specs=(VMEM,) * 2,
        compiler_params=params(16),
        name="residual",
    )(where, lengths, stream, inverse, item_grad)
    peer_grad = swap_core(send)
    context_grad = pl.pallas_call(
        context_kernel,
        out_shape=shaped((tokens, head), BF16),
        in_specs=[SMEM] + [VMEM] * 13,
        out_specs=VMEM,
        compiler_params=params(14),
        name="context",
    )(where, residual_grad, *pieces)

    operands = (where, own_context, peer_context, residual_grad, peer_grad)
    first_send, second, *second_send = pl.pallas_call(
        blocks_kernel,
        out_shape=(shaped((4 * rows, part), BF16), shaped((2, rows, part)))
        + (shaped((2, rows, part), BF16),) * 3,
        in_specs=[SMEM] + [VMEM] * 4,
        out_specs=(VMEM,) * 5,
        compiler_params=params(14),
        name="blocks_sent",
    )(*operands)
    first = pl.pallas_call(
        blocks_kernel,
        out_shape=shaped((4 * rows, part)),
        in_specs=[SMEM] + [VMEM] * 4,
        out_specs=VMEM,
        compiler_params=params(14),
        name="blocks_kept",
    )(*operands)

    first = (first + swap_y_hi(first_send).astype(F32)).reshape(4, rows, part)
    for k in (1, 2, 3):
        second = second + shift(second_send[k - 1], "x", 4 - k).astype(F32)
    arrived = [shift(first[k].astype(BF16), "x", 4 - k) for k in (1, 2, 3)]
    second = second[0] + swap_y_hi(second[1].astype(BF16)).astype(F32)
    first = first[0]
    for piece in arrived:
        first = first + piece.astype(F32)
    own = jnp.concatenate([first, second], axis=1)
    own, context_grad = lax.optimization_barrier((own, context_grad))
    for swap in (swap_y_lo, lambda v: swap_z(v, 1), lambda v: swap_z(v, 3)):
        own = lax.reduce_precision(own, 8, 7)
        own = own + swap(own.astype(BF16)).astype(F32)
    own = own.astype(BF16)
    other = swap_core(own)
    weight_grad = jnp.where(
        core == 0, jnp.concatenate([own, other], axis=1), jnp.concatenate([other, own], axis=1)
    )
    return (loss[0, 0], residual_grad, context_grad, weight_grad, gain_grad[0], user_grad)


def solution(mesh):
    placed = (
        P(AXES, None),
        P(AXES, None),
        P("fsdp", None),
        P(),
        P(AXES, None),
        P(AXES),
        P(AXES),
        P(AXES),
        P(AXES),
    )
    return jax.shard_map(
        on_device,
        mesh=mesh,
        in_specs=placed,
        out_specs=(P(), P(AXES, None), P(AXES, None), P("fsdp", None), P(), P(AXES, None)),
        check_vma=False,
    )
```

```python
import functools

import jax
import jax.numpy as jnp
from jax import lax
from jax.experimental import pallas as pl
from jax.experimental.pallas import tpu as pltpu
from jax.sharding import PartitionSpec as P

EPSILON = 1e-06
MASKED_FILL = -1e30
AXES = ("dp", "fsdp")
F32 = jnp.float32
BF16 = jnp.bfloat16
VMEM = pl.BlockSpec(memory_space=pltpu.VMEM)
SMEM = pl.BlockSpec(memory_space=pltpu.SMEM)
ANY = pl.BlockSpec(memory_space=pl.ANY)


def params(mebibytes):
    return pltpu.CompilerParams(vmem_limit_bytes=mebibytes * 1024 * 1024)


def after(value, other):
    return lax.optimization_barrier((value, other))[0]

LABELS = 128


def linear(x, y, z, c):
    return ((((y % 2) * 4 + z) * 2 + c) * 2 + y // 2) * 4 + x


def move(value, where):
    perm = []
    for x in range(4):
        for y in range(4):
            for z in range(4):
                for c in range(2):
                    perm.append((linear(x, y, z, c), linear(*where(x, y, z, c))))
    return lax.ppermute(value, AXES, perm)


def swap_core(value):
    return move(value, lambda x, y, z, c: (x, y, z, 1 - c))


def swap_x(value, bits):
    return move(value, lambda x, y, z, c: (x ^ bits, y, z, c))


def swap_y(value, bits):
    return move(value, lambda x, y, z, c: (x, y ^ bits, z, c))


def swap_z(value, bits):
    return move(value, lambda x, y, z, c: (x, y, z ^ bits, c))


def doubled(value, swap, bits):
    return jnp.concatenate([value, swap(value, bits)], axis=0)


def dot(left, right):
    return jnp.dot(left, right, preferred_element_type=F32)


def contract_rows(left, right):
    return lax.dot_general(left, right, (((0,), (0,)), ((), ())), preferred_element_type=F32)


def contract_last(left, right):
    return lax.dot_general(left, right, (((1,), (1,)), ((), ())), preferred_element_type=F32)


def column_offsets(core, width):
    half, part = width // 2, width // 4
    mine = pl.multiple_of(core * half, half)
    other = pl.multiple_of((1 - core) * half, half)
    return (
        (mine, pl.multiple_of(mine + part, part)),
        (other, pl.multiple_of(other + part, part)),
    )


def second_order(half):
    return [r3 * 4 + r1 * 2 + half for r3 in range(2) for r1 in range(2)]


def block_home(x, y_hi, r3, r1, ry):
    return (y_hi ^ ry) * 4 + (x ^ (r1 ^ (3 * r3)))


def forward_kernel(where, lengths, context, residual, gain, labels, *refs):
    firsts, seconds = (refs[0:2], refs[4:6]), (refs[2:4], refs[6:8])
    stream, inverse, pooled, embedding = refs[8:]
    tokens, width = residual.shape
    part = width // 4
    block = context.shape[1] // 8
    items = lengths.shape[0]
    length = tokens // items
    ordered = [
        jnp.concatenate(
            [context[:, b * block : (b + 1) * block] for b in second_order(half)], axis=1
        )
        for half in range(2)
    ]
    for side, (first_at, second_at) in enumerate(column_offsets(where[3], width)):
        acc = residual[:, pl.ds(first_at, part)].astype(F32)
        for half in range(2):
            span = context[:, half * 4 * block : (half + 1) * 4 * block]
            acc = acc + dot(span, firsts[side][half][...])
        stream[:, pl.ds(first_at, part)] = acc
        acc = residual[:, pl.ds(second_at, part)].astype(F32)
        for half in range(2):
            acc = acc + dot(ordered[half], seconds[side][half][...])
        stream[:, pl.ds(second_at, part)] = acc
    for i in range(items):
        rows = stream[i * length : (i + 1) * length, :]
        inv = lax.rsqrt(jnp.mean(rows * rows, axis=-1, keepdims=True) + EPSILON)
        inverse[i * length : (i + 1) * length, :] = inv
        position = lax.broadcasted_iota(jnp.int32, (length, 1), 0)
        kept = jnp.where(position < lengths[i], inv, 0.0)
        total = jnp.sum(rows * kept, axis=0, keepdims=True)
        pooled[i : i + 1, :] = total * gain[...] / lengths[i].astype(F32)
    pool = pooled[...]
    scale = lax.rsqrt(jnp.mean(pool * pool, axis=-1, keepdims=True) + EPSILON)
    embedding[:, :width] = (pool * scale).astype(BF16)
    embedding[:, width:] = labels[...]


def bit(value, k):
    return (value >> k) & 1


def one_hot_turn(rows, home):
    to = lax.broadcasted_iota(jnp.int32, (rows, rows), 0)
    of = lax.broadcasted_iota(jnp.int32, (rows, rows), 1)
    return jnp.where(to == home(of), 1.0, 0.0).astype(BF16)


def loss_kernel(users_here, items_here, where, gain, *refs):
    user_refs, emb_refs = refs[:2], refs[2:6]
    sums, user_grad, grads, emb_grads = refs[6:]
    x, y, z, core = where[0], where[1], where[2], where[3]
    group, full = emb_refs[0].shape
    width = full - LABELS
    items = 4 * group
    people = 2 * user_refs[0].shape[0]

    def item_home(s):
        one = s // items_here
        ax = x ^ bit(one, 0) ^ (3 * bit(one, 1))
        ay = y ^ bit(one, 2) ^ (3 * bit(one, 3))
        az = z ^ bit(one, 4) ^ (3 * bit(one, 5))
        ac = core ^ bit(one, 6)
        return (((ac * 4 + az) * 4 + ay) * 4 + ax) * items_here + s % items_here

    def user_home(s):
        one = s // users_here
        ay = y ^ (3 * bit(one, 0)) ^ bit(one, 1)
        az = z ^ bit(one, 2) ^ (3 * bit(one, 3))
        ac = core ^ bit(one, 4)
        return ((ac * 4 + az) * 4 + ay) * users_here + s % users_here

    placed = jnp.concatenate([ref[...] for ref in emb_refs], axis=0)
    turned = dot(one_hot_turn(items, item_home), placed).astype(BF16)
    emb, labels = turned[:, :width], turned[:, width:]
    placed = jnp.concatenate([ref[...] for ref in user_refs], axis=0)
    turned = dot(one_hot_turn(people, user_home), placed).astype(BF16)
    users = turned[:, :width]
    positive = turned[:, width : width + 1].astype(F32)
    item_labels = contract_rows(labels, one_hot_turn(items, lambda s: s))
    ids = item_labels[0:1, :]
    log_counts = jnp.log(item_labels[1:2, :] * 128.0 + item_labels[2:3, :])
    item = lax.broadcasted_iota(jnp.int32, (1, items), 1)
    chip = item // items_here
    index = linear(chip % 4, (chip // 4) % 4, (chip // 16) % 4, chip // 64) * items_here
    index = (index + item % items_here).astype(F32)
    onehot = index == positive
    positive_id = jnp.sum(jnp.where(onehot, ids, 0.0), axis=1, keepdims=True)
    excluded = (ids == positive_id) & jnp.logical_not(onehot)
    scores = contract_last(users, emb)
    logits = jnp.where(excluded, MASKED_FILL, scores - log_counts)
    row_max = jnp.max(logits, axis=1, keepdims=True)
    weights = jnp.where(excluded, 0.0, jnp.exp(logits - row_max))
    row_total = jnp.sum(weights, axis=1, keepdims=True)
    picked = jnp.sum(jnp.where(onehot, logits, 0.0), axis=1, keepdims=True)
    losses = row_max + jnp.log(row_total) - picked
    grad = (weights / row_total - jnp.where(onehot, 1.0, 0.0)).astype(BF16)
    grads[...] = grad.astype(F32)
    all_grads = contract_rows(grad, users)
    emb_grads[...] = all_grads
    emb_float = emb.astype(F32)
    product = emb_float * all_grads
    mean = jnp.mean(product, axis=-1, keepdims=True)
    gain_sum = jnp.sum(product - emb_float * emb_float * mean, axis=0, keepdims=True)
    place = (core * 4 + z) * 4 + y
    near = 4 * items_here
    sums[:, :width] = emb_grads[pl.ds(pl.multiple_of(place * near, near), near), :]
    piece = width // near
    for j in range(near):
        sums[j : j + 1, width : width + piece] = gain_sum[:, j * piece : (j + 1) * piece]
    loss = jnp.sum(losses, axis=0, keepdims=True)
    sums[:, width + piece :] = jnp.broadcast_to(loss, (near, LABELS))
    own = grads[pl.ds(pl.multiple_of(place * users_here, users_here), users_here), :]
    user_grad[...] = dot(own.astype(BF16), emb).astype(BF16)


def residual_kernel(people, where, lengths, stream, inverse, pooled, gain, sums, *refs):
    residual_grad, send, gain_grad, loss = refs
    tokens, width = stream.shape
    half = width // 2
    items = lengths.shape[0]
    length = tokens // items
    near = sums.shape[0]
    piece = width // near
    line = lax.broadcasted_iota(jnp.int32, (near, 1), 0)
    for i in range(items):
        mine = jnp.sum(
            jnp.where(line == where[0] * items + i, sums[:, :width], 0.0), axis=0, keepdims=True
        )
        pool = pooled[i : i + 1, :]
        scale = lax.rsqrt(jnp.mean(pool * pool, axis=-1, keepdims=True) + EPSILON)
        pool_grad = scale * mine - pool * scale * scale * scale * jnp.mean(
            pool * mine, axis=-1, keepdims=True
        )
        row = gain[...] * pool_grad / lengths[i].astype(F32)
        span = slice(i * length, (i + 1) * length)
        rows = stream[span, :]
        inv = inverse[span, :]
        position = lax.broadcasted_iota(jnp.int32, (length, 1), 0)
        kept = jnp.where(position < lengths[i], inv, 0.0)
        mean = jnp.mean(rows * row, axis=-1, keepdims=True)
        residual_grad[span, :] = (kept * row - rows * (kept * inv * inv * mean)).astype(BF16)
    send[...] = residual_grad[:, pl.ds(pl.multiple_of((1 - where[3]) * half, half), half)]
    for j in range(near):
        at = slice(j * piece, (j + 1) * piece)
        gain_grad[:, at] = sums[j : j + 1, width : width + piece] / gain[:, at]
    loss[...] = sums[0:1, width + piece : width + piece + 1] / people


def context_kernel(where, residual_grad, *refs):
    firsts, seconds = (refs[0:2], refs[4:6]), (refs[2:4], refs[6:8])
    context_grad = refs[8]
    width = residual_grad.shape[1]
    part = width // 4
    block = context_grad.shape[1] // 8
    offsets = column_offsets(where[3], width)
    near = [residual_grad[:, pl.ds(first, part)] for first, _ in offsets]
    far = [residual_grad[:, pl.ds(second, part)] for _, second in offsets]
    from_first = [sum(contract_last(near[s], firsts[s][h][...]) for s in range(2)) for h in range(2)]
    from_second = [sum(contract_last(far[s], seconds[s][h][...]) for s in range(2)) for h in range(2)]
    for r3 in range(2):
        for r1 in range(2):
            for ry in range(2):
                a, b = (r1 * 2 + ry) * block, (r3 * 2 + r1) * block
                value = from_first[r3][:, a : a + block] + from_second[ry][:, b : b + block]
                home = block_home(where[0], where[1] // 2, r3, r1, ry)
                context_grad[:, pl.ds(pl.multiple_of(home * block, block), block)] = value.astype(BF16)


def blocks_kernel(half, where, own_context, peer_context, residual_grad, peer_grad, first, second):
    width = residual_grad.shape[1]
    part = width // 4
    block = own_context.shape[0] // 8
    first_at, second_at = column_offsets(where[3], width)[0]
    span = slice(half * 4 * block, (half + 1) * 4 * block)
    value = dot(own_context[span, :], residual_grad[:, pl.ds(first_at, part)])
    value = value + dot(peer_context[span, :], peer_grad[:, :part])
    first[...] = value.astype(first.dtype)

    def ordered(ref):
        return jnp.concatenate(
            [ref[b * block : (b + 1) * block, :] for b in second_order(half)], axis=0
        )

    value = dot(ordered(own_context), residual_grad[:, pl.ds(second_at, part)])
    value = value + dot(ordered(peer_context), peer_grad[:, part:])
    second[...] = value.astype(second.dtype)


def shaped(shape, dtype=F32):
    return jax.ShapeDtypeStruct(shape, dtype)


def added(kept, sent, swap, bits):
    return kept + swap(sent.astype(BF16), bits).astype(F32)


def folded(value, swap, bits):
    rows = value.shape[0] // 2
    return added(value[:rows], value[rows:], swap, bits)


def all_added(value, swap, bits):
    value = lax.reduce_precision(value, 8, 7)
    return added(value, value, swap, bits)


def on_device(
    context, residual, out_weight, norm_gain, user_vectors, positive, item_ids, item_counts, lengths
):
    tokens, head = context.shape
    width = residual.shape[1]
    items_here = lengths.shape[0]
    users_here = user_vectors.shape[0]
    dp, fsdp = lax.axis_index("dp"), lax.axis_index("fsdp")
    y_lo, z, core = dp // 8, (dp // 2) % 4, dp % 2
    y_hi, x = fsdp // 4, fsdp % 4
    y = y_hi * 2 + y_lo
    where = jnp.stack([x, y, z, core]).astype(jnp.int32)
    half, part = width // 2, width // 4
    rows = out_weight.shape[0]
    gain = norm_gain[None, :]

    mine = lax.dynamic_slice(out_weight, (0, core * half), (rows, half))
    first = doubled(mine[:, :part], swap_y, 3)
    second = doubled(mine[:, part:], swap_x, 1)
    step_one = first
    first = doubled(first, swap_x, 1)
    second = doubled(second, swap_x, 3)
    step_two = first
    firsts = [first, swap_x(first, 3)]
    seconds = [second, swap_y(second, 3)]
    pieces = firsts + seconds
    pieces = pieces + [swap_core(p) for p in pieces]

    order = [
        block_home(x, y_hi, r3, r1, ry) for r3 in range(2) for r1 in range(2) for ry in range(2)
    ]
    later = after(context, step_one)
    turned = jnp.concatenate(
        [lax.dynamic_slice(later, (0, at * rows), (tokens, rows)) for at in order], axis=1
    )

    labels = jnp.pad(positive[:, None], ((0, 0), (0, LABELS - 1))).astype(BF16)
    users = after(jnp.concatenate([user_vectors, labels], axis=1), step_one)
    users = doubled(users, swap_y, 3)
    users = doubled(users, swap_y, 1)
    users = after(users, step_two)
    users = doubled(users, swap_z, 1)
    users = doubled(users, swap_z, 3)
    labels = jnp.stack([item_ids, item_counts // 128, item_counts % 128], axis=1)
    labels = jnp.pad(labels, ((0, 0), (0, LABELS - 3))).astype(BF16)

    stream, inverse, pooled, emb = pl.pallas_call(
        forward_kernel,
        out_shape=(
            shaped((tokens, width)),
            shaped((tokens, 1)),
            shaped((items_here, width)),
            shaped((items_here, width + LABELS), BF16),
        ),
        in_specs=[SMEM, SMEM] + [VMEM] * 12,
        out_specs=(VMEM,) * 4,
        compiler_params=params(20),
        name="forward",
    )(where, lengths, turned, residual, gain, labels, *pieces)

    users, turned = lax.optimization_barrier((users, turned, emb))[:2]
    user_pieces = [users, swap_core(users)]
    own_context = turned.T
    peer_context = swap_core(own_context)
    for swap, bits in ((swap_x, 1), (swap_x, 3), (swap_y, 1), (swap_y, 3), (swap_z, 1)):
        emb = doubled(emb, swap, bits)
    emb_pieces = [emb, swap_z(emb, 3)]
    emb_pieces = emb_pieces + [swap_core(p) for p in emb_pieces]

    near = 4 * items_here
    items, people = 128 * items_here, 32 * users_here
    sums, user_grad = pl.pallas_call(
        functools.partial(loss_kernel, users_here, items_here),
        out_shape=(
            shaped((near, width + width // near + LABELS)),
            shaped((users_here, width), BF16),
        ),
        in_specs=[SMEM] + [VMEM] * 7,
        out_specs=(VMEM,) * 2,
        scratch_shapes=[pltpu.VMEM((people, items), F32), pltpu.VMEM((items, width), F32)],
        compiler_params=params(24),
        name="loss",
    )(where, gain, *user_pieces, *emb_pieces)
    sums = sums + swap_x(sums, 3)
    sums = sums + swap_x(sums, 1)

    residual_grad, send, gain_grad, loss = pl.pallas_call(
        functools.partial(residual_kernel, 4 * people),
        out_shape=(
            shaped((tokens, width), BF16),
            shaped((tokens, half), BF16),
            shaped((1, width)),
            shaped((1, 1)),
        ),
        in_specs=[SMEM, SMEM] + [VMEM] * 5,
        out_specs=(VMEM,) * 4,
        compiler_params=params(16),
        name="residual",
    )(where, lengths, stream, inverse, pooled, gain, sums)
    peer_grad = swap_core(send)
    context_grad = pl.pallas_call(
        context_kernel,
        out_shape=shaped((tokens, head), BF16),
        in_specs=[SMEM] + [VMEM] * 9,
        out_specs=VMEM,
        compiler_params=params(14),
        name="context",
    )(where, residual_grad, *pieces)

    operands = (where, own_context, peer_context, residual_grad, peer_grad)

    def blocks(which, dtype, name):
        return pl.pallas_call(
            functools.partial(blocks_kernel, which),
            out_shape=(shaped((4 * rows, part), dtype),) * 2,
            in_specs=[SMEM] + [VMEM] * 4,
            out_specs=(VMEM,) * 2,
            compiler_params=params(14),
            name=name,
        )(*operands)

    first_sent, second_sent = blocks(1, BF16, "blocks_sent")
    first, second = blocks(0, F32, "blocks_kept")
    first = added(first, first_sent, swap_x, 3)
    second = added(second, second_sent, swap_y, 3)
    first = folded(first, swap_x, 1)
    second = folded(second, swap_x, 3)
    first = folded(first, swap_y, 3)
    second = folded(second, swap_x, 1)
    first, second, context_grad = lax.optimization_barrier((first, second, context_grad))
    first = all_added(first, swap_y, 1)
    second = all_added(second, swap_z, 1)
    first = all_added(first, swap_z, 1)
    second = all_added(second, swap_z, 3)
    first = all_added(first, swap_z, 3)
    second = all_added(second, swap_y, 1)
    own = jnp.concatenate([first, second], axis=1).astype(BF16)
    other = swap_core(own)
    weight_grad = jnp.where(
        core == 0, jnp.concatenate([own, other], axis=1), jnp.concatenate([other, own], axis=1)
    )
    return (loss[0, 0], residual_grad, context_grad, weight_grad, gain_grad[0], user_grad)


def solution(mesh):
    placed = (
        P(AXES, None),
        P(AXES, None),
        P("fsdp", None),
        P(),
        P(AXES, None),
        P(AXES),
        P(AXES),
        P(AXES),
        P(AXES),
    )
    return jax.shard_map(
        on_device,
        mesh=mesh,
        in_specs=placed,
        out_specs=(P(), P(AXES, None), P(AXES, None), P("fsdp", None), P(), P(AXES, None)),
        check_vma=False,
    )
```

```python
import functools

import jax
import jax.numpy as jnp
from jax import lax
from jax.experimental import pallas as pl
from jax.experimental.pallas import tpu as pltpu
from jax.sharding import PartitionSpec as P

EPSILON = 1e-06
MASKED_FILL = -1e30
AXES = ("dp", "fsdp")
F32 = jnp.float32
BF16 = jnp.bfloat16
VMEM = pl.BlockSpec(memory_space=pltpu.VMEM)
SMEM = pl.BlockSpec(memory_space=pltpu.SMEM)
HBM = pl.BlockSpec(memory_space=pltpu.HBM)


def params(mebibytes):
    return pltpu.CompilerParams(vmem_limit_bytes=mebibytes * 1024 * 1024)


def after(value, other):
    return lax.optimization_barrier((value, other))[0]

LABELS = 128


def linear(x, y, z, c):
    return ((((y % 2) * 4 + z) * 2 + c) * 2 + y // 2) * 4 + x


def move(value, where):
    perm = []
    for x in range(4):
        for y in range(4):
            for z in range(4):
                for c in range(2):
                    perm.append((linear(x, y, z, c), linear(*where(x, y, z, c))))
    return lax.ppermute(value, AXES, perm)


def swap_core(value):
    return move(value, lambda x, y, z, c: (x, y, z, 1 - c))


def swap_x(value, bits):
    return move(value, lambda x, y, z, c: (x ^ bits, y, z, c))


def swap_y(value, bits):
    return move(value, lambda x, y, z, c: (x, y ^ bits, z, c))


def swap_z(value, bits):
    return move(value, lambda x, y, z, c: (x, y, z ^ bits, c))


def doubled(value, swap, bits):
    return lax.optimization_barrier(jnp.concatenate([value, swap(value, bits)], axis=0))


def dot(left, right):
    return jnp.dot(left, right, preferred_element_type=F32)


def contract_rows(left, right):
    return lax.dot_general(left, right, (((0,), (0,)), ((), ())), preferred_element_type=F32)


def contract_last(left, right):
    return lax.dot_general(left, right, (((1,), (1,)), ((), ())), preferred_element_type=F32)


def column_offsets(core, width):
    half, part = width // 2, width // 4
    mine = pl.multiple_of(core * half, half)
    other = pl.multiple_of((1 - core) * half, half)
    return (
        (mine, pl.multiple_of(mine + part, part)),
        (other, pl.multiple_of(other + part, part)),
    )


def second_order(half):
    return [r3 * 4 + r1 * 2 + half for r3 in range(2) for r1 in range(2)]


def block_home(x, y_hi, r3, r1, ry):
    return (y_hi ^ ry) * 4 + (x ^ (r1 ^ (3 * r3)))


def forward_kernel(where, lengths, context, residual, gain, labels, *refs):
    firsts, seconds = (refs[0:2], refs[4:6]), (refs[2:4], refs[6:8])
    stream, inverse, pooled, embedding, added_rows, sem = refs[8:]
    tokens, width = residual.shape
    part = width // 4
    block = context.shape[1] // 8
    items = lengths.shape[0]
    length = tokens // items
    copy = pltpu.make_async_copy(residual, added_rows, sem)
    copy.start()
    ordered = [
        jnp.concatenate(
            [context[:, b * block : (b + 1) * block] for b in second_order(half)], axis=1
        )
        for half in range(2)
    ]
    for side, (first_at, second_at) in enumerate(column_offsets(where[3], width)):
        spans = [context[:, half * 4 * block : (half + 1) * 4 * block] for half in range(2)]
        stream[:, pl.ds(first_at, part)] = dot(spans[0], firsts[side][0][...]) + dot(
            spans[1], firsts[side][1][...]
        )
        stream[:, pl.ds(second_at, part)] = dot(ordered[0], seconds[side][0][...]) + dot(
            ordered[1], seconds[side][1][...]
        )
    copy.wait()
    for i in range(items):
        span = slice(i * length, (i + 1) * length)
        rows = stream[span, :] + added_rows[span, :].astype(F32)
        stream[span, :] = rows
        inv = lax.rsqrt(jnp.mean(rows * rows, axis=-1, keepdims=True) + EPSILON)
        inverse[i * length : (i + 1) * length, :] = inv
        position = lax.broadcasted_iota(jnp.int32, (length, 1), 0)
        kept = jnp.where(position < lengths[i], inv, 0.0)
        total = jnp.sum(rows * kept, axis=0, keepdims=True)
        pooled[i : i + 1, :] = total * gain[...] / lengths[i].astype(F32)
    pool = pooled[...]
    scale = lax.rsqrt(jnp.mean(pool * pool, axis=-1, keepdims=True) + EPSILON)
    embedding[:, :width] = (pool * scale).astype(BF16)
    embedding[:, width:] = labels[...]


def bit(value, k):
    return (value >> k) & 1


def one_hot_turn(rows, home):
    to = lax.broadcasted_iota(jnp.int32, (rows, rows), 0)
    of = lax.broadcasted_iota(jnp.int32, (rows, rows), 1)
    return jnp.where(to == home(of), 1.0, 0.0).astype(BF16)


def loss_kernel(users_here, items_here, where, gain, *refs):
    user_refs, emb_refs = refs[:2], refs[2:6]
    sums, user_grad, grads, emb_grads = refs[6:]
    x, y, z, core = where[0], where[1], where[2], where[3]
    group, full = emb_refs[0].shape
    width = full - LABELS
    items = 4 * group
    people = 2 * user_refs[0].shape[0]

    def item_home(s):
        one = s // items_here
        ax = x ^ bit(one, 0) ^ (3 * bit(one, 1))
        ay = y ^ bit(one, 2) ^ (3 * bit(one, 3))
        az = z ^ bit(one, 4) ^ (3 * bit(one, 5))
        ac = core ^ bit(one, 6)
        return (((ac * 4 + az) * 4 + ay) * 4 + ax) * items_here + s % items_here

    def user_home(s):
        one = s // users_here
        az = z ^ bit(one, 0) ^ (3 * bit(one, 1))
        ay = y ^ bit(one, 2) ^ (3 * bit(one, 3))
        ac = core ^ bit(one, 4)
        return ((ac * 4 + az) * 4 + ay) * users_here + s % users_here

    placed = jnp.concatenate([ref[...] for ref in emb_refs], axis=0)
    turned = dot(one_hot_turn(items, item_home), placed).astype(BF16)
    emb, labels = turned[:, :width], turned[:, width:]
    placed = jnp.concatenate([ref[...] for ref in user_refs], axis=0)
    turned = dot(one_hot_turn(people, user_home), placed).astype(BF16)
    users = turned[:, :width]
    positive = turned[:, width : width + 1].astype(F32)
    item_labels = contract_rows(labels, one_hot_turn(items, lambda s: s))
    ids = item_labels[0:1, :]
    log_counts = jnp.log(item_labels[1:2, :] * 128.0 + item_labels[2:3, :])
    item = lax.broadcasted_iota(jnp.int32, (1, items), 1)
    chip = item // items_here
    index = linear(chip % 4, (chip // 4) % 4, (chip // 16) % 4, chip // 64) * items_here
    index = (index + item % items_here).astype(F32)
    onehot = index == positive
    positive_id = jnp.sum(jnp.where(onehot, ids, 0.0), axis=1, keepdims=True)
    excluded = (ids == positive_id) & jnp.logical_not(onehot)
    scores = contract_last(users, emb)
    logits = jnp.where(excluded, MASKED_FILL, scores - log_counts)
    row_max = jnp.max(logits, axis=1, keepdims=True)
    weights = jnp.where(excluded, 0.0, jnp.exp(logits - row_max))
    row_total = jnp.sum(weights, axis=1, keepdims=True)
    picked = jnp.sum(jnp.where(onehot, logits, 0.0), axis=1, keepdims=True)
    losses = row_max + jnp.log(row_total) - picked
    grad = (weights / row_total - jnp.where(onehot, 1.0, 0.0)).astype(BF16)
    grads[...] = grad.astype(F32)
    all_grads = contract_rows(grad, users)
    emb_grads[...] = all_grads
    emb_float = emb.astype(F32)
    product = emb_float * all_grads
    mean = jnp.mean(product, axis=-1, keepdims=True)
    gain_sum = jnp.sum(product - emb_float * emb_float * mean, axis=0, keepdims=True)
    place = (core * 4 + z) * 4 + y
    near = 4 * items_here
    sums[:, :width] = emb_grads[pl.ds(pl.multiple_of(place * near, near), near), :]
    piece = width // near
    for j in range(near):
        sums[j : j + 1, width : width + piece] = gain_sum[:, j * piece : (j + 1) * piece]
    loss = jnp.sum(losses, axis=0, keepdims=True)
    sums[:, width + piece :] = jnp.broadcast_to(loss, (near, LABELS))
    own = grads[pl.ds(pl.multiple_of(place * users_here, users_here), users_here), :]
    user_grad[...] = dot(own.astype(BF16), emb).astype(BF16)


def residual_kernel(people, where, lengths, stream, inverse, pooled, gain, sums, *refs):
    residual_grad, keep, send, gain_grad, loss = refs
    tokens, width = stream.shape
    half = width // 2
    items = lengths.shape[0]
    length = tokens // items
    near = sums.shape[0]
    piece = width // near
    line = lax.broadcasted_iota(jnp.int32, (near, 1), 0)
    for i in range(items):
        mine = jnp.sum(
            jnp.where(line == where[0] * items + i, sums[:, :width], 0.0), axis=0, keepdims=True
        )
        pool = pooled[i : i + 1, :]
        scale = lax.rsqrt(jnp.mean(pool * pool, axis=-1, keepdims=True) + EPSILON)
        pool_grad = scale * mine - pool * scale * scale * scale * jnp.mean(
            pool * mine, axis=-1, keepdims=True
        )
        row = gain[...] * pool_grad / lengths[i].astype(F32)
        span = slice(i * length, (i + 1) * length)
        rows = stream[span, :]
        inv = inverse[span, :]
        position = lax.broadcasted_iota(jnp.int32, (length, 1), 0)
        kept = jnp.where(position < lengths[i], inv, 0.0)
        mean = jnp.mean(rows * row, axis=-1, keepdims=True)
        residual_grad[span, :] = (kept * row - rows * (kept * inv * inv * mean)).astype(BF16)
    keep[...] = residual_grad[:, pl.ds(pl.multiple_of(where[3] * half, half), half)]
    send[...] = residual_grad[:, pl.ds(pl.multiple_of((1 - where[3]) * half, half), half)]
    for j in range(near):
        at = slice(j * piece, (j + 1) * piece)
        gain_grad[:, at] = sums[j : j + 1, width : width + piece] / gain[:, at]
    loss[...] = sums[0:1, width + piece : width + piece + 1] / people


def context_kernel(where, keep, send, *refs):
    firsts, seconds = (refs[0:2], refs[4:6]), (refs[2:4], refs[6:8])
    context_grad = refs[8]
    part = keep.shape[1] // 2
    block = context_grad.shape[1] // 8
    near = [ref[:, :part] for ref in (keep, send)]
    far = [ref[:, part:] for ref in (keep, send)]
    from_first = [sum(contract_last(near[s], firsts[s][h][...]) for s in range(2)) for h in range(2)]
    from_second = [sum(contract_last(far[s], seconds[s][h][...]) for s in range(2)) for h in range(2)]
    for r3 in range(2):
        for r1 in range(2):
            for ry in range(2):
                a, b = (r1 * 2 + ry) * block, (r3 * 2 + r1) * block
                value = from_first[r3][:, a : a + block] + from_second[ry][:, b : b + block]
                home = block_home(where[0], where[1] // 2, r3, r1, ry)
                context_grad[:, pl.ds(pl.multiple_of(home * block, block), block)] = value.astype(BF16)


def blocks_kernel(half, own_context, peer_context, own_grad, peer_grad, first, second):
    part = own_grad.shape[1] // 2
    block = own_context.shape[0] // 8
    span = slice(half * 4 * block, (half + 1) * 4 * block)
    value = dot(own_context[span, :], own_grad[:, :part])
    value = value + dot(peer_context[span, :], peer_grad[:, :part])
    first[...] = value.astype(first.dtype)

    def ordered(ref):
        return jnp.concatenate(
            [ref[b * block : (b + 1) * block, :] for b in second_order(half)], axis=0
        )

    value = dot(ordered(own_context), own_grad[:, part:])
    value = value + dot(ordered(peer_context), peer_grad[:, part:])
    second[...] = value.astype(second.dtype)


def shaped(shape, dtype=F32):
    return jax.ShapeDtypeStruct(shape, dtype)


def added(kept, sent, swap, bits):
    return kept + swap(sent.astype(BF16), bits).astype(F32)


def folded(value, swap, bits):
    rows = value.shape[0] // 2
    return added(value[:rows], value[rows:], swap, bits)


def all_added(value, swap, bits):
    value = lax.reduce_precision(value, 8, 7)
    return added(value, value, swap, bits)


def on_device(
    context, residual, out_weight, norm_gain, user_vectors, positive, item_ids, item_counts, lengths
):
    tokens, head = context.shape
    width = residual.shape[1]
    items_here = lengths.shape[0]
    users_here = user_vectors.shape[0]
    dp, fsdp = lax.axis_index("dp"), lax.axis_index("fsdp")
    y_lo, z, core = dp // 8, (dp // 2) % 4, dp % 2
    y_hi, x = fsdp // 4, fsdp % 4
    y = y_hi * 2 + y_lo
    where = jnp.stack([x, y, z, core]).astype(jnp.int32)
    half, part = width // 2, width // 4
    rows = out_weight.shape[0]
    gain = norm_gain[None, :]

    mine = lax.dynamic_slice(out_weight, (0, core * half), (rows, half))
    first = doubled(mine[:, :part], swap_y, 3)
    second = doubled(mine[:, part:], swap_x, 1)
    step_one = first
    first = doubled(first, swap_x, 1)
    second = doubled(second, swap_x, 3)
    firsts = [first, swap_x(first, 3)]
    seconds = [second, swap_y(second, 3)]
    pieces = firsts + seconds
    pieces = pieces + [swap_core(p) for p in pieces]

    order = [
        block_home(x, y_hi, r3, r1, ry) for r3 in range(2) for r1 in range(2) for ry in range(2)
    ]
    later = after(context, step_one)
    turned = jnp.concatenate(
        [lax.dynamic_slice(later, (0, at * rows), (tokens, rows)) for at in order], axis=1
    )

    labels = jnp.pad(positive[:, None], ((0, 0), (0, LABELS - 1))).astype(BF16)
    users = jnp.concatenate([user_vectors, labels], axis=1)
    users = doubled(users, swap_z, 1)
    users = doubled(users, swap_z, 3)
    users = doubled(users, swap_y, 1)
    labels = jnp.stack([item_ids, item_counts // 128, item_counts % 128], axis=1)
    labels = jnp.pad(labels, ((0, 0), (0, LABELS - 3))).astype(BF16)
    users, labels = lax.optimization_barrier((users, labels))

    stream, inverse, pooled, emb = pl.pallas_call(
        forward_kernel,
        out_shape=(
            shaped((tokens, width)),
            shaped((tokens, 1)),
            shaped((items_here, width)),
            shaped((items_here, width + LABELS), BF16),
        ),
        in_specs=[SMEM, SMEM, VMEM, HBM] + [VMEM] * 10,
        out_specs=(VMEM,) * 4,
        scratch_shapes=[pltpu.VMEM((tokens, width), BF16), pltpu.SemaphoreType.DMA],
        compiler_params=params(20),
        name="forward",
    )(where, lengths, turned, residual, gain, labels, *pieces)

    users = doubled(after(users, emb), swap_y, 3)
    user_pieces = [users, swap_core(users)]
    own_context = after(turned, emb).T
    peer_context = swap_core(own_context)
    for swap, bits in ((swap_x, 1), (swap_x, 3), (swap_y, 1), (swap_y, 3), (swap_z, 1)):
        emb = doubled(emb, swap, bits)
    emb_pieces = [emb, swap_z(emb, 3)]
    emb_pieces = emb_pieces + [swap_core(p) for p in emb_pieces]

    near = 4 * items_here
    items, people = 128 * items_here, 32 * users_here
    sums, user_grad = pl.pallas_call(
        functools.partial(loss_kernel, users_here, items_here),
        out_shape=(
            shaped((near, width + width // near + LABELS)),
            shaped((users_here, width), BF16),
        ),
        in_specs=[SMEM] + [VMEM] * 7,
        out_specs=(VMEM,) * 2,
        scratch_shapes=[pltpu.VMEM((people, items), F32), pltpu.VMEM((items, width), F32)],
        compiler_params=params(24),
        name="loss",
    )(where, gain, *user_pieces, *emb_pieces)
    sums = sums + swap_x(sums, 3)
    sums = sums + swap_x(sums, 1)

    residual_grad, keep, send, gain_grad, loss = pl.pallas_call(
        functools.partial(residual_kernel, 4 * people),
        out_shape=(
            shaped((tokens, width), BF16),
            shaped((tokens, half), BF16),
            shaped((tokens, half), BF16),
            shaped((1, width)),
            shaped((1, 1)),
        ),
        in_specs=[SMEM, SMEM] + [VMEM] * 5,
        out_specs=(VMEM,) * 5,
        compiler_params=params(16),
        name="residual",
    )(where, lengths, stream, inverse, pooled, gain, sums)
    peer_grad = swap_core(send)
    context_grad = pl.pallas_call(
        context_kernel,
        out_shape=shaped((tokens, head), BF16),
        in_specs=[SMEM] + [VMEM] * 10,
        out_specs=VMEM,
        compiler_params=params(14),
        name="context",
    )(where, keep, send, *pieces)

    operands = (own_context, peer_context, keep, peer_grad)

    def blocks(which, dtype, name):
        return pl.pallas_call(
            functools.partial(blocks_kernel, which),
            out_shape=(shaped((4 * rows, part), dtype),) * 2,
            in_specs=[VMEM] * 4,
            out_specs=(VMEM,) * 2,
            compiler_params=params(14),
            name=name,
        )(*operands)

    first_sent, second_sent = blocks(1, BF16, "blocks_sent")
    first, second = blocks(0, F32, "blocks_kept")
    first, second, context_grad = lax.optimization_barrier((first, second, context_grad))
    first = added(first, first_sent, swap_x, 3)
    second = added(second, second_sent, swap_y, 3)
    first = folded(first, swap_x, 1)
    second = folded(second, swap_x, 3)
    first = folded(first, swap_y, 3)
    second = folded(second, swap_x, 1)
    first = all_added(first, swap_y, 1)
    second = all_added(second, swap_z, 1)
    first = all_added(first, swap_z, 1)
    second = all_added(second, swap_z, 3)
    first = all_added(first, swap_z, 3)
    second = all_added(second, swap_y, 1)
    own = jnp.concatenate([first, second], axis=1).astype(BF16)
    other = swap_core(own)
    weight_grad = jnp.where(
        core == 0, jnp.concatenate([own, other], axis=1), jnp.concatenate([other, own], axis=1)
    )
    return (loss[0, 0], residual_grad, context_grad, weight_grad, gain_grad[0], user_grad)


def solution(mesh):
    placed = (
        P(AXES, None),
        P(AXES, None),
        P("fsdp", None),
        P(),
        P(AXES, None),
        P(AXES),
        P(AXES),
        P(AXES),
        P(AXES),
    )
    return jax.shard_map(
        on_device,
        mesh=mesh,
        in_specs=placed,
        out_specs=(P(), P(AXES, None), P(AXES, None), P("fsdp", None), P(), P(AXES, None)),
        check_vma=False,
    )
```

```python
import functools

import jax
import jax.numpy as jnp
from jax import lax
from jax.experimental import pallas as pl
from jax.experimental.pallas import tpu as pltpu
from jax.sharding import PartitionSpec as P

EPSILON = 1e-06
MASKED_FILL = -1e30
AXES = ("dp", "fsdp")
F32 = jnp.float32
BF16 = jnp.bfloat16
VMEM = pl.BlockSpec(memory_space=pltpu.VMEM)
SMEM = pl.BlockSpec(memory_space=pltpu.SMEM)
HBM = pl.BlockSpec(memory_space=pltpu.HBM)


def params(mebibytes):
    return pltpu.CompilerParams(vmem_limit_bytes=mebibytes * 1024 * 1024)


def after(value, other):
    return lax.optimization_barrier((value, other))[0]

LABELS = 128
OFFSETS = (0, 1, 3, 2)


def linear(x, y, z, c):
    return ((((y % 2) * 4 + z) * 2 + c) * 2 + y // 2) * 4 + x


def move(value, where):
    perm = []
    for x in range(4):
        for y in range(4):
            for z in range(4):
                for c in range(2):
                    perm.append((linear(x, y, z, c), linear(*where(x, y, z, c))))
    return lax.ppermute(value, AXES, perm)


def swap_core(value):
    return move(value, lambda x, y, z, c: (x, y, z, 1 - c))


def swap_x(value, bits):
    return move(value, lambda x, y, z, c: (x ^ bits, y, z, c))


def swap_y(value, bits):
    return move(value, lambda x, y, z, c: (x, y ^ bits, z, c))


def swap_z(value, bits):
    return move(value, lambda x, y, z, c: (x, y, z ^ bits, c))


def four(value, swap):
    return [value] + [swap(value, bits) for bits in OFFSETS[1:]]


def doubled(value, swap, bits):
    return lax.optimization_barrier(jnp.concatenate([value, swap(value, bits)], axis=0))


def dot(left, right):
    return jnp.dot(left, right, preferred_element_type=F32)


def contract_rows(left, right):
    return lax.dot_general(left, right, (((0,), (0,)), ((), ())), preferred_element_type=F32)


def contract_last(left, right):
    return lax.dot_general(left, right, (((1,), (1,)), ((), ())), preferred_element_type=F32)


def column_offsets(core, width):
    half, part = width // 2, width // 4
    mine = pl.multiple_of(core * half, half)
    other = pl.multiple_of((1 - core) * half, half)
    return (
        (mine, pl.multiple_of(mine + part, part)),
        (other, pl.multiple_of(other + part, part)),
    )


def with_ry(ry):
    return [q * 2 + ry for q in range(4)]


def block_home(x, y_hi, q, ry):
    return (y_hi ^ ry) * 4 + (x ^ OFFSETS[q])


def forward_kernel(where, lengths, context, residual, gain, labels, *refs):
    firsts, seconds = (refs[0:2], refs[6:8]), (refs[2:6], refs[8:12])
    stream, inverse, pooled, embedding, added_rows, sem = refs[12:]
    tokens, width = residual.shape
    part = width // 4
    block = context.shape[1] // 8
    items = lengths.shape[0]
    length = tokens // items
    copy = pltpu.make_async_copy(residual, added_rows, sem)
    copy.start()
    ordered = [
        jnp.concatenate([context[:, b * block : (b + 1) * block] for b in with_ry(ry)], axis=1)
        for ry in range(2)
    ]
    for side, (first_at, second_at) in enumerate(column_offsets(where[3], width)):
        stream[:, pl.ds(first_at, part)] = dot(ordered[0], firsts[side][0][...]) + dot(
            ordered[1], firsts[side][1][...]
        )
        stream[:, pl.ds(second_at, part)] = sum(
            dot(context[:, q * 2 * block : (q + 1) * 2 * block], seconds[side][q][...])
            for q in range(4)
        )
    copy.wait()
    for i in range(items):
        span = slice(i * length, (i + 1) * length)
        rows = stream[span, :] + added_rows[span, :].astype(F32)
        stream[span, :] = rows
        inv = lax.rsqrt(jnp.mean(rows * rows, axis=-1, keepdims=True) + EPSILON)
        inverse[i * length : (i + 1) * length, :] = inv
        position = lax.broadcasted_iota(jnp.int32, (length, 1), 0)
        kept = jnp.where(position < lengths[i], inv, 0.0)
        total = jnp.sum(rows * kept, axis=0, keepdims=True)
        pooled[i : i + 1, :] = total * gain[...] / lengths[i].astype(F32)
    pool = pooled[...]
    scale = lax.rsqrt(jnp.mean(pool * pool, axis=-1, keepdims=True) + EPSILON)
    embedding[:, :width] = (pool * scale).astype(BF16)
    embedding[:, width:] = labels[...]


def bit(value, k):
    return (value >> k) & 1


def one_hot_turn(rows, home):
    to = lax.broadcasted_iota(jnp.int32, (rows, rows), 0)
    of = lax.broadcasted_iota(jnp.int32, (rows, rows), 1)
    return jnp.where(to == home(of), 1.0, 0.0).astype(BF16)


def loss_kernel(users_here, items_here, where, gain, *refs):
    user_refs, emb_refs = refs[:2], refs[2:10]
    sums, user_grad, grads, emb_grads = refs[10:14], refs[14], refs[15], refs[16]
    x, y, z, core = where[0], where[1], where[2], where[3]
    group, full = emb_refs[0].shape
    width = full - LABELS
    items = 8 * group
    people = 2 * user_refs[0].shape[0]

    def item_home(s):
        one = s // items_here
        ax = x ^ bit(one, 0) ^ (3 * bit(one, 1))
        ay = y ^ bit(one, 2) ^ (3 * bit(one, 3))
        az = z ^ bit(one, 4) ^ (3 * bit(one, 5))
        ac = core ^ bit(one, 6)
        return (((ac * 4 + az) * 4 + ay) * 4 + ax) * items_here + s % items_here

    def user_home(s):
        one = s // users_here
        az = z ^ bit(one, 0) ^ (3 * bit(one, 1))
        ay = y ^ bit(one, 2) ^ (3 * bit(one, 3))
        ac = core ^ bit(one, 4)
        return ((ac * 4 + az) * 4 + ay) * users_here + s % users_here

    placed = jnp.concatenate([ref[...] for ref in emb_refs], axis=0)
    turned = dot(one_hot_turn(items, item_home), placed).astype(BF16)
    emb, labels = turned[:, :width], turned[:, width:]
    placed = jnp.concatenate([ref[...] for ref in user_refs], axis=0)
    turned = dot(one_hot_turn(people, user_home), placed).astype(BF16)
    users = turned[:, :width]
    positive = turned[:, width : width + 1].astype(F32)
    item_labels = contract_rows(labels, one_hot_turn(items, lambda s: s))
    ids = item_labels[0:1, :]
    log_counts = jnp.log(item_labels[1:2, :] * 128.0 + item_labels[2:3, :])
    item = lax.broadcasted_iota(jnp.int32, (1, items), 1)
    chip = item // items_here
    index = linear(chip % 4, (chip // 4) % 4, (chip // 16) % 4, chip // 64) * items_here
    index = (index + item % items_here).astype(F32)
    onehot = index == positive
    positive_id = jnp.sum(jnp.where(onehot, ids, 0.0), axis=1, keepdims=True)
    excluded = (ids == positive_id) & jnp.logical_not(onehot)
    scores = contract_last(users, emb)
    logits = jnp.where(excluded, MASKED_FILL, scores - log_counts)
    row_max = jnp.max(logits, axis=1, keepdims=True)
    weights = jnp.where(excluded, 0.0, jnp.exp(logits - row_max))
    row_total = jnp.sum(weights, axis=1, keepdims=True)
    picked = jnp.sum(jnp.where(onehot, logits, 0.0), axis=1, keepdims=True)
    losses = row_max + jnp.log(row_total) - picked
    grad = (weights / row_total - jnp.where(onehot, 1.0, 0.0)).astype(BF16)
    grads[...] = grad.astype(F32)
    all_grads = contract_rows(grad, users)
    emb_grads[...] = all_grads
    emb_float = emb.astype(F32)
    product = emb_float * all_grads
    mean = jnp.mean(product, axis=-1, keepdims=True)
    gain_sum = jnp.sum(product - emb_float * emb_float * mean, axis=0, keepdims=True)
    place = (core * 4 + z) * 4 + y
    near = 4 * items_here
    rows = emb_grads[pl.ds(pl.multiple_of(place * near, near), near), :]
    line = lax.broadcasted_iota(jnp.int32, (near, 1), 0)
    loss = jnp.broadcast_to(jnp.sum(losses, axis=0, keepdims=True), (1, width))
    for q in range(4):
        for i in range(items_here):
            chosen = line == (x ^ OFFSETS[q]) * items_here + i
            sums[q][i : i + 1, :] = jnp.sum(jnp.where(chosen, rows, 0.0), axis=0, keepdims=True)
        sums[q][items_here : items_here + 1, :] = gain_sum
        sums[q][items_here + 1 :, :] = loss
    own = grads[pl.ds(pl.multiple_of(place * users_here, users_here), users_here), :]
    user_grad[...] = dot(own.astype(BF16), emb).astype(BF16)


def residual_kernel(people, where, lengths, stream, inverse, pooled, gain, *refs):
    residual_grad, keep, send, gain_grad, loss = refs[4:]
    sums = (refs[0][...] + refs[1][...]) + (refs[2][...] + refs[3][...])
    tokens, width = stream.shape
    half = width // 2
    items = lengths.shape[0]
    length = tokens // items
    for i in range(items):
        mine = sums[i : i + 1, :]
        pool = pooled[i : i + 1, :]
        scale = lax.rsqrt(jnp.mean(pool * pool, axis=-1, keepdims=True) + EPSILON)
        pool_grad = scale * mine - pool * scale * scale * scale * jnp.mean(
            pool * mine, axis=-1, keepdims=True
        )
        row = gain[...] * pool_grad / lengths[i].astype(F32)
        span = slice(i * length, (i + 1) * length)
        rows = stream[span, :]
        inv = inverse[span, :]
        position = lax.broadcasted_iota(jnp.int32, (length, 1), 0)
        kept = jnp.where(position < lengths[i], inv, 0.0)
        mean = jnp.mean(rows * row, axis=-1, keepdims=True)
        residual_grad[span, :] = (kept * row - rows * (kept * inv * inv * mean)).astype(BF16)
    keep[...] = residual_grad[:, pl.ds(pl.multiple_of(where[3] * half, half), half)]
    send[...] = residual_grad[:, pl.ds(pl.multiple_of((1 - where[3]) * half, half), half)]
    gain_grad[...] = sums[items : items + 1, :] / gain[...]
    loss[...] = sums[items + 1 :, 0:1] / people


def context_kernel(where, keep, send, *refs):
    firsts, seconds = (refs[0:2], refs[6:8]), (refs[2:6], refs[8:12])
    context_grad = refs[12]
    part = keep.shape[1] // 2
    block = context_grad.shape[1] // 8
    near = [ref[:, :part] for ref in (keep, send)]
    far = [ref[:, part:] for ref in (keep, send)]
    from_first = [
        sum(contract_last(near[s], firsts[s][ry][...]) for s in range(2)) for ry in range(2)
    ]
    for q in range(4):
        from_second = sum(contract_last(far[s], seconds[s][q][...]) for s in range(2))
        for ry in range(2):
            value = (
                from_first[ry][:, q * block : (q + 1) * block]
                + from_second[:, ry * block : (ry + 1) * block]
            )
            home = block_home(where[0], where[1] // 2, q, ry)
            context_grad[:, pl.ds(pl.multiple_of(home * block, block), block)] = value.astype(BF16)


def blocks_kernel(half, own_context, peer_context, own_grad, peer_grad, first, second):
    part = own_grad.shape[1] // 2
    block = own_context.shape[0] // 8
    span = slice(half * 4 * block, (half + 1) * 4 * block)
    value = dot(own_context[span, :], own_grad[:, :part])
    value = value + dot(peer_context[span, :], peer_grad[:, :part])
    first[...] = value.astype(first.dtype)

    def ordered(ref):
        return jnp.concatenate(
            [ref[b * block : (b + 1) * block, :] for b in with_ry(half)], axis=0
        )

    value = dot(ordered(own_context), own_grad[:, part:])
    value = value + dot(ordered(peer_context), peer_grad[:, part:])
    second[...] = value.astype(second.dtype)


def shaped(shape, dtype=F32):
    return jax.ShapeDtypeStruct(shape, dtype)


def added(kept, sent, swap, bits):
    return kept + swap(sent.astype(BF16), bits).astype(F32)


def folded(value, swap, bits):
    rows = value.shape[0] // 2
    return added(value[:rows], value[rows:], swap, bits)


def all_added(value, swap, bits):
    value = lax.reduce_precision(value, 8, 7)
    return added(value, value, swap, bits)


def on_device(
    context, residual, out_weight, norm_gain, user_vectors, positive, item_ids, item_counts, lengths
):
    tokens, head = context.shape
    width = residual.shape[1]
    items_here = lengths.shape[0]
    users_here = user_vectors.shape[0]
    dp, fsdp = lax.axis_index("dp"), lax.axis_index("fsdp")
    y_lo, z, core = dp // 8, (dp // 2) % 4, dp % 2
    y_hi, x = fsdp // 4, fsdp % 4
    y = y_hi * 2 + y_lo
    where = jnp.stack([x, y, z, core]).astype(jnp.int32)
    half, part = width // 2, width // 4
    rows = out_weight.shape[0]
    gain = norm_gain[None, :]

    mine = lax.dynamic_slice(out_weight, (0, core * half), (rows, half))
    second = doubled(mine[:, part:], swap_y, 3)
    first = lax.optimization_barrier(jnp.concatenate(four(mine[:, :part], swap_x), axis=0))
    pieces = [first, swap_y(first, 3)] + four(second, swap_x)
    pieces = pieces + [swap_core(p) for p in pieces]

    order = [block_home(x, y_hi, q, ry) for q in range(4) for ry in range(2)]
    later = after(context, second)
    turned = jnp.concatenate(
        [lax.dynamic_slice(later, (0, at * rows), (tokens, rows)) for at in order], axis=1
    )

    labels = jnp.pad(positive[:, None], ((0, 0), (0, LABELS - 1))).astype(BF16)
    users = jnp.concatenate([user_vectors, labels], axis=1)
    users = doubled(users, swap_z, 1)
    users = doubled(users, swap_z, 3)
    labels = jnp.stack([item_ids, item_counts // 128, item_counts % 128], axis=1)
    labels = jnp.pad(labels, ((0, 0), (0, LABELS - 3))).astype(BF16)
    users, labels = lax.optimization_barrier((users, labels))

    stream, inverse, pooled, emb = pl.pallas_call(
        forward_kernel,
        out_shape=(
            shaped((tokens, width)),
            shaped((tokens, 1)),
            shaped((items_here, width)),
            shaped((items_here, width + LABELS), BF16),
        ),
        in_specs=[SMEM, SMEM, VMEM, HBM] + [VMEM] * 14,
        out_specs=(VMEM,) * 4,
        scratch_shapes=[pltpu.VMEM((tokens, width), BF16), pltpu.SemaphoreType.DMA],
        compiler_params=params(20),
        name="forward",
    )(where, lengths, turned, residual, gain, labels, *pieces)

    own_context = after(turned, emb).T
    peer_context = swap_core(own_context)
    emb = lax.optimization_barrier(jnp.concatenate(four(emb, swap_x), axis=0))
    users = doubled(doubled(after(users, emb), swap_y, 1), swap_y, 3)
    user_pieces = [users, swap_core(users)]
    emb = lax.optimization_barrier(jnp.concatenate(four(emb, swap_y), axis=0))
    emb_pieces = four(emb, swap_z)
    emb_pieces = emb_pieces + [swap_core(p) for p in emb_pieces]

    items, people = 128 * items_here, 32 * users_here
    *sums, user_grad = pl.pallas_call(
        functools.partial(loss_kernel, users_here, items_here),
        out_shape=(shaped((items_here + 2, width)),) * 4 + (shaped((users_here, width), BF16),),
        in_specs=[SMEM] + [VMEM] * 11,
        out_specs=(VMEM,) * 5,
        scratch_shapes=[pltpu.VMEM((people, items), F32), pltpu.VMEM((items, width), F32)],
        compiler_params=params(24),
        name="loss",
    )(where, gain, *user_pieces, *emb_pieces)
    sums = [sums[0]] + [swap_x(sums[q], OFFSETS[q]) for q in (1, 2, 3)]

    residual_grad, keep, send, gain_grad, loss = pl.pallas_call(
        functools.partial(residual_kernel, 4 * people),
        out_shape=(
            shaped((tokens, width), BF16),
            shaped((tokens, half), BF16),
            shaped((tokens, half), BF16),
            shaped((1, width)),
            shaped((1, 1)),
        ),
        in_specs=[SMEM, SMEM] + [VMEM] * 8,
        out_specs=(VMEM,) * 5,
        compiler_params=params(16),
        name="residual",
    )(where, lengths, stream, inverse, pooled, gain, *sums)
    peer_grad = swap_core(send)
    context_grad = pl.pallas_call(
        context_kernel,
        out_shape=shaped((tokens, head), BF16),
        in_specs=[SMEM] + [VMEM] * 14,
        out_specs=VMEM,
        compiler_params=params(14),
        name="context",
    )(where, keep, send, *pieces)

    operands = (own_context, peer_context, keep, peer_grad)

    def blocks(which, dtype, name):
        return pl.pallas_call(
            functools.partial(blocks_kernel, which),
            out_shape=(shaped((4 * rows, part), dtype),) * 2,
            in_specs=[VMEM] * 4,
            out_specs=(VMEM,) * 2,
            compiler_params=params(14),
            name=name,
        )(*operands)

    first_sent, second_sent = blocks(1, BF16, "blocks_sent")
    first, second = blocks(0, F32, "blocks_kept")
    first, second, context_grad = lax.optimization_barrier((first, second, context_grad))
    first = added(first, first_sent, swap_x, 3)
    second = added(second, second_sent, swap_y, 3)
    first = folded(first, swap_x, 1)
    second = folded(second, swap_x, 3)
    first = folded(first, swap_y, 3)
    second = folded(second, swap_x, 1)
    first = all_added(first, swap_y, 1)
    second = all_added(second, swap_z, 1)
    first = all_added(first, swap_z, 1)
    second = all_added(second, swap_z, 3)
    first = all_added(first, swap_z, 3)
    second = all_added(second, swap_y, 1)
    own = jnp.concatenate([first, second], axis=1).astype(BF16)
    other = swap_core(own)
    weight_grad = jnp.where(
        core == 0, jnp.concatenate([own, other], axis=1), jnp.concatenate([other, own], axis=1)
    )
    return (loss[0, 0], residual_grad, context_grad, weight_grad, gain_grad[0], user_grad)


def solution(mesh):
    placed = (
        P(AXES, None),
        P(AXES, None),
        P("fsdp", None),
        P(),
        P(AXES, None),
        P(AXES),
        P(AXES),
        P(AXES),
        P(AXES),
    )
    return jax.shard_map(
        on_device,
        mesh=mesh,
        in_specs=placed,
        out_specs=(P(), P(AXES, None), P(AXES, None), P("fsdp", None), P(), P(AXES, None)),
        check_vma=False,
    )
```

```python
import functools

import jax
import jax.numpy as jnp
from jax import lax
from jax.experimental import pallas as pl
from jax.experimental.pallas import tpu as pltpu
from jax.sharding import PartitionSpec as P

EPSILON = 1e-06
MASKED_FILL = -1e30
AXES = ("dp", "fsdp")
F32 = jnp.float32
BF16 = jnp.bfloat16
VMEM = pl.BlockSpec(memory_space=pltpu.VMEM)
SMEM = pl.BlockSpec(memory_space=pltpu.SMEM)
HBM = pl.BlockSpec(memory_space=pltpu.HBM)
ANY = pl.BlockSpec(memory_space=pl.ANY)


def params(mebibytes):
    return pltpu.CompilerParams(vmem_limit_bytes=mebibytes * 1024 * 1024)


def after(value, other):
    return lax.optimization_barrier((value, other))[0]

LABELS = 128
POSITIVE = 8
OFFSETS = (0, 1, 3, 2)


def linear(x, y, z, c):
    return ((((y % 2) * 4 + z) * 2 + c) * 2 + y // 2) * 4 + x


def move(value, where):
    perm = []
    for x in range(4):
        for y in range(4):
            for z in range(4):
                for c in range(2):
                    perm.append((linear(x, y, z, c), linear(*where(x, y, z, c))))
    return lax.ppermute(value, AXES, perm)


def swap_core(value):
    return move(value, lambda x, y, z, c: (x, y, z, 1 - c))


def swap_x(value, bits):
    return move(value, lambda x, y, z, c: (x ^ bits, y, z, c))


def swap_y(value, bits):
    return move(value, lambda x, y, z, c: (x, y ^ bits, z, c))


def swap_z(value, bits):
    return move(value, lambda x, y, z, c: (x, y, z ^ bits, c))


def four(value, swap):
    return [value] + [swap(value, bits) for bits in OFFSETS[1:]]


def doubled(value, swap, bits):
    return lax.optimization_barrier(jnp.concatenate([value, swap(value, bits)], axis=0))


def dot(left, right):
    return jnp.dot(left, right, preferred_element_type=F32)


def contract_rows(left, right):
    return lax.dot_general(left, right, (((0,), (0,)), ((), ())), preferred_element_type=F32)


def contract_last(left, right):
    return lax.dot_general(left, right, (((1,), (1,)), ((), ())), preferred_element_type=F32)


def column_offsets(core, width):
    half, part = width // 2, width // 4
    mine = pl.multiple_of(core * half, half)
    other = pl.multiple_of((1 - core) * half, half)
    return (
        (mine, pl.multiple_of(mine + part, part)),
        (other, pl.multiple_of(other + part, part)),
    )


def block_home(x, y_hi, q, ry):
    return (y_hi ^ ry) * 4 + (x ^ OFFSETS[q])


def blocks_of(ref, where, pairs, block):
    picked = []
    for q, ry in pairs:
        home = block_home(where[0], where[1] // 2, q, ry)
        picked.append(ref[:, pl.ds(pl.multiple_of(home * block, block), block)])
    return jnp.concatenate(picked, axis=1)


def weight_rows(ref, block):
    rows = ref.shape[0] // 2
    return jnp.concatenate([ref[:block, :], ref[rows : rows + block, :]], axis=0)


def forward_kernel(where, lengths, ids, counts, positive, context, residual, gain, *refs):
    firsts, seconds = (refs[0:2], refs[6:8]), (refs[2:6], refs[8:12])
    stream, inverse, pooled, embedding, added_rows, sem = refs[12:]
    tokens, width = residual.shape
    part = width // 4
    block = context.shape[1] // 8
    items = lengths.shape[0]
    length = tokens // items
    copy = pltpu.make_async_copy(residual, added_rows, sem)
    copy.start()
    by_ry = [blocks_of(context, where, [(q, ry) for q in range(4)], block) for ry in range(2)]
    by_q = [blocks_of(context, where, [(q, 0), (q, 1)], block) for q in range(4)]
    for side, (first_at, second_at) in enumerate(column_offsets(where[3], width)):
        stream[:, pl.ds(first_at, part)] = sum(
            dot(by_ry[ry], firsts[side][ry][...]) for ry in range(2)
        )
        stream[:, pl.ds(second_at, part)] = sum(
            dot(by_q[q], weight_rows(seconds[side][q], block)) for q in range(4)
        )
    copy.wait()
    for i in range(items):
        span = slice(i * length, (i + 1) * length)
        rows = stream[span, :] + added_rows[span, :].astype(F32)
        stream[span, :] = rows
        inv = lax.rsqrt(jnp.mean(rows * rows, axis=-1, keepdims=True) + EPSILON)
        inverse[i * length : (i + 1) * length, :] = inv
        position = lax.broadcasted_iota(jnp.int32, (length, 1), 0)
        kept = jnp.where(position < lengths[i], inv, 0.0)
        total = jnp.sum(rows * kept, axis=0, keepdims=True)
        pooled[i : i + 1, :] = total * gain[...] / lengths[i].astype(F32)
    pool = pooled[...]
    scale = lax.rsqrt(jnp.mean(pool * pool, axis=-1, keepdims=True) + EPSILON)
    embedding[:, :width] = (pool * scale).astype(BF16)
    row = lax.broadcasted_iota(jnp.int32, (items, LABELS), 0)
    lane = lax.broadcasted_iota(jnp.int32, (items, LABELS), 1)
    labels = jnp.zeros((items, LABELS), jnp.int32)
    for i in range(items):
        for at, value in enumerate((ids[i], counts[i] // 128, counts[i] % 128)):
            labels = jnp.where((row == i) & (lane == at), value, labels)
    for u in range(positive.shape[0]):
        labels = jnp.where((row == 0) & (lane == POSITIVE + u), positive[u], labels)
    embedding[:, width:] = labels.astype(F32).astype(BF16)


def bit(value, k):
    return (value >> k) & 1


def one_hot_turn(rows, home):
    to = lax.broadcasted_iota(jnp.int32, (rows, rows), 0)
    of = lax.broadcasted_iota(jnp.int32, (rows, rows), 1)
    return jnp.where(to == home(of), 1.0, 0.0).astype(BF16)


def loss_kernel(users_here, items_here, block, where, gain, *refs):
    piece_refs, emb_refs = refs[:8], refs[8:16]
    sums, user_grad, grads, emb_grads, riders, sems = refs[16:20], *refs[20:]
    x, y, z, core = where[0], where[1], where[2], where[3]
    group, full = emb_refs[0].shape
    width = full - LABELS
    items = 8 * group
    people = 16 * users_here
    half_rows, part = piece_refs[0].shape[0] // 2, piece_refs[0].shape[1]
    parts = width // part
    rode = parts * users_here
    copies = []
    for n in range(8):
        for ry in range(2):
            copies.append(
                pltpu.make_async_copy(
                    piece_refs[n].at[pl.ds(ry * half_rows + block, rode)],
                    riders.at[pl.ds((n * 2 + ry) * rode, rode)],
                    sems.at[n * 2 + ry],
                )
            )
    for copy in copies:
        copy.start()

    def item_home(s):
        one = s // items_here
        ax = x ^ bit(one, 0) ^ (3 * bit(one, 1))
        ay = y ^ bit(one, 2) ^ (3 * bit(one, 3))
        az = z ^ bit(one, 4) ^ (3 * bit(one, 5))
        ac = core ^ bit(one, 6)
        return (((ac * 4 + az) * 4 + ay) * 4 + ax) * items_here + s % items_here

    placed = jnp.concatenate([ref[...] for ref in emb_refs], axis=0)
    turned = dot(one_hot_turn(items, item_home), placed).astype(BF16)
    emb, labels = turned[:, :width], turned[:, width:]
    for copy in copies:
        copy.wait()
    to = lax.broadcasted_iota(jnp.int32, (people, 16 * rode), 0)
    of = lax.broadcasted_iota(jnp.int32, (people, 16 * rode), 1)
    one = of // rode
    holder = ((core ^ bit(one, 3)) * 2 + ((y // 2) ^ bit(one, 0))) * 4 + (
        x ^ bit(one, 1) ^ (3 * bit(one, 2))
    )
    home = holder * users_here + of % users_here
    column = (of % rode) // users_here
    users = jnp.concatenate(
        [
            dot(
                jnp.where((to == home) & (column == j), 1.0, 0.0).astype(BF16), riders[...]
            ).astype(BF16)
            for j in range(parts)
        ],
        axis=1,
    )
    person = lax.broadcasted_iota(jnp.int32, (people, items), 0)
    at = lax.broadcasted_iota(jnp.int32, (people, items), 1)
    g = person // users_here
    g_y = jnp.where((g // 4) % 2 == y // 2, y, 3 - y)
    g_row = (((g // 8 * 4 + z) * 4 + g_y) * 4 + g % 4) * items_here
    positives = dot(jnp.where(at == g_row, 1.0, 0.0).astype(BF16), labels)
    lane = lax.broadcasted_iota(jnp.int32, (people, LABELS), 1)
    slot = lax.broadcasted_iota(jnp.int32, (people, LABELS), 0) % users_here
    positive = jnp.sum(jnp.where(lane == POSITIVE + slot, positives, 0.0), axis=1, keepdims=True)
    item_labels = contract_rows(labels, one_hot_turn(items, lambda s: s))
    ids = item_labels[0:1, :]
    log_counts = jnp.log(item_labels[1:2, :] * 128.0 + item_labels[2:3, :])
    item = lax.broadcasted_iota(jnp.int32, (1, items), 1)
    chip = item // items_here
    index = linear(chip % 4, (chip // 4) % 4, (chip // 16) % 4, chip // 64) * items_here
    index = (index + item % items_here).astype(F32)
    onehot = index == positive
    positive_id = jnp.sum(jnp.where(onehot, ids, 0.0), axis=1, keepdims=True)
    excluded = (ids == positive_id) & jnp.logical_not(onehot)
    scores = contract_last(users, emb)
    logits = jnp.where(excluded, MASKED_FILL, scores - log_counts)
    row_max = jnp.max(logits, axis=1, keepdims=True)
    weights = jnp.where(excluded, 0.0, jnp.exp(logits - row_max))
    row_total = jnp.sum(weights, axis=1, keepdims=True)
    picked = jnp.sum(jnp.where(onehot, logits, 0.0), axis=1, keepdims=True)
    losses = row_max + jnp.log(row_total) - picked
    grad = (weights / row_total - jnp.where(onehot, 1.0, 0.0)).astype(BF16)
    grads[...] = grad.astype(F32)
    all_grads = contract_rows(grad, users)
    emb_grads[...] = all_grads
    emb_float = emb.astype(F32)
    product = emb_float * all_grads
    mean = jnp.mean(product, axis=-1, keepdims=True)
    gain_sum = jnp.sum(product - emb_float * emb_float * mean, axis=0, keepdims=True)
    line = lax.broadcasted_iota(jnp.int32, (8 * items_here, 1), 0)
    loss = jnp.broadcast_to(jnp.sum(losses, axis=0, keepdims=True), (1, width))
    for q in range(4):
        az = z ^ OFFSETS[q]
        start = ((core * 4 + az) * 4 + (y // 2) * 2) * 4 * items_here
        rows = emb_grads[pl.ds(pl.multiple_of(start, 8 * items_here), 8 * items_here), :]
        for other in range(2):
            for i in range(items_here):
                chosen = line == (((y % 2) ^ other) * 4 + x) * items_here + i
                n = other * items_here + i
                sums[q][n : n + 1, :] = jnp.sum(
                    jnp.where(chosen, rows, 0.0), axis=0, keepdims=True
                )
        sums[q][2 * items_here : 2 * items_here + 1, :] = gain_sum
        sums[q][2 * items_here + 1 :, :] = jnp.broadcast_to(loss, (6 - 2 * items_here + 1, width))
    place = ((core * 2 + y // 2) * 4 + x) * users_here
    own = grads[pl.ds(pl.multiple_of(place, users_here), users_here), :]
    user_grad[...] = dot(own.astype(BF16), emb).astype(BF16)


def residual_kernel(people, where, lengths, stream, inverse, pooled, gain, *refs):
    own_sums, other_sums, residual_grad, keep, send, gain_grad, loss = refs
    tokens, width = stream.shape
    half = width // 2
    items = lengths.shape[0]
    length = tokens // items
    for i in range(items):
        mine = own_sums[i : i + 1, :] + other_sums[items + i : items + i + 1, :]
        pool = pooled[i : i + 1, :]
        scale = lax.rsqrt(jnp.mean(pool * pool, axis=-1, keepdims=True) + EPSILON)
        pool_grad = scale * mine - pool * scale * scale * scale * jnp.mean(
            pool * mine, axis=-1, keepdims=True
        )
        row = gain[...] * pool_grad / lengths[i].astype(F32)
        span = slice(i * length, (i + 1) * length)
        rows = stream[span, :]
        inv = inverse[span, :]
        position = lax.broadcasted_iota(jnp.int32, (length, 1), 0)
        kept = jnp.where(position < lengths[i], inv, 0.0)
        mean = jnp.mean(rows * row, axis=-1, keepdims=True)
        residual_grad[span, :] = (kept * row - rows * (kept * inv * inv * mean)).astype(BF16)
    keep[...] = residual_grad[:, pl.ds(pl.multiple_of(where[3] * half, half), half)]
    send[...] = residual_grad[:, pl.ds(pl.multiple_of((1 - where[3]) * half, half), half)]
    at = 2 * items
    gain_grad[...] = (own_sums[at : at + 1, :] + other_sums[at : at + 1, :]) / gain[...]
    at = at + 1
    loss[...] = (own_sums[at : at + 1, 0:1] + other_sums[at : at + 1, 0:1]) / people


def context_kernel(where, keep, send, *refs):
    firsts, seconds = (refs[0:2], refs[6:8]), (refs[2:6], refs[8:12])
    context_grad = refs[12]
    part = keep.shape[1] // 2
    block = context_grad.shape[1] // 8
    near = [ref[:, :part] for ref in (keep, send)]
    far = [ref[:, part:] for ref in (keep, send)]
    from_first = [
        sum(contract_last(near[s], firsts[s][ry][...]) for s in range(2)) for ry in range(2)
    ]
    for q in range(4):
        from_second = sum(contract_last(far[s], weight_rows(seconds[s][q], block)) for s in range(2))
        for ry in range(2):
            value = (
                from_first[ry][:, q * block : (q + 1) * block]
                + from_second[:, ry * block : (ry + 1) * block]
            )
            home = block_home(where[0], where[1] // 2, q, ry)
            context_grad[:, pl.ds(pl.multiple_of(home * block, block), block)] = value.astype(BF16)


def blocks_kernel(half, where, own_context, peer_context, own_grad, peer_grad, first, second):
    part = own_grad.shape[1] // 2
    block = own_context.shape[1] // 8

    def product(pairs, at):
        return contract_rows(
            blocks_of(own_context, where, pairs, block), own_grad[:, at : at + part]
        ) + contract_rows(blocks_of(peer_context, where, pairs, block), peer_grad[:, at : at + part])

    pairs = [(q, ry) for q in (2 * half, 2 * half + 1) for ry in range(2)]
    first[...] = product(pairs, 0).astype(first.dtype)
    second[...] = product([(q, half) for q in range(4)], part).astype(second.dtype)


def shaped(shape, dtype=F32):
    return jax.ShapeDtypeStruct(shape, dtype)


def added(kept, sent, swap, bits):
    return kept + swap(sent.astype(BF16), bits).astype(F32)


def folded(value, swap, bits):
    rows = value.shape[0] // 2
    return added(value[:rows], value[rows:], swap, bits)


def all_added(value, swap, bits):
    value = lax.reduce_precision(value, 8, 7)
    return added(value, value, swap, bits)


def on_device(
    context, residual, out_weight, norm_gain, user_vectors, positive, item_ids, item_counts, lengths
):
    tokens, head = context.shape
    width = residual.shape[1]
    items_here = lengths.shape[0]
    users_here = user_vectors.shape[0]
    dp, fsdp = lax.axis_index("dp"), lax.axis_index("fsdp")
    y_lo, z, core = dp // 8, (dp // 2) % 4, dp % 2
    y_hi, x = fsdp // 4, fsdp % 4
    y = y_hi * 2 + y_lo
    where = jnp.stack([x, y, z, core]).astype(jnp.int32)
    half, part = width // 2, width // 4
    rows = out_weight.shape[0]
    gain = norm_gain[None, :]

    mine = lax.dynamic_slice(out_weight, (0, core * half), (rows, half))
    riders = [user_vectors[:, j * part : (j + 1) * part] for j in range(width // part)]
    second = doubled(jnp.concatenate([mine[:, part:]] + riders, axis=0), swap_y, 3)
    first = lax.optimization_barrier(jnp.concatenate(four(mine[:, :part], swap_x), axis=0))
    pieces = [first, swap_y(first, 3)] + four(second, swap_x)
    pieces = pieces + [swap_core(p) for p in pieces]

    stream, inverse, pooled, emb = pl.pallas_call(
        forward_kernel,
        out_shape=(
            shaped((tokens, width)),
            shaped((tokens, 1)),
            shaped((items_here, width)),
            shaped((items_here, width + LABELS), BF16),
        ),
        in_specs=[SMEM] * 5 + [VMEM, HBM] + [VMEM] * 13,
        out_specs=(VMEM,) * 4,
        scratch_shapes=[pltpu.VMEM((tokens, width), BF16), pltpu.SemaphoreType.DMA],
        compiler_params=params(20),
        name="forward",
    )(where, lengths, item_ids, item_counts, positive, context, residual, gain, *pieces)

    emb = lax.optimization_barrier(jnp.concatenate(four(emb, swap_x), axis=0))
    peer_context = swap_core(after(context, emb))
    emb = lax.optimization_barrier(jnp.concatenate(four(emb, swap_y), axis=0))
    emb_pieces = four(emb, swap_z)
    emb_pieces = emb_pieces + [swap_core(p) for p in emb_pieces]

    items, people = 128 * items_here, 16 * users_here
    riding = pieces[2:6] + pieces[8:12]
    *sums, user_grad = pl.pallas_call(
        functools.partial(loss_kernel, users_here, items_here, rows),
        out_shape=(shaped((8, width)),) * 4 + (shaped((users_here, width), BF16),),
        in_specs=[SMEM, VMEM] + [ANY] * 8 + [VMEM] * 8,
        out_specs=(VMEM,) * 5,
        scratch_shapes=[
            pltpu.VMEM((people, items), F32),
            pltpu.VMEM((items, width), F32),
            pltpu.VMEM((people * (width // part), part), BF16),
            pltpu.SemaphoreType.DMA((16,)),
        ],
        compiler_params=params(24),
        name="loss",
    )(where, gain, *riding, *emb_pieces)
    sums = [sums[0]] + [swap_z(sums[q], OFFSETS[q]) for q in (1, 2, 3)]
    sums = (sums[0] + sums[1]) + (sums[2] + sums[3])

    residual_grad, keep, send, gain_grad, loss = pl.pallas_call(
        functools.partial(residual_kernel, 8 * people),
        out_shape=(
            shaped((tokens, width), BF16),
            shaped((tokens, half), BF16),
            shaped((tokens, half), BF16),
            shaped((1, width)),
            shaped((1, 1)),
        ),
        in_specs=[SMEM, SMEM] + [VMEM] * 6,
        out_specs=(VMEM,) * 5,
        compiler_params=params(16),
        name="residual",
    )(where, lengths, stream, inverse, pooled, gain, sums, swap_y(sums, 1))
    peer_grad = swap_core(send)
    context_grad = pl.pallas_call(
        context_kernel,
        out_shape=shaped((tokens, head), BF16),
        in_specs=[SMEM] + [VMEM] * 14,
        out_specs=VMEM,
        compiler_params=params(14),
        name="context",
    )(where, keep, send, *pieces)

    operands = (where, context, peer_context, keep, peer_grad)

    def blocks(which, dtype, name):
        return pl.pallas_call(
            functools.partial(blocks_kernel, which),
            out_shape=(shaped((4 * rows, part), dtype),) * 2,
            in_specs=[SMEM] + [VMEM] * 4,
            out_specs=(VMEM,) * 2,
            compiler_params=params(14),
            name=name,
        )(*operands)

    first_sent, second_sent = blocks(1, BF16, "blocks_sent")
    first, second = blocks(0, F32, "blocks_kept")
    first, second, context_grad = lax.optimization_barrier((first, second, context_grad))
    first = added(first, first_sent, swap_x, 3)
    second = added(second, second_sent, swap_y, 3)
    first = folded(first, swap_x, 1)
    second = folded(second, swap_x, 3)
    first = folded(first, swap_y, 3)
    second = folded(second, swap_x, 1)
    first = all_added(first, swap_y, 1)
    second = all_added(second, swap_z, 1)
    first = all_added(first, swap_z, 1)
    second = all_added(second, swap_z, 3)
    first = all_added(first, swap_z, 3)
    second = all_added(second, swap_y, 1)
    own = jnp.concatenate([first, second], axis=1).astype(BF16)
    other = swap_core(own)
    weight_grad = jnp.where(
        core == 0, jnp.concatenate([own, other], axis=1), jnp.concatenate([other, own], axis=1)
    )
    return (loss[0, 0], residual_grad, context_grad, weight_grad, gain_grad[0], user_grad)


def solution(mesh):
    placed = (
        P(AXES, None),
        P(AXES, None),
        P("fsdp", None),
        P(),
        P(AXES, None),
        P(AXES),
        P(AXES),
        P(AXES),
        P(AXES),
    )
    return jax.shard_map(
        on_device,
        mesh=mesh,
        in_specs=placed,
        out_specs=(P(), P(AXES, None), P(AXES, None), P("fsdp", None), P(), P(AXES, None)),
        check_vma=False,
    )
```

```python
import functools

import jax
import jax.numpy as jnp
from jax import lax
from jax.experimental import pallas as pl
from jax.experimental.pallas import tpu as pltpu
from jax.sharding import PartitionSpec as P

EPSILON = 1e-06
MASKED_FILL = -1e30
AXES = ("dp", "fsdp")
F32 = jnp.float32
BF16 = jnp.bfloat16
VMEM = pl.BlockSpec(memory_space=pltpu.VMEM)
SMEM = pl.BlockSpec(memory_space=pltpu.SMEM)
HBM = pl.BlockSpec(memory_space=pltpu.HBM)
ANY = pl.BlockSpec(memory_space=pl.ANY)


def params(mebibytes):
    return pltpu.CompilerParams(vmem_limit_bytes=mebibytes * 1024 * 1024)


def after(value, other):
    return lax.optimization_barrier((value, other))[0]

LABELS = 128
POSITIVE = 8
OFFSETS = (0, 1, 3, 2)


def linear(x, y, z, c):
    return ((((y % 2) * 4 + z) * 2 + c) * 2 + y // 2) * 4 + x


def move(value, where):
    perm = []
    for x in range(4):
        for y in range(4):
            for z in range(4):
                for c in range(2):
                    perm.append((linear(x, y, z, c), linear(*where(x, y, z, c))))
    return lax.ppermute(value, AXES, perm)


def swap_core(value):
    return move(value, lambda x, y, z, c: (x, y, z, 1 - c))


def swap_x(value, bits):
    return move(value, lambda x, y, z, c: (x ^ bits, y, z, c))


def swap_y(value, bits):
    return move(value, lambda x, y, z, c: (x, y ^ bits, z, c))


def swap_z(value, bits):
    return move(value, lambda x, y, z, c: (x, y, z ^ bits, c))


def four(value, swap):
    return [value] + [swap(value, bits) for bits in OFFSETS[1:]]


def doubled(value, swap, bits):
    return lax.optimization_barrier(jnp.concatenate([value, swap(value, bits)], axis=0))


def dot(left, right):
    return jnp.dot(left, right, preferred_element_type=F32)


def contract_rows(left, right):
    return lax.dot_general(left, right, (((0,), (0,)), ((), ())), preferred_element_type=F32)


def contract_last(left, right):
    return lax.dot_general(left, right, (((1,), (1,)), ((), ())), preferred_element_type=F32)


def column_offsets(core, width):
    half, part = width // 2, width // 4
    mine = pl.multiple_of(core * half, half)
    other = pl.multiple_of((1 - core) * half, half)
    return (
        (mine, pl.multiple_of(mine + part, part)),
        (other, pl.multiple_of(other + part, part)),
    )


def block_home(x, y_hi, q, ry):
    return (y_hi ^ ry) * 4 + (x ^ OFFSETS[q])


def blocks_of(ref, where, pairs, block):
    picked = []
    for q, ry in pairs:
        home = block_home(where[0], where[1] // 2, q, ry)
        picked.append(ref[:, pl.ds(pl.multiple_of(home * block, block), block)])
    return jnp.concatenate(picked, axis=1)


def weight_rows(ref, block):
    rows = ref.shape[0] // 4
    return jnp.concatenate([ref[q * rows : q * rows + block, :] for q in range(4)], axis=0)


def pack_kernel(weight, users, first, second):
    rows, width = weight.shape
    part = width // 4
    first_at, second_at = column_offsets(lax.axis_index("dp") % 2, width)[0]
    first[:rows, :] = weight[:, pl.ds(first_at, part)]
    second[...] = weight[:, pl.ds(second_at, part)]
    wide = users[...].astype(F32)
    riding = jnp.concatenate([wide[:, j * part : (j + 1) * part] for j in range(4)], axis=0)
    first[rows:, :] = riding.astype(BF16)


def forward_kernel(where, lengths, ids, counts, positive, context, residual, gain, *refs):
    firsts, seconds = (refs[0:2], refs[6:8]), (refs[2:6], refs[8:12])
    stream, inverse, pooled, embedding, added_rows, sem = refs[12:]
    tokens, width = residual.shape
    part = width // 4
    block = context.shape[1] // 8
    items = lengths.shape[0]
    length = tokens // items
    copy = pltpu.make_async_copy(residual, added_rows, sem)
    copy.start()
    by_ry = [blocks_of(context, where, [(q, ry) for q in range(4)], block) for ry in range(2)]
    by_q = [blocks_of(context, where, [(q, 0), (q, 1)], block) for q in range(4)]
    for side, (first_at, second_at) in enumerate(column_offsets(where[3], width)):
        stream[:, pl.ds(first_at, part)] = sum(
            dot(by_ry[ry], weight_rows(firsts[side][ry], block)) for ry in range(2)
        )
        stream[:, pl.ds(second_at, part)] = sum(
            dot(by_q[q], seconds[side][q][...]) for q in range(4)
        )
    copy.wait()
    for i in range(items):
        span = slice(i * length, (i + 1) * length)
        rows = stream[span, :] + added_rows[span, :].astype(F32)
        stream[span, :] = rows
        inv = lax.rsqrt(jnp.mean(rows * rows, axis=-1, keepdims=True) + EPSILON)
        inverse[i * length : (i + 1) * length, :] = inv
        position = lax.broadcasted_iota(jnp.int32, (length, 1), 0)
        kept = jnp.where(position < lengths[i], inv, 0.0)
        total = jnp.sum(rows * kept, axis=0, keepdims=True)
        pooled[i : i + 1, :] = total * gain[...] / lengths[i].astype(F32)
    pool = pooled[...]
    scale = lax.rsqrt(jnp.mean(pool * pool, axis=-1, keepdims=True) + EPSILON)
    embedding[:, :width] = (pool * scale).astype(BF16)
    row = lax.broadcasted_iota(jnp.int32, (items, LABELS), 0)
    lane = lax.broadcasted_iota(jnp.int32, (items, LABELS), 1)
    labels = jnp.zeros((items, LABELS), jnp.int32)
    for i in range(items):
        for at, value in enumerate((ids[i], counts[i] // 128, counts[i] % 128)):
            labels = jnp.where((row == i) & (lane == at), value, labels)
    for u in range(positive.shape[0]):
        labels = jnp.where((row == 0) & (lane == POSITIVE + u), positive[u], labels)
    embedding[:, width:] = labels.astype(F32).astype(BF16)


def bit(value, k):
    return (value >> k) & 1


def one_hot_turn(rows, home):
    to = lax.broadcasted_iota(jnp.int32, (rows, rows), 0)
    of = lax.broadcasted_iota(jnp.int32, (rows, rows), 1)
    return jnp.where(to == home(of), 1.0, 0.0).astype(BF16)


def loss_kernel(users_here, items_here, block, where, gain, *refs):
    piece_refs, emb_refs = refs[:4], refs[4:12]
    sums, user_grad, grads, emb_grads, riders, sems = refs[12:16], *refs[16:]
    x, y, z, core = where[0], where[1], where[2], where[3]
    group, full = emb_refs[0].shape
    width = full - LABELS
    items = 8 * group
    people = 16 * users_here
    stride, part = piece_refs[0].shape[0] // 4, piece_refs[0].shape[1]
    parts = width // part
    rode = parts * users_here
    copies = []
    for n in range(4):
        for q in range(4):
            copies.append(
                pltpu.make_async_copy(
                    piece_refs[n].at[pl.ds(q * stride + block, rode)],
                    riders.at[pl.ds((n * 4 + q) * rode, rode)],
                    sems.at[n * 4 + q],
                )
            )
    for copy in copies:
        copy.start()

    def item_home(s):
        one = s // items_here
        ax = x ^ bit(one, 0) ^ (3 * bit(one, 1))
        ay = y ^ bit(one, 2) ^ (3 * bit(one, 3))
        az = z ^ bit(one, 4) ^ (3 * bit(one, 5))
        ac = core ^ bit(one, 6)
        return (((ac * 4 + az) * 4 + ay) * 4 + ax) * items_here + s % items_here

    placed = jnp.concatenate([ref[...] for ref in emb_refs], axis=0)
    turned = dot(one_hot_turn(items, item_home), placed).astype(BF16)
    emb, labels = turned[:, :width], turned[:, width:]
    for copy in copies:
        copy.wait()
    to = lax.broadcasted_iota(jnp.int32, (people, 16 * rode), 0)
    of = lax.broadcasted_iota(jnp.int32, (people, 16 * rode), 1)
    one = of // rode
    holder = ((core ^ bit(one, 3)) * 2 + ((y // 2) ^ bit(one, 2))) * 4 + (
        x ^ bit(one, 0) ^ (3 * bit(one, 1))
    )
    home = holder * users_here + of % users_here
    column = (of % rode) // users_here
    users = jnp.concatenate(
        [
            dot(
                jnp.where((to == home) & (column == j), 1.0, 0.0).astype(BF16), riders[...]
            ).astype(BF16)
            for j in range(parts)
        ],
        axis=1,
    )
    person = lax.broadcasted_iota(jnp.int32, (people, items), 0)
    at = lax.broadcasted_iota(jnp.int32, (people, items), 1)
    g = person // users_here
    g_y = jnp.where((g // 4) % 2 == y // 2, y, 3 - y)
    g_row = (((g // 8 * 4 + z) * 4 + g_y) * 4 + g % 4) * items_here
    positives = dot(jnp.where(at == g_row, 1.0, 0.0).astype(BF16), labels)
    lane = lax.broadcasted_iota(jnp.int32, (people, LABELS), 1)
    slot = lax.broadcasted_iota(jnp.int32, (people, LABELS), 0) % users_here
    positive = jnp.sum(jnp.where(lane == POSITIVE + slot, positives, 0.0), axis=1, keepdims=True)
    item_labels = contract_rows(labels, one_hot_turn(items, lambda s: s))
    ids = item_labels[0:1, :]
    log_counts = jnp.log(item_labels[1:2, :] * 128.0 + item_labels[2:3, :])
    item = lax.broadcasted_iota(jnp.int32, (1, items), 1)
    chip = item // items_here
    index = linear(chip % 4, (chip // 4) % 4, (chip // 16) % 4, chip // 64) * items_here
    index = (index + item % items_here).astype(F32)
    onehot = index == positive
    positive_id = jnp.sum(jnp.where(onehot, ids, 0.0), axis=1, keepdims=True)
    excluded = (ids == positive_id) & jnp.logical_not(onehot)
    scores = contract_last(users, emb)
    logits = jnp.where(excluded, MASKED_FILL, scores - log_counts)
    row_max = jnp.max(logits, axis=1, keepdims=True)
    weights = jnp.where(excluded, 0.0, jnp.exp(logits - row_max))
    row_total = jnp.sum(weights, axis=1, keepdims=True)
    picked = jnp.sum(jnp.where(onehot, logits, 0.0), axis=1, keepdims=True)
    losses = row_max + jnp.log(row_total) - picked
    grad = (weights / row_total - jnp.where(onehot, 1.0, 0.0)).astype(BF16)
    grads[...] = grad.astype(F32)
    all_grads = contract_rows(grad, users)
    emb_grads[...] = all_grads
    emb_float = emb.astype(F32)
    product = emb_float * all_grads
    mean = jnp.mean(product, axis=-1, keepdims=True)
    gain_sum = jnp.sum(product - emb_float * emb_float * mean, axis=0, keepdims=True)
    line = lax.broadcasted_iota(jnp.int32, (8 * items_here, 1), 0)
    loss = jnp.broadcast_to(jnp.sum(losses, axis=0, keepdims=True), (1, width))
    for q in range(4):
        az = z ^ OFFSETS[q]
        start = ((core * 4 + az) * 4 + (y // 2) * 2) * 4 * items_here
        rows = emb_grads[pl.ds(pl.multiple_of(start, 8 * items_here), 8 * items_here), :]
        for other in range(2):
            for i in range(items_here):
                chosen = line == (((y % 2) ^ other) * 4 + x) * items_here + i
                n = other * items_here + i
                sums[q][n : n + 1, :] = jnp.sum(
                    jnp.where(chosen, rows, 0.0), axis=0, keepdims=True
                )
        sums[q][2 * items_here : 2 * items_here + 1, :] = gain_sum
        sums[q][2 * items_here + 1 :, :] = jnp.broadcast_to(loss, (6 - 2 * items_here + 1, width))
    place = ((core * 2 + y // 2) * 4 + x) * users_here
    own = grads[pl.ds(pl.multiple_of(place, users_here), users_here), :]
    user_grad[...] = dot(own.astype(BF16), emb).astype(BF16)


def residual_kernel(people, where, lengths, stream, inverse, pooled, gain, *refs):
    own_sums, other_sums, residual_grad, keep, send, gain_grad, loss = refs
    tokens, width = stream.shape
    half = width // 2
    items = lengths.shape[0]
    length = tokens // items
    for i in range(items):
        mine = own_sums[i : i + 1, :] + other_sums[items + i : items + i + 1, :]
        pool = pooled[i : i + 1, :]
        scale = lax.rsqrt(jnp.mean(pool * pool, axis=-1, keepdims=True) + EPSILON)
        pool_grad = scale * mine - pool * scale * scale * scale * jnp.mean(
            pool * mine, axis=-1, keepdims=True
        )
        row = gain[...] * pool_grad / lengths[i].astype(F32)
        span = slice(i * length, (i + 1) * length)
        rows = stream[span, :]
        inv = inverse[span, :]
        position = lax.broadcasted_iota(jnp.int32, (length, 1), 0)
        kept = jnp.where(position < lengths[i], inv, 0.0)
        mean = jnp.mean(rows * row, axis=-1, keepdims=True)
        residual_grad[span, :] = (kept * row - rows * (kept * inv * inv * mean)).astype(BF16)
    keep[...] = residual_grad[:, pl.ds(pl.multiple_of(where[3] * half, half), half)]
    send[...] = residual_grad[:, pl.ds(pl.multiple_of((1 - where[3]) * half, half), half)]
    at = 2 * items
    gain_grad[...] = (own_sums[at : at + 1, :] + other_sums[at : at + 1, :]) / gain[...]
    at = at + 1
    loss[...] = (own_sums[at : at + 1, 0:1] + other_sums[at : at + 1, 0:1]) / people


def context_kernel(where, keep, send, *refs):
    firsts, seconds = (refs[0:2], refs[6:8]), (refs[2:6], refs[8:12])
    context_grad = refs[12]
    part = keep.shape[1] // 2
    block = context_grad.shape[1] // 8
    near = [ref[:, :part] for ref in (keep, send)]
    far = [ref[:, part:] for ref in (keep, send)]
    from_first = [
        sum(contract_last(near[s], weight_rows(firsts[s][ry], block)) for s in range(2))
        for ry in range(2)
    ]
    for q in range(4):
        from_second = sum(contract_last(far[s], seconds[s][q][...]) for s in range(2))
        for ry in range(2):
            value = (
                from_first[ry][:, q * block : (q + 1) * block]
                + from_second[:, ry * block : (ry + 1) * block]
            )
            home = block_home(where[0], where[1] // 2, q, ry)
            context_grad[:, pl.ds(pl.multiple_of(home * block, block), block)] = value.astype(BF16)


def blocks_kernel(kept, where, own_context, peer_context, own_grad, peer_grad, first, *seconds):
    part = own_grad.shape[1] // 2
    block = own_context.shape[1] // 8

    def product(pairs, at):
        return contract_rows(
            blocks_of(own_context, where, pairs, block), own_grad[:, at : at + part]
        ) + contract_rows(blocks_of(peer_context, where, pairs, block), peer_grad[:, at : at + part])

    ry = 0 if kept else 1
    first[...] = product([(q, ry) for q in range(4)], 0).astype(first.dtype)
    places = (0,) if kept else (1, 2, 3)
    value = product([(q, ry) for q in places for ry in range(2)], part)
    for n, second in enumerate(seconds):
        second[...] = value[n * 2 * block : (n + 1) * 2 * block].astype(second.dtype)


def shaped(shape, dtype=F32):
    return jax.ShapeDtypeStruct(shape, dtype)


def added(kept, sent, swap, bits):
    return kept + swap(sent.astype(BF16), bits).astype(F32)


def folded(value, swap, bits):
    rows = value.shape[0] // 2
    return added(value[:rows], value[rows:], swap, bits)


def all_added(value, swap, bits):
    value = lax.reduce_precision(value, 8, 7)
    return added(value, value, swap, bits)


def on_device(
    context, residual, out_weight, norm_gain, user_vectors, positive, item_ids, item_counts, lengths
):
    tokens, head = context.shape
    width = residual.shape[1]
    items_here = lengths.shape[0]
    users_here = user_vectors.shape[0]
    dp, fsdp = lax.axis_index("dp"), lax.axis_index("fsdp")
    y_lo, z, core = dp // 8, (dp // 2) % 4, dp % 2
    y_hi, x = fsdp // 4, fsdp % 4
    y = y_hi * 2 + y_lo
    where = jnp.stack([x, y, z, core]).astype(jnp.int32)
    half, part = width // 2, width // 4
    rows = out_weight.shape[0]
    gain = norm_gain[None, :]

    rode = users_here * (width // part)
    first, second = pl.pallas_call(
        pack_kernel,
        out_shape=(shaped((rows + rode, part), BF16), shaped((rows, part), BF16)),
        in_specs=[VMEM] * 2,
        out_specs=(VMEM,) * 2,
        compiler_params=params(6),
        name="pack",
    )(out_weight, user_vectors)
    second = doubled(second, swap_y, 3)
    first = jnp.concatenate(four(first, swap_x), axis=0)
    first, second = lax.optimization_barrier((first, second))
    pieces = [first, swap_y(first, 3)] + four(second, swap_x)
    pieces = pieces + [swap_core(p) for p in pieces]

    stream, inverse, pooled, emb = pl.pallas_call(
        forward_kernel,
        out_shape=(
            shaped((tokens, width)),
            shaped((tokens, 1)),
            shaped((items_here, width)),
            shaped((items_here, width + LABELS), BF16),
        ),
        in_specs=[SMEM] * 5 + [VMEM, HBM] + [VMEM] * 13,
        out_specs=(VMEM,) * 4,
        scratch_shapes=[pltpu.VMEM((tokens, width), BF16), pltpu.SemaphoreType.DMA],
        compiler_params=params(20),
        name="forward",
    )(where, lengths, item_ids, item_counts, positive, context, residual, gain, *pieces)

    emb = lax.optimization_barrier(jnp.concatenate(four(emb, swap_x), axis=0))
    peer_context = swap_core(after(context, emb))
    emb = lax.optimization_barrier(jnp.concatenate(four(emb, swap_y), axis=0))
    emb_pieces = four(emb, swap_z)
    emb_pieces = emb_pieces + [swap_core(p) for p in emb_pieces]

    items, people = 128 * items_here, 16 * users_here
    riding = pieces[0:2] + pieces[6:8]
    *sums, user_grad = pl.pallas_call(
        functools.partial(loss_kernel, users_here, items_here, rows),
        out_shape=(shaped((8, width)),) * 4 + (shaped((users_here, width), BF16),),
        in_specs=[SMEM, VMEM] + [ANY] * 4 + [VMEM] * 8,
        out_specs=(VMEM,) * 5,
        scratch_shapes=[
            pltpu.VMEM((people, items), F32),
            pltpu.VMEM((items, width), F32),
            pltpu.VMEM((people * (width // part), part), BF16),
            pltpu.SemaphoreType.DMA((16,)),
        ],
        compiler_params=params(24),
        name="loss",
    )(where, gain, *riding, *emb_pieces)
    sums = [sums[0]] + [swap_z(sums[q], OFFSETS[q]) for q in (1, 2, 3)]
    sums = (sums[0] + sums[1]) + (sums[2] + sums[3])

    residual_grad, keep, send, gain_grad, loss = pl.pallas_call(
        functools.partial(residual_kernel, 8 * people),
        out_shape=(
            shaped((tokens, width), BF16),
            shaped((tokens, half), BF16),
            shaped((tokens, half), BF16),
            shaped((1, width)),
            shaped((1, 1)),
        ),
        in_specs=[SMEM, SMEM] + [VMEM] * 6,
        out_specs=(VMEM,) * 5,
        compiler_params=params(16),
        name="residual",
    )(where, lengths, stream, inverse, pooled, gain, sums, swap_y(sums, 1))
    peer_grad = swap_core(send)
    context_grad = pl.pallas_call(
        context_kernel,
        out_shape=shaped((tokens, head), BF16),
        in_specs=[SMEM] + [VMEM] * 14,
        out_specs=VMEM,
        compiler_params=params(14),
        name="context",
    )(where, keep, send, *pieces)

    operands = (where, context, peer_context, keep, peer_grad)

    def blocks(kept, dtype, name):
        counts = 1 if kept else 3
        return pl.pallas_call(
            functools.partial(blocks_kernel, kept),
            out_shape=(shaped((4 * rows, part), dtype),) + (shaped((2 * rows, part), dtype),) * counts,
            in_specs=[SMEM] + [VMEM] * 4,
            out_specs=(VMEM,) * (1 + counts),
            compiler_params=params(16),
            name=name,
        )(*operands)

    first_sent, *second_sent = blocks(False, BF16, "blocks_sent")
    first, second = blocks(True, F32, "blocks_kept")
    first, second, context_grad = lax.optimization_barrier((first, second, context_grad))
    first = added(first, first_sent, swap_y, 3)
    arrived = [swap_x(first[q * rows : (q + 1) * rows].astype(BF16), OFFSETS[q]) for q in (1, 2, 3)]
    for q in (1, 2, 3):
        second = second + swap_x(second_sent[q - 1], OFFSETS[q]).astype(F32)
    second = folded(second, swap_y, 3)
    first = first[:rows]
    for piece in arrived:
        first = first + piece.astype(F32)
    first = all_added(first, swap_y, 1)
    second = all_added(second, swap_z, 1)
    first = all_added(first, swap_z, 1)
    second = all_added(second, swap_z, 3)
    first = all_added(first, swap_z, 3)
    second = all_added(second, swap_y, 1)
    own = jnp.concatenate([first, second], axis=1).astype(BF16)
    other = swap_core(own)
    weight_grad = jnp.where(
        core == 0, jnp.concatenate([own, other], axis=1), jnp.concatenate([other, own], axis=1)
    )
    return (loss[0, 0], residual_grad, context_grad, weight_grad, gain_grad[0], user_grad)


def solution(mesh):
    placed = (
        P(AXES, None),
        P(AXES, None),
        P("fsdp", None),
        P(),
        P(AXES, None),
        P(AXES),
        P(AXES),
        P(AXES),
        P(AXES),
    )
    return jax.shard_map(
        on_device,
        mesh=mesh,
        in_specs=placed,
        out_specs=(P(), P(AXES, None), P(AXES, None), P("fsdp", None), P(), P(AXES, None)),
        check_vma=False,
    )
```

```python
import functools

import jax
import jax.numpy as jnp
from jax import lax
from jax.experimental import pallas as pl
from jax.experimental.pallas import tpu as pltpu
from jax.sharding import PartitionSpec as P

EPSILON = 1e-06
MASKED_FILL = -1e30
AXES = ("dp", "fsdp")
F32 = jnp.float32
BF16 = jnp.bfloat16
VMEM = pl.BlockSpec(memory_space=pltpu.VMEM)
SMEM = pl.BlockSpec(memory_space=pltpu.SMEM)
HBM = pl.BlockSpec(memory_space=pltpu.HBM)
ANY = pl.BlockSpec(memory_space=pl.ANY)


def params(mebibytes):
    return pltpu.CompilerParams(vmem_limit_bytes=mebibytes * 1024 * 1024)


def after(value, other):
    return lax.optimization_barrier((value, other))[0]

LABELS = 128
POSITIVE = 8
OFFSETS = (0, 1, 3, 2)


def linear(x, y, z, c):
    return ((((y % 2) * 4 + z) * 2 + c) * 2 + y // 2) * 4 + x


def move(value, where):
    perm = []
    for x in range(4):
        for y in range(4):
            for z in range(4):
                for c in range(2):
                    perm.append((linear(x, y, z, c), linear(*where(x, y, z, c))))
    return lax.ppermute(value, AXES, perm)


def swap_core(value):
    return move(value, lambda x, y, z, c: (x, y, z, 1 - c))


def swap_x(value, bits):
    return move(value, lambda x, y, z, c: (x ^ bits, y, z, c))


def swap_y(value, bits):
    return move(value, lambda x, y, z, c: (x, y ^ bits, z, c))


def swap_z(value, bits):
    return move(value, lambda x, y, z, c: (x, y, z ^ bits, c))


def four(value, swap):
    return [value] + [swap(value, bits) for bits in OFFSETS[1:]]


def doubled(value, swap, bits):
    return lax.optimization_barrier(jnp.concatenate([value, swap(value, bits)], axis=0))


def dot(left, right):
    return jnp.dot(left, right, preferred_element_type=F32)


def contract_rows(left, right):
    return lax.dot_general(left, right, (((0,), (0,)), ((), ())), preferred_element_type=F32)


def contract_last(left, right):
    return lax.dot_general(left, right, (((1,), (1,)), ((), ())), preferred_element_type=F32)


def column_offsets(core, width):
    half, part = width // 2, width // 4
    mine = pl.multiple_of(core * half, half)
    other = pl.multiple_of((1 - core) * half, half)
    return (
        (mine, pl.multiple_of(mine + part, part)),
        (other, pl.multiple_of(other + part, part)),
    )


def with_r3(r3):
    return [(q, ry) for q in (2 * r3, 2 * r3 + 1) for ry in range(2)]


def with_ry(ry):
    return [(q, ry) for q in range(4)]


def block_home(x, y_hi, q, ry):
    return (y_hi ^ ry) * 4 + (x ^ OFFSETS[q])


def blocks_of(ref, where, pairs, block):
    picked = []
    for q, ry in pairs:
        home = block_home(where[0], where[1] // 2, q, ry)
        picked.append(ref[:, pl.ds(pl.multiple_of(home * block, block), block)])
    return jnp.concatenate(picked, axis=1)


def weight_rows(ref, block):
    rows = ref.shape[0] // 4
    return jnp.concatenate([ref[q * rows : q * rows + block, :] for q in range(4)], axis=0)


def pack_kernel(weight, users, first, second):
    rows, width = weight.shape
    part = width // 4
    first_at, second_at = column_offsets(lax.axis_index("dp") % 2, width)[0]
    first[:rows, :] = weight[:, pl.ds(first_at, part)]
    second[...] = weight[:, pl.ds(second_at, part)]
    wide = users[...].astype(F32)
    riding = jnp.concatenate([wide[:, j * part : (j + 1) * part] for j in range(4)], axis=0)
    first[rows:, :] = riding.astype(BF16)


def forward_kernel(items, ints, context, residual, gain, *refs):
    firsts, seconds = (refs[0:2], refs[4:6]), (refs[2:4], refs[6:8])
    stream, inverse, pooled, embedding, added_rows, sem = refs[8:]
    where = [ints[i] for i in range(4)]
    lengths, ids, counts = ([ints[4 + j * items + i] for i in range(items)] for j in range(3))
    positive = [ints[i] for i in range(4 + 3 * items, ints.shape[0])]
    tokens, width = residual.shape
    part = width // 4
    block = context.shape[1] // 8
    length = tokens // items
    copy = pltpu.make_async_copy(residual, added_rows, sem)
    copy.start()
    by_r3 = [blocks_of(context, where, with_r3(r3), block) for r3 in range(2)]
    by_ry = [blocks_of(context, where, with_ry(ry), block) for ry in range(2)]
    for side, (first_at, second_at) in enumerate(column_offsets(where[3], width)):
        stream[:, pl.ds(first_at, part)] = sum(
            dot(by_r3[r3], weight_rows(firsts[side][r3], block)) for r3 in range(2)
        )
        stream[:, pl.ds(second_at, part)] = sum(
            dot(by_ry[ry], seconds[side][ry][...]) for ry in range(2)
        )
    copy.wait()
    for i in range(items):
        span = slice(i * length, (i + 1) * length)
        rows = stream[span, :] + added_rows[span, :].astype(F32)
        stream[span, :] = rows
        inv = lax.rsqrt(jnp.mean(rows * rows, axis=-1, keepdims=True) + EPSILON)
        inverse[i * length : (i + 1) * length, :] = inv
        position = lax.broadcasted_iota(jnp.int32, (length, 1), 0)
        kept = jnp.where(position < lengths[i], inv, 0.0)
        total = jnp.sum(rows * kept, axis=0, keepdims=True)
        pooled[i : i + 1, :] = total * gain[...] / lengths[i].astype(F32)
    pool = pooled[...]
    scale = lax.rsqrt(jnp.mean(pool * pool, axis=-1, keepdims=True) + EPSILON)
    embedding[:, :width] = (pool * scale).astype(BF16)
    row = lax.broadcasted_iota(jnp.int32, (items, LABELS), 0)
    lane = lax.broadcasted_iota(jnp.int32, (items, LABELS), 1)
    labels = jnp.zeros((items, LABELS), jnp.int32)
    for i in range(items):
        for at, value in enumerate((ids[i], counts[i] // 128, counts[i] % 128)):
            labels = jnp.where((row == i) & (lane == at), value, labels)
    for u in range(len(positive)):
        labels = jnp.where((row == 0) & (lane == POSITIVE + u), positive[u], labels)
    embedding[:, width:] = labels.astype(F32).astype(BF16)


def bit(value, k):
    return (value >> k) & 1


def one_hot_turn(rows, home):
    to = lax.broadcasted_iota(jnp.int32, (rows, rows), 0)
    of = lax.broadcasted_iota(jnp.int32, (rows, rows), 1)
    return jnp.where(to == home(of), 1.0, 0.0).astype(BF16)


def loss_kernel(users_here, items_here, block, where, gain, *refs):
    piece_refs, emb_refs = refs[:4], refs[4:12]
    sums, user_grad, grads, emb_grads, riders, sems = refs[12:16], *refs[16:]
    x, y, z, core = where[0], where[1], where[2], where[3]
    group, full = emb_refs[0].shape
    width = full - LABELS
    items = 8 * group
    people = 16 * users_here
    stride, part = piece_refs[0].shape[0] // 4, piece_refs[0].shape[1]
    parts = width // part
    rode = parts * users_here
    copies = []
    for n in range(4):
        for b in range(4):
            copies.append(
                pltpu.make_async_copy(
                    piece_refs[n].at[pl.ds(b * stride + block, rode)],
                    riders.at[pl.ds((n * 4 + b) * rode, rode)],
                    sems.at[n * 4 + b],
                )
            )
    for copy in copies:
        copy.start()

    def item_home(s):
        one = s // items_here
        ax = x ^ bit(one, 0) ^ (3 * bit(one, 1))
        ay = y ^ bit(one, 2) ^ (3 * bit(one, 3))
        az = z ^ bit(one, 4) ^ (3 * bit(one, 5))
        ac = core ^ bit(one, 6)
        return (((ac * 4 + az) * 4 + ay) * 4 + ax) * items_here + s % items_here

    placed = jnp.concatenate([ref[...] for ref in emb_refs], axis=0)
    turned = dot(one_hot_turn(items, item_home), placed).astype(BF16)
    emb, labels = turned[:, :width], turned[:, width:]
    for copy in copies:
        copy.wait()
    to = lax.broadcasted_iota(jnp.int32, (people, 16 * rode), 0)
    of = lax.broadcasted_iota(jnp.int32, (people, 16 * rode), 1)
    one = of // rode
    holder = ((core ^ bit(one, 3)) * 2 + ((y // 2) ^ bit(one, 0))) * 4 + (
        x ^ bit(one, 1) ^ (3 * bit(one, 2))
    )
    home = holder * users_here + of % users_here
    column = (of % rode) // users_here
    users = jnp.concatenate(
        [
            dot(
                jnp.where((to == home) & (column == j), 1.0, 0.0).astype(BF16), riders[...]
            ).astype(BF16)
            for j in range(parts)
        ],
        axis=1,
    )
    person = lax.broadcasted_iota(jnp.int32, (people, items), 0)
    at = lax.broadcasted_iota(jnp.int32, (people, items), 1)
    g = person // users_here
    g_y = jnp.where((g // 4) % 2 == y // 2, y, 3 - y)
    g_row = (((g // 8 * 4 + z) * 4 + g_y) * 4 + g % 4) * items_here
    positives = dot(jnp.where(at == g_row, 1.0, 0.0).astype(BF16), labels)
    lane = lax.broadcasted_iota(jnp.int32, (people, LABELS), 1)
    slot = lax.broadcasted_iota(jnp.int32, (people, LABELS), 0) % users_here
    positive = jnp.sum(jnp.where(lane == POSITIVE + slot, positives, 0.0), axis=1, keepdims=True)
    item_labels = contract_rows(labels, one_hot_turn(items, lambda s: s))
    ids = item_labels[0:1, :]
    log_counts = jnp.log(item_labels[1:2, :] * 128.0 + item_labels[2:3, :])
    item = lax.broadcasted_iota(jnp.int32, (1, items), 1)
    chip = item // items_here
    index = linear(chip % 4, (chip // 4) % 4, (chip // 16) % 4, chip // 64) * items_here
    index = (index + item % items_here).astype(F32)
    onehot = index == positive
    positive_id = jnp.sum(jnp.where(onehot, ids, 0.0), axis=1, keepdims=True)
    excluded = (ids == positive_id) & jnp.logical_not(onehot)
    scores = contract_last(users, emb)
    logits = jnp.where(excluded, MASKED_FILL, scores - log_counts)
    row_max = jnp.max(logits, axis=1, keepdims=True)
    weights = jnp.where(excluded, 0.0, jnp.exp(logits - row_max))
    row_total = jnp.sum(weights, axis=1, keepdims=True)
    picked = jnp.sum(jnp.where(onehot, logits, 0.0), axis=1, keepdims=True)
    losses = row_max + jnp.log(row_total) - picked
    grad = (weights / row_total - jnp.where(onehot, 1.0, 0.0)).astype(BF16)
    grads[...] = grad.astype(F32)
    all_grads = contract_rows(grad, users)
    emb_grads[...] = all_grads
    emb_float = emb.astype(F32)
    product = emb_float * all_grads
    mean = jnp.mean(product, axis=-1, keepdims=True)
    gain_sum = jnp.sum(product - emb_float * emb_float * mean, axis=0, keepdims=True)
    line = lax.broadcasted_iota(jnp.int32, (8 * items_here, 1), 0)
    loss = jnp.broadcast_to(jnp.sum(losses, axis=0, keepdims=True), (1, width))
    for q in range(4):
        az = z ^ OFFSETS[q]
        start = ((core * 4 + az) * 4 + (y // 2) * 2) * 4 * items_here
        rows = emb_grads[pl.ds(pl.multiple_of(start, 8 * items_here), 8 * items_here), :]
        for other in range(2):
            for i in range(items_here):
                chosen = line == (((y % 2) ^ other) * 4 + x) * items_here + i
                n = other * items_here + i
                sums[q][n : n + 1, :] = jnp.sum(
                    jnp.where(chosen, rows, 0.0), axis=0, keepdims=True
                )
        sums[q][2 * items_here : 2 * items_here + 1, :] = gain_sum
        sums[q][2 * items_here + 1 :, :] = jnp.broadcast_to(loss, (6 - 2 * items_here + 1, width))
    place = ((core * 2 + y // 2) * 4 + x) * users_here
    own = grads[pl.ds(pl.multiple_of(place, users_here), users_here), :]
    user_grad[...] = dot(own.astype(BF16), emb).astype(BF16)


def residual_kernel(people, where, lengths, stream, inverse, pooled, gain, *refs):
    own_sums, other_sums, residual_grad, keep, send, gain_grad, loss = refs
    tokens, width = stream.shape
    half = width // 2
    items = lengths.shape[0]
    length = tokens // items
    for i in range(items):
        mine = own_sums[i : i + 1, :] + other_sums[items + i : items + i + 1, :]
        pool = pooled[i : i + 1, :]
        scale = lax.rsqrt(jnp.mean(pool * pool, axis=-1, keepdims=True) + EPSILON)
        pool_grad = scale * mine - pool * scale * scale * scale * jnp.mean(
            pool * mine, axis=-1, keepdims=True
        )
        row = gain[...] * pool_grad / lengths[i].astype(F32)
        span = slice(i * length, (i + 1) * length)
        rows = stream[span, :]
        inv = inverse[span, :]
        position = lax.broadcasted_iota(jnp.int32, (length, 1), 0)
        kept = jnp.where(position < lengths[i], inv, 0.0)
        mean = jnp.mean(rows * row, axis=-1, keepdims=True)
        residual_grad[span, :] = (kept * row - rows * (kept * inv * inv * mean)).astype(BF16)
    keep[...] = residual_grad[:, pl.ds(pl.multiple_of(where[3] * half, half), half)]
    send[...] = residual_grad[:, pl.ds(pl.multiple_of((1 - where[3]) * half, half), half)]
    at = 2 * items
    gain_grad[...] = (own_sums[at : at + 1, :] + other_sums[at : at + 1, :]) / gain[...]
    at = at + 1
    loss[...] = (own_sums[at : at + 1, 0:1] + other_sums[at : at + 1, 0:1]) / people


def context_kernel(where, keep, send, *refs):
    firsts, seconds = (refs[0:2], refs[4:6]), (refs[2:4], refs[6:8])
    context_grad = refs[8]
    part = keep.shape[1] // 2
    block = context_grad.shape[1] // 8
    near = [ref[:, :part] for ref in (keep, send)]
    far = [ref[:, part:] for ref in (keep, send)]
    from_first = [
        sum(contract_last(near[s], weight_rows(firsts[s][r3], block)) for s in range(2))
        for r3 in range(2)
    ]
    for ry in range(2):
        from_second = sum(contract_last(far[s], seconds[s][ry][...]) for s in range(2))
        for q in range(4):
            b = ((q % 2) * 2 + ry) * block
            value = from_first[q // 2][:, b : b + block] + from_second[:, q * block : (q + 1) * block]
            home = block_home(where[0], where[1] // 2, q, ry)
            context_grad[:, pl.ds(pl.multiple_of(home * block, block), block)] = value.astype(BF16)


def blocks_kernel(kept, where, own_context, peer_context, own_grad, peer_grad, first, *seconds):
    part = own_grad.shape[1] // 2
    block = own_context.shape[1] // 8

    def product(pairs, at):
        return contract_rows(
            blocks_of(own_context, where, pairs, block), own_grad[:, at : at + part]
        ) + contract_rows(blocks_of(peer_context, where, pairs, block), peer_grad[:, at : at + part])

    ry = 0 if kept else 1
    first[...] = product([(q, ry) for q in range(4)], 0).astype(first.dtype)
    places = (0,) if kept else (1, 2, 3)
    value = product([(q, ry) for q in places for ry in range(2)], part)
    for n, second in enumerate(seconds):
        second[...] = value[n * 2 * block : (n + 1) * 2 * block].astype(second.dtype)


def shaped(shape, dtype=F32):
    return jax.ShapeDtypeStruct(shape, dtype)


def added(kept, sent, swap, bits):
    return kept + swap(sent.astype(BF16), bits).astype(F32)


def folded(value, swap, bits):
    rows = value.shape[0] // 2
    return added(value[:rows], value[rows:], swap, bits)


def all_added(value, swap, bits):
    value = lax.reduce_precision(value, 8, 7)
    return added(value, value, swap, bits)


def on_device(
    context, residual, out_weight, norm_gain, user_vectors, positive, item_ids, item_counts, lengths
):
    tokens, head = context.shape
    width = residual.shape[1]
    items_here = lengths.shape[0]
    users_here = user_vectors.shape[0]
    dp, fsdp = lax.axis_index("dp"), lax.axis_index("fsdp")
    y_lo, z, core = dp // 8, (dp // 2) % 4, dp % 2
    y_hi, x = fsdp // 4, fsdp % 4
    y = y_hi * 2 + y_lo
    where = jnp.stack([x, y, z, core]).astype(jnp.int32)
    half, part = width // 2, width // 4
    rows = out_weight.shape[0]
    gain = norm_gain[None, :]

    rode = users_here * (width // part)
    first, second = pl.pallas_call(
        pack_kernel,
        out_shape=(shaped((rows + rode, part), BF16), shaped((rows, part), BF16)),
        in_specs=[VMEM] * 2,
        out_specs=(VMEM,) * 2,
        compiler_params=params(6),
        name="pack",
    )(out_weight, user_vectors)
    for (first_swap, n), (second_swap, m) in (
        ((swap_y, 3), (swap_x, 1)),
        ((swap_x, 1), (swap_x, 3)),
    ):
        first = jnp.concatenate([first, first_swap(first, n)], axis=0)
        second = jnp.concatenate([second, second_swap(second, m)], axis=0)
        first, second = lax.optimization_barrier((first, second))
    first_far, second_far = lax.optimization_barrier((swap_x(first, 3), swap_y(second, 3)))
    pieces = [first, first_far, second, second_far]
    pieces = pieces + [swap_core(p) for p in pieces]
    ints = jnp.concatenate([where, lengths, item_ids, item_counts, positive])

    stream, inverse, pooled, emb = pl.pallas_call(
        functools.partial(forward_kernel, items_here),
        out_shape=(
            shaped((tokens, width)),
            shaped((tokens, 1)),
            shaped((items_here, width)),
            shaped((items_here, width + LABELS), BF16),
        ),
        in_specs=[SMEM, VMEM, HBM] + [VMEM] * 9,
        out_specs=(VMEM,) * 4,
        scratch_shapes=[pltpu.VMEM((tokens, width), BF16), pltpu.SemaphoreType.DMA],
        compiler_params=params(20),
        name="forward",
    )(ints, context, residual, gain, *pieces)

    emb = lax.optimization_barrier(jnp.concatenate(four(emb, swap_x), axis=0))
    peer_context = swap_core(after(context, emb))
    emb = lax.optimization_barrier(jnp.concatenate(four(emb, swap_y), axis=0))
    emb_pieces = four(emb, swap_z)
    emb_pieces = emb_pieces + [swap_core(p) for p in emb_pieces]

    items, people = 128 * items_here, 16 * users_here
    riding = pieces[0:2] + pieces[4:6]
    *sums, user_grad = pl.pallas_call(
        functools.partial(loss_kernel, users_here, items_here, rows),
        out_shape=(shaped((8, width)),) * 4 + (shaped((users_here, width), BF16),),
        in_specs=[SMEM, VMEM] + [ANY] * 4 + [VMEM] * 8,
        out_specs=(VMEM,) * 5,
        scratch_shapes=[
            pltpu.VMEM((people, items), F32),
            pltpu.VMEM((items, width), F32),
            pltpu.VMEM((people * (width // part), part), BF16),
            pltpu.SemaphoreType.DMA((16,)),
        ],
        compiler_params=params(24),
        name="loss",
    )(where, gain, *riding, *emb_pieces)
    sums = [sums[0]] + [swap_z(sums[q], OFFSETS[q]) for q in (1, 2, 3)]
    sums = (sums[0] + sums[1]) + (sums[2] + sums[3])

    residual_grad, keep, send, gain_grad, loss = pl.pallas_call(
        functools.partial(residual_kernel, 8 * people),
        out_shape=(
            shaped((tokens, width), BF16),
            shaped((tokens, half), BF16),
            shaped((tokens, half), BF16),
            shaped((1, width)),
            shaped((1, 1)),
        ),
        in_specs=[SMEM, SMEM] + [VMEM] * 6,
        out_specs=(VMEM,) * 5,
        compiler_params=params(16),
        name="residual",
    )(where, lengths, stream, inverse, pooled, gain, sums, swap_y(sums, 1))
    peer_grad = swap_core(send)
    context_grad = pl.pallas_call(
        context_kernel,
        out_shape=shaped((tokens, head), BF16),
        in_specs=[SMEM] + [VMEM] * 10,
        out_specs=VMEM,
        compiler_params=params(14),
        name="context",
    )(where, keep, send, *pieces)

    operands = (where, context, peer_context, keep, peer_grad)

    def blocks(kept, dtype, name):
        counts = 1 if kept else 3
        return pl.pallas_call(
            functools.partial(blocks_kernel, kept),
            out_shape=(shaped((4 * rows, part), dtype),) + (shaped((2 * rows, part), dtype),) * counts,
            in_specs=[SMEM] + [VMEM] * 4,
            out_specs=(VMEM,) * (1 + counts),
            compiler_params=params(16),
            name=name,
        )(*operands)

    first_sent, *second_sent = blocks(False, BF16, "blocks_sent")
    first, second = blocks(True, F32, "blocks_kept")
    first, second, context_grad = lax.optimization_barrier((first, second, context_grad))
    first = added(first, first_sent, swap_y, 3)
    arrived = [swap_x(first[q * rows : (q + 1) * rows].astype(BF16), OFFSETS[q]) for q in (1, 2, 3)]
    for q in (1, 2, 3):
        second = second + swap_x(second_sent[q - 1], OFFSETS[q]).astype(F32)
    second = folded(second, swap_y, 3)
    first = first[:rows]
    for piece in arrived:
        first = first + piece.astype(F32)
    first = all_added(first, swap_y, 1)
    second = all_added(second, swap_z, 1)
    first = all_added(first, swap_z, 1)
    second = all_added(second, swap_z, 3)
    first = all_added(first, swap_z, 3)
    second = all_added(second, swap_y, 1)
    own = jnp.concatenate([first, second], axis=1).astype(BF16)
    other = swap_core(own)
    weight_grad = jnp.where(
        core == 0, jnp.concatenate([own, other], axis=1), jnp.concatenate([other, own], axis=1)
    )
    return (loss[0, 0], residual_grad, context_grad, weight_grad, gain_grad[0], user_grad)


def solution(mesh):
    placed = (
        P(AXES, None),
        P(AXES, None),
        P("fsdp", None),
        P(),
        P(AXES, None),
        P(AXES),
        P(AXES),
        P(AXES),
        P(AXES),
    )
    return jax.shard_map(
        on_device,
        mesh=mesh,
        in_specs=placed,
        out_specs=(P(), P(AXES, None), P(AXES, None), P("fsdp", None), P(), P(AXES, None)),
        check_vma=False,
    )
```

```python
import functools

import jax
import jax.numpy as jnp
from jax import lax
from jax.experimental import pallas as pl
from jax.experimental.pallas import tpu as pltpu
from jax.sharding import PartitionSpec as P

EPSILON = 1e-06
MASKED_FILL = -1e30
AXES = ("dp", "fsdp")
F32 = jnp.float32
BF16 = jnp.bfloat16
VMEM = pl.BlockSpec(memory_space=pltpu.VMEM)
SMEM = pl.BlockSpec(memory_space=pltpu.SMEM)
HBM = pl.BlockSpec(memory_space=pltpu.HBM)
ANY = pl.BlockSpec(memory_space=pl.ANY)


def params(mebibytes):
    return pltpu.CompilerParams(vmem_limit_bytes=mebibytes * 1024 * 1024)


def after(value, other):
    return lax.optimization_barrier((value, other))[0]

LABELS = 128
POSITIVE = 8
OFFSETS = (0, 1, 3, 2)


def linear(x, y, z, c):
    return ((((y % 2) * 4 + z) * 2 + c) * 2 + y // 2) * 4 + x


def move(value, where):
    perm = []
    for x in range(4):
        for y in range(4):
            for z in range(4):
                for c in range(2):
                    perm.append((linear(x, y, z, c), linear(*where(x, y, z, c))))
    return lax.ppermute(value, AXES, perm)


def swap_core(value):
    return move(value, lambda x, y, z, c: (x, y, z, 1 - c))


def swap_x(value, bits):
    return move(value, lambda x, y, z, c: (x ^ bits, y, z, c))


def swap_y(value, bits):
    return move(value, lambda x, y, z, c: (x, y ^ bits, z, c))


def swap_z(value, bits):
    return move(value, lambda x, y, z, c: (x, y, z ^ bits, c))


def four(value, swap):
    return [value] + [swap(value, bits) for bits in OFFSETS[1:]]


def doubled(value, swap, bits):
    return lax.optimization_barrier(jnp.concatenate([value, swap(value, bits)], axis=0))


def dot(left, right):
    return jnp.dot(left, right, preferred_element_type=F32)


def contract_rows(left, right):
    return lax.dot_general(left, right, (((0,), (0,)), ((), ())), preferred_element_type=F32)


def contract_last(left, right):
    return lax.dot_general(left, right, (((1,), (1,)), ((), ())), preferred_element_type=F32)


def parts_of(half):
    wide = half * 3 // 8
    pair = range(2)
    return (
        (0, wide, [[(r3 * 2 + r1, ry) for r1 in pair for ry in pair] for r3 in pair]),
        (wide, wide, [[(q, ry) for q in range(4)] for ry in pair]),
        (
            2 * wide,
            half - 2 * wide,
            [[(r3 * 2 + r1, ry) for ry in pair for r3 in pair] for r1 in pair],
        ),
    )


def block_home(x, y_hi, q, ry):
    return (y_hi ^ ry) * 4 + (x ^ OFFSETS[q])


def blocks_of(ref, where, pairs, block):
    picked = []
    for q, ry in pairs:
        home = block_home(where[0], where[1] // 2, q, ry)
        picked.append(ref[:, pl.ds(pl.multiple_of(home * block, block), block)])
    return jnp.concatenate(picked, axis=1)


def weight_rows(ref, block):
    rows = ref.shape[0] // 4
    if rows == block:
        return ref[...]
    return jnp.concatenate([ref[q * rows : q * rows + block, :] for q in range(4)], axis=0)


def pack_kernel(weight, users, first, second, third, held, sems):
    rows, width = weight.shape
    half = width // 2
    mine = (lax.axis_index("dp") % 2) * half
    copies = [pltpu.make_async_copy(users, held, sems.at[3])]
    for n, ((start, columns, _), out) in enumerate(zip(parts_of(half), (first, second, third))):
        at = pl.multiple_of(mine + start, 128)
        copies.append(
            pltpu.make_async_copy(
                weight.at[:, pl.ds(at, columns)], out.at[pl.ds(0, rows)], sems.at[n]
            )
        )
    for copy in copies:
        copy.start()
    for copy in copies:
        copy.wait()
    part = third.shape[1]
    wide = held[...].astype(F32)
    riding = [wide[:, j * part : (j + 1) * part] for j in range(width // part)]
    third[rows:, :] = jnp.concatenate(riding, axis=0).astype(BF16)


def forward_kernel(items, ints, context, residual, gain, *refs):
    stream, inverse, pooled, embedding, added_rows, sem = refs[12:]
    where = [ints[i] for i in range(4)]
    lengths, ids, counts = ([ints[4 + j * items + i] for i in range(items)] for j in range(3))
    positive = [ints[i] for i in range(4 + 3 * items, ints.shape[0])]
    tokens, width = residual.shape
    half = width // 2
    block = context.shape[1] // 8
    length = tokens // items
    copy = pltpu.make_async_copy(residual, added_rows, sem)
    copy.start()
    for p, (start, columns, orders) in enumerate(parts_of(half)):
        lanes = [blocks_of(context, where, order, block) for order in orders]
        for side in range(2):
            base = where[3] * half if side == 0 else (1 - where[3]) * half
            stream[:, pl.ds(pl.multiple_of(base + start, 128), columns)] = sum(
                dot(lanes[k], weight_rows(refs[side * 6 + p * 2 + k], block)) for k in range(2)
            )
    copy.wait()
    for i in range(items):
        span = slice(i * length, (i + 1) * length)
        rows = stream[span, :] + added_rows[span, :].astype(F32)
        stream[span, :] = rows
        inv = lax.rsqrt(jnp.mean(rows * rows, axis=-1, keepdims=True) + EPSILON)
        inverse[i * length : (i + 1) * length, :] = inv
        position = lax.broadcasted_iota(jnp.int32, (length, 1), 0)
        kept = jnp.where(position < lengths[i], inv, 0.0)
        total = jnp.sum(rows * kept, axis=0, keepdims=True)
        pooled[i : i + 1, :] = total * gain[...] / lengths[i].astype(F32)
    pool = pooled[...]
    scale = lax.rsqrt(jnp.mean(pool * pool, axis=-1, keepdims=True) + EPSILON)
    embedding[:, :width] = (pool * scale).astype(BF16)
    row = lax.broadcasted_iota(jnp.int32, (items, LABELS), 0)
    lane = lax.broadcasted_iota(jnp.int32, (items, LABELS), 1)
    labels = jnp.zeros((items, LABELS), jnp.int32)
    for i in range(items):
        for at, value in enumerate((ids[i], counts[i] // 128, counts[i] % 128)):
            labels = jnp.where((row == i) & (lane == at), value, labels)
    for u in range(len(positive)):
        labels = jnp.where((row == 0) & (lane == POSITIVE + u), positive[u], labels)
    embedding[:, width:] = labels.astype(F32).astype(BF16)


def bit(value, k):
    return (value >> k) & 1


def one_hot_turn(rows, home):
    to = lax.broadcasted_iota(jnp.int32, (rows, rows), 0)
    of = lax.broadcasted_iota(jnp.int32, (rows, rows), 1)
    return jnp.where(to == home(of), 1.0, 0.0).astype(BF16)


def loss_kernel(users_here, items_here, block, where, gain, *refs):
    piece_refs, emb_refs = refs[:4], refs[4:12]
    sums, user_grad, grads, emb_grads, riders, sems = refs[12:16], *refs[16:]
    x, y, z, core = where[0], where[1], where[2], where[3]
    group, full = emb_refs[0].shape
    width = full - LABELS
    items = 8 * group
    people = 16 * users_here
    stride, part = piece_refs[0].shape[0] // 4, piece_refs[0].shape[1]
    parts = width // part
    rode = parts * users_here
    copies = []
    for n in range(4):
        for b in range(4):
            copies.append(
                pltpu.make_async_copy(
                    piece_refs[n].at[pl.ds(b * stride + block, rode)],
                    riders.at[pl.ds((n * 4 + b) * rode, rode)],
                    sems.at[n * 4 + b],
                )
            )
    for copy in copies:
        copy.start()

    def item_home(s):
        one = s // items_here
        ax = x ^ bit(one, 0) ^ (3 * bit(one, 1))
        ay = y ^ bit(one, 2) ^ (3 * bit(one, 3))
        az = z ^ bit(one, 4) ^ (3 * bit(one, 5))
        ac = core ^ bit(one, 6)
        return (((ac * 4 + az) * 4 + ay) * 4 + ax) * items_here + s % items_here

    placed = jnp.concatenate([ref[...] for ref in emb_refs], axis=0)
    turned = dot(one_hot_turn(items, item_home), placed).astype(BF16)
    emb, labels = turned[:, :width], turned[:, width:]
    for copy in copies:
        copy.wait()
    def user_home(s):
        one = s // users_here
        ac, ay = core ^ bit(one, 3), (y // 2) ^ bit(one, 1)
        ax = x ^ bit(one, 2) ^ (3 * bit(one, 0))
        return ((ac * 2 + ay) * 4 + ax) * users_here + s % users_here

    wide = riders[...].astype(F32)
    placed = jnp.concatenate(
        [
            jnp.concatenate(
                [
                    wide[n * rode + j * users_here : n * rode + (j + 1) * users_here, :]
                    for n in range(16)
                ],
                axis=0,
            )
            for j in range(parts)
        ],
        axis=1,
    ).astype(BF16)
    users = dot(one_hot_turn(people, user_home), placed).astype(BF16)
    person = lax.broadcasted_iota(jnp.int32, (people, items), 0)
    at = lax.broadcasted_iota(jnp.int32, (people, items), 1)
    g = person // users_here
    g_y = jnp.where((g // 4) % 2 == y // 2, y, 3 - y)
    g_row = (((g // 8 * 4 + z) * 4 + g_y) * 4 + g % 4) * items_here
    positives = dot(jnp.where(at == g_row, 1.0, 0.0).astype(BF16), labels)
    lane = lax.broadcasted_iota(jnp.int32, (people, LABELS), 1)
    slot = lax.broadcasted_iota(jnp.int32, (people, LABELS), 0) % users_here
    positive = jnp.sum(jnp.where(lane == POSITIVE + slot, positives, 0.0), axis=1, keepdims=True)
    item_labels = contract_rows(labels, one_hot_turn(items, lambda s: s))
    ids = item_labels[0:1, :]
    log_counts = jnp.log(item_labels[1:2, :] * 128.0 + item_labels[2:3, :])
    item = lax.broadcasted_iota(jnp.int32, (1, items), 1)
    chip = item // items_here
    index = linear(chip % 4, (chip // 4) % 4, (chip // 16) % 4, chip // 64) * items_here
    index = (index + item % items_here).astype(F32)
    onehot = index == positive
    positive_id = jnp.sum(jnp.where(onehot, ids, 0.0), axis=1, keepdims=True)
    excluded = (ids == positive_id) & jnp.logical_not(onehot)
    scores = contract_last(users, emb)
    logits = jnp.where(excluded, MASKED_FILL, scores - log_counts)
    row_max = jnp.max(logits, axis=1, keepdims=True)
    weights = jnp.where(excluded, 0.0, jnp.exp(logits - row_max))
    row_total = jnp.sum(weights, axis=1, keepdims=True)
    picked = jnp.sum(jnp.where(onehot, logits, 0.0), axis=1, keepdims=True)
    losses = row_max + jnp.log(row_total) - picked
    grad = (weights / row_total - jnp.where(onehot, 1.0, 0.0)).astype(BF16)
    grads[...] = grad.astype(F32)
    all_grads = contract_rows(grad, users)
    emb_grads[...] = all_grads
    emb_float = emb.astype(F32)
    product = emb_float * all_grads
    mean = jnp.mean(product, axis=-1, keepdims=True)
    gain_sum = jnp.sum(product - emb_float * emb_float * mean, axis=0, keepdims=True)
    line = lax.broadcasted_iota(jnp.int32, (8 * items_here, 1), 0)
    loss = jnp.broadcast_to(jnp.sum(losses, axis=0, keepdims=True), (1, width))
    for q in range(4):
        az = z ^ OFFSETS[q]
        start = ((core * 4 + az) * 4 + (y // 2) * 2) * 4 * items_here
        rows = emb_grads[pl.ds(pl.multiple_of(start, 8 * items_here), 8 * items_here), :]
        for other in range(2):
            for i in range(items_here):
                chosen = line == (((y % 2) ^ other) * 4 + x) * items_here + i
                n = other * items_here + i
                sums[q][n : n + 1, :] = jnp.sum(
                    jnp.where(chosen, rows, 0.0), axis=0, keepdims=True
                )
        sums[q][2 * items_here : 2 * items_here + 1, :] = gain_sum
        sums[q][2 * items_here + 1 :, :] = jnp.broadcast_to(loss, (6 - 2 * items_here + 1, width))
    place = ((core * 2 + y // 2) * 4 + x) * users_here
    own = grads[pl.ds(pl.multiple_of(place, users_here), users_here), :]
    user_grad[...] = dot(own.astype(BF16), emb).astype(BF16)


def residual_kernel(people, where, lengths, stream, inverse, pooled, gain, *refs):
    own_sums, other_sums, residual_grad, keep, send, gain_grad, loss = refs
    tokens, width = stream.shape
    half = width // 2
    items = lengths.shape[0]
    length = tokens // items
    for i in range(items):
        mine = own_sums[i : i + 1, :] + other_sums[items + i : items + i + 1, :]
        pool = pooled[i : i + 1, :]
        scale = lax.rsqrt(jnp.mean(pool * pool, axis=-1, keepdims=True) + EPSILON)
        pool_grad = scale * mine - pool * scale * scale * scale * jnp.mean(
            pool * mine, axis=-1, keepdims=True
        )
        row = gain[...] * pool_grad / lengths[i].astype(F32)
        span = slice(i * length, (i + 1) * length)
        rows = stream[span, :]
        inv = inverse[span, :]
        position = lax.broadcasted_iota(jnp.int32, (length, 1), 0)
        kept = jnp.where(position < lengths[i], inv, 0.0)
        mean = jnp.mean(rows * row, axis=-1, keepdims=True)
        residual_grad[span, :] = (kept * row - rows * (kept * inv * inv * mean)).astype(BF16)
    keep[...] = residual_grad[:, pl.ds(pl.multiple_of(where[3] * half, half), half)]
    send[...] = residual_grad[:, pl.ds(pl.multiple_of((1 - where[3]) * half, half), half)]
    at = 2 * items
    gain_grad[...] = (own_sums[at : at + 1, :] + other_sums[at : at + 1, :]) / gain[...]
    at = at + 1
    loss[...] = (own_sums[at : at + 1, 0:1] + other_sums[at : at + 1, 0:1]) / people


def context_kernel(where, keep, send, *refs):
    context_grad = refs[12]
    half = keep.shape[1]
    block = context_grad.shape[1] // 8
    values = {}
    for p, (start, columns, orders) in enumerate(parts_of(half)):
        for k, order in enumerate(orders):
            product = sum(
                contract_last(
                    grad[:, start : start + columns], weight_rows(refs[side * 6 + p * 2 + k], block)
                )
                for side, grad in enumerate((keep, send))
            )
            for b, place in enumerate(order):
                piece = product[:, b * block : (b + 1) * block]
                values[place] = values[place] + piece if place in values else piece
    for (q, ry), value in values.items():
        home = block_home(where[0], where[1] // 2, q, ry)
        context_grad[:, pl.ds(pl.multiple_of(home * block, block), block)] = value.astype(BF16)


def blocks_kernel(kept, where, own_context, peer_context, own_grad, peer_grad, first, *seconds):
    part = own_grad.shape[1] // 2
    block = own_context.shape[1] // 8

    def product(pairs, at):
        return contract_rows(
            blocks_of(own_context, where, pairs, block), own_grad[:, at : at + part]
        ) + contract_rows(blocks_of(peer_context, where, pairs, block), peer_grad[:, at : at + part])

    ry = 0 if kept else 1
    first[...] = product([(q, ry) for q in range(4)], 0).astype(first.dtype)
    places = (0,) if kept else (1, 2, 3)
    value = product([(q, ry) for q in places for ry in range(2)], part)
    for n, second in enumerate(seconds):
        second[...] = value[n * 2 * block : (n + 1) * 2 * block].astype(second.dtype)


def shaped(shape, dtype=F32):
    return jax.ShapeDtypeStruct(shape, dtype)


def added(kept, sent, swap, bits):
    return kept + swap(sent.astype(BF16), bits).astype(F32)


def folded(value, swap, bits):
    rows = value.shape[0] // 2
    return added(value[:rows], value[rows:], swap, bits)


def all_added(value, swap, bits):
    value = lax.reduce_precision(value, 8, 7)
    return added(value, value, swap, bits)


def on_device(
    context, residual, out_weight, norm_gain, user_vectors, positive, item_ids, item_counts, lengths
):
    tokens, head = context.shape
    width = residual.shape[1]
    items_here = lengths.shape[0]
    users_here = user_vectors.shape[0]
    dp, fsdp = lax.axis_index("dp"), lax.axis_index("fsdp")
    y_lo, z, core = dp // 8, (dp // 2) % 4, dp % 2
    y_hi, x = fsdp // 4, fsdp % 4
    y = y_hi * 2 + y_lo
    where = jnp.stack([x, y, z, core]).astype(jnp.int32)
    half, part = width // 2, width // 4
    rows = out_weight.shape[0]
    gain = norm_gain[None, :]

    columns = [part_columns for _, part_columns, _ in parts_of(half)]
    rode = users_here * (width // columns[2])
    travel = pl.pallas_call(
        pack_kernel,
        out_shape=(
            shaped((rows, columns[0]), BF16),
            shaped((rows, columns[1]), BF16),
            shaped((rows + rode, columns[2]), BF16),
        ),
        in_specs=[ANY] * 2,
        out_specs=(VMEM,) * 3,
        scratch_shapes=[
            pltpu.VMEM((users_here, width), BF16),
            pltpu.SemaphoreType.DMA((4,)),
        ],
        compiler_params=params(6),
        name="pack",
    )(out_weight, user_vectors)
    steps = ((swap_y, 3), (swap_x, 1), (swap_x, 3))
    for step in range(2):
        turns = [steps[step], steps[step + 1], steps[(step + 2) % 3]]
        travel = [jnp.concatenate([v, swap(v, n)], axis=0) for v, (swap, n) in zip(travel, turns)]
        travel = lax.optimization_barrier(travel)
    arrived = [swap_x(travel[0], 3), swap_y(travel[1], 3), swap_x(travel[2], 1)]
    arrived = lax.optimization_barrier(arrived)
    pieces = [piece for both in zip(travel, arrived) for piece in both]
    pieces = pieces + [swap_core(p) for p in pieces]
    ints, filled = 0, 0
    numbers = (where, lengths, item_ids, item_counts, positive)
    count = sum(v.shape[0] for v in numbers)
    for v in numbers:
        ints = ints + jnp.pad(v, (filled, count - filled - v.shape[0]))
        filled += v.shape[0]

    stream, inverse, pooled, emb = pl.pallas_call(
        functools.partial(forward_kernel, items_here),
        out_shape=(
            shaped((tokens, width)),
            shaped((tokens, 1)),
            shaped((items_here, width)),
            shaped((items_here, width + LABELS), BF16),
        ),
        in_specs=[SMEM, VMEM, HBM] + [VMEM] * 13,
        out_specs=(VMEM,) * 4,
        scratch_shapes=[pltpu.VMEM((tokens, width), BF16), pltpu.SemaphoreType.DMA],
        compiler_params=params(20),
        name="forward",
    )(ints, context, residual, gain, *pieces)

    emb = lax.optimization_barrier(jnp.concatenate(four(emb, swap_x), axis=0))
    peer_context = swap_core(after(context, emb))
    emb = lax.optimization_barrier(jnp.concatenate(four(emb, swap_y), axis=0))
    emb_pieces = four(emb, swap_z)
    emb_pieces = emb_pieces + [swap_core(p) for p in emb_pieces]

    items, people = 128 * items_here, 16 * users_here
    riding = pieces[4:6] + pieces[10:12]
    *sums, user_grad = pl.pallas_call(
        functools.partial(loss_kernel, users_here, items_here, rows),
        out_shape=(shaped((8, width)),) * 4 + (shaped((users_here, width), BF16),),
        in_specs=[SMEM, VMEM] + [ANY] * 4 + [VMEM] * 8,
        out_specs=(VMEM,) * 5,
        scratch_shapes=[
            pltpu.VMEM((people, items), F32),
            pltpu.VMEM((items, width), F32),
            pltpu.VMEM((16 * rode, columns[2]), BF16),
            pltpu.SemaphoreType.DMA((16,)),
        ],
        compiler_params=params(24),
        name="loss",
    )(where, gain, *riding, *emb_pieces)
    sums = [sums[0]] + [swap_z(sums[q], OFFSETS[q]) for q in (1, 2, 3)]
    sums = (sums[0] + sums[1]) + (sums[2] + sums[3])

    residual_grad, keep, send, gain_grad, loss = pl.pallas_call(
        functools.partial(residual_kernel, 8 * people),
        out_shape=(
            shaped((tokens, width), BF16),
            shaped((tokens, half), BF16),
            shaped((tokens, half), BF16),
            shaped((1, width)),
            shaped((1, 1)),
        ),
        in_specs=[SMEM, SMEM] + [VMEM] * 6,
        out_specs=(VMEM,) * 5,
        compiler_params=params(16),
        name="residual",
    )(where, lengths, stream, inverse, pooled, gain, sums, swap_y(sums, 1))
    peer_grad = swap_core(send)
    context_grad = pl.pallas_call(
        context_kernel,
        out_shape=shaped((tokens, head), BF16),
        in_specs=[SMEM] + [VMEM] * 14,
        out_specs=VMEM,
        compiler_params=params(14),
        name="context",
    )(where, keep, send, *pieces)

    operands = (where, context, peer_context, keep, peer_grad)

    def blocks(kept, dtype, name):
        counts = 1 if kept else 3
        return pl.pallas_call(
            functools.partial(blocks_kernel, kept),
            out_shape=(shaped((4 * rows, part), dtype),) + (shaped((2 * rows, part), dtype),) * counts,
            in_specs=[SMEM] + [VMEM] * 4,
            out_specs=(VMEM,) * (1 + counts),
            compiler_params=params(16),
            name=name,
        )(*operands)

    first_sent, *second_sent = blocks(False, BF16, "blocks_sent")
    first, second = blocks(True, F32, "blocks_kept")
    first, second, context_grad = lax.optimization_barrier((first, second, context_grad))
    first = added(first, first_sent, swap_y, 3)
    arrived = [swap_x(first[q * rows : (q + 1) * rows].astype(BF16), OFFSETS[q]) for q in (1, 2, 3)]
    for q in (1, 2, 3):
        second = second + swap_x(second_sent[q - 1], OFFSETS[q]).astype(F32)
    second = folded(second, swap_y, 3)
    first = first[:rows]
    for piece in arrived:
        first = first + piece.astype(F32)
    first = all_added(first, swap_y, 1)
    second = all_added(second, swap_z, 1)
    first = all_added(first, swap_z, 1)
    second = all_added(second, swap_z, 3)
    first = all_added(first, swap_z, 3)
    second = all_added(second, swap_y, 1)
    own = jnp.concatenate([first, second], axis=1).astype(BF16)
    other = swap_core(own)
    weight_grad = jnp.where(
        core == 0, jnp.concatenate([own, other], axis=1), jnp.concatenate([other, own], axis=1)
    )
    return (loss[0, 0], residual_grad, context_grad, weight_grad, gain_grad[0], user_grad)


def solution(mesh):
    placed = (
        P(AXES, None),
        P(AXES, None),
        P("fsdp", None),
        P(),
        P(AXES, None),
        P(AXES),
        P(AXES),
        P(AXES),
        P(AXES),
    )
    return jax.shard_map(
        on_device,
        mesh=mesh,
        in_specs=placed,
        out_specs=(P(), P(AXES, None), P(AXES, None), P("fsdp", None), P(), P(AXES, None)),
        check_vma=False,
    )
```

```python
import functools

import jax
import jax.numpy as jnp
from jax import lax
from jax.experimental import pallas as pl
from jax.experimental.pallas import tpu as pltpu
from jax.sharding import PartitionSpec as P

EPSILON = 1e-06
MASKED_FILL = -1e30
AXES = ("dp", "fsdp")
F32 = jnp.float32
BF16 = jnp.bfloat16
VMEM = pl.BlockSpec(memory_space=pltpu.VMEM)
SMEM = pl.BlockSpec(memory_space=pltpu.SMEM)
HBM = pl.BlockSpec(memory_space=pltpu.HBM)
ANY = pl.BlockSpec(memory_space=pl.ANY)


def params(mebibytes):
    return pltpu.CompilerParams(vmem_limit_bytes=mebibytes * 1024 * 1024)


def after(value, other):
    return lax.optimization_barrier((value, other))[0]

LABELS = 128
POSITIVE = 8
OFFSETS = (0, 1, 3, 2)


def linear(x, y, z, c):
    return ((((y % 2) * 4 + z) * 2 + c) * 2 + y // 2) * 4 + x


def move(value, where):
    perm = []
    for x in range(4):
        for y in range(4):
            for z in range(4):
                for c in range(2):
                    perm.append((linear(x, y, z, c), linear(*where(x, y, z, c))))
    return lax.ppermute(value, AXES, perm)


def swap_core(value):
    return move(value, lambda x, y, z, c: (x, y, z, 1 - c))


def swap_x(value, bits):
    return move(value, lambda x, y, z, c: (x ^ bits, y, z, c))


def swap_y(value, bits):
    return move(value, lambda x, y, z, c: (x, y ^ bits, z, c))


def swap_z(value, bits):
    return move(value, lambda x, y, z, c: (x, y, z ^ bits, c))


def four(value, swap):
    return [value] + [swap(value, bits) for bits in OFFSETS[1:]]


def doubled(value, swap, bits):
    return lax.optimization_barrier(jnp.concatenate([value, swap(value, bits)], axis=0))


def dot(left, right):
    return jnp.dot(left, right, preferred_element_type=F32)


def contract_rows(left, right):
    return lax.dot_general(left, right, (((0,), (0,)), ((), ())), preferred_element_type=F32)


def contract_last(left, right):
    return lax.dot_general(left, right, (((1,), (1,)), ((), ())), preferred_element_type=F32)


def parts_of(half):
    wide = half * 3 // 8
    pair = range(2)
    return (
        (0, wide, [[(r3 * 2 + r1, ry) for r1 in pair for ry in pair] for r3 in pair]),
        (wide, wide, [[(q, ry) for q in range(4)] for ry in pair]),
        (
            2 * wide,
            half - 2 * wide,
            [[(r3 * 2 + r1, ry) for ry in pair for r3 in pair] for r1 in pair],
        ),
    )


def block_home(x, y_hi, q, ry):
    return (y_hi ^ ry) * 4 + (x ^ OFFSETS[q])


def blocks_of(ref, where, pairs, block):
    picked = []
    for q, ry in pairs:
        home = block_home(where[0], where[1] // 2, q, ry)
        picked.append(ref[:, pl.ds(pl.multiple_of(home * block, block), block)])
    return jnp.concatenate(picked, axis=1)


def weight_rows(ref, block):
    rows = ref.shape[0] // 4
    if rows == block:
        return ref[...]
    return jnp.concatenate([ref[q * rows : q * rows + block, :] for q in range(4)], axis=0)


def pack_kernel(weight, users, first, second, third, held, sems):
    rows, width = weight.shape
    half = width // 2
    mine = (lax.axis_index("dp") % 2) * half
    copies = [pltpu.make_async_copy(users, held, sems.at[3])]
    for n, ((start, columns, _), out) in enumerate(zip(parts_of(half), (first, second, third))):
        at = pl.multiple_of(mine + start, 128)
        copies.append(
            pltpu.make_async_copy(
                weight.at[:, pl.ds(at, columns)], out.at[pl.ds(0, rows)], sems.at[n]
            )
        )
    for copy in copies:
        copy.start()
    for copy in copies:
        copy.wait()
    part = third.shape[1]
    wide = held[...].astype(F32)
    riding = [wide[:, j * part : (j + 1) * part] for j in range(width // part)]
    third[rows:, :] = jnp.concatenate(riding, axis=0).astype(BF16)


def forward_kernel(items, ints, context, residual, gain, *refs):
    stream, inverse, pooled, embedding, added_rows, sem = refs[12:]
    where = [ints[i] for i in range(4)]
    lengths, ids, counts = ([ints[4 + j * items + i] for i in range(items)] for j in range(3))
    positive = [ints[i] for i in range(4 + 3 * items, ints.shape[0])]
    tokens, width = residual.shape
    half = width // 2
    block = context.shape[1] // 8
    length = tokens // items
    copy = pltpu.make_async_copy(residual, added_rows, sem)
    copy.start()
    for p, (start, columns, orders) in enumerate(parts_of(half)):
        lanes = [blocks_of(context, where, order, block) for order in orders]
        for side in range(2):
            base = where[3] * half if side == 0 else (1 - where[3]) * half
            stream[:, pl.ds(pl.multiple_of(base + start, 128), columns)] = sum(
                dot(lanes[k], weight_rows(refs[side * 6 + p * 2 + k], block)) for k in range(2)
            )
    copy.wait()
    for i in range(items):
        span = slice(i * length, (i + 1) * length)
        rows = stream[span, :] + added_rows[span, :].astype(F32)
        stream[span, :] = rows
        inv = lax.rsqrt(jnp.mean(rows * rows, axis=-1, keepdims=True) + EPSILON)
        inverse[i * length : (i + 1) * length, :] = inv
        position = lax.broadcasted_iota(jnp.int32, (length, 1), 0)
        kept = jnp.where(position < lengths[i], inv, 0.0)
        total = jnp.sum(rows * kept, axis=0, keepdims=True)
        pooled[i : i + 1, :] = total * gain[...] / lengths[i].astype(F32)
    pool = pooled[...]
    scale = lax.rsqrt(jnp.mean(pool * pool, axis=-1, keepdims=True) + EPSILON)
    embedding[:, :width] = (pool * scale).astype(BF16)
    row = lax.broadcasted_iota(jnp.int32, (items, LABELS), 0)
    lane = lax.broadcasted_iota(jnp.int32, (items, LABELS), 1)
    labels = jnp.zeros((items, LABELS), jnp.int32)
    for i in range(items):
        for at, value in enumerate((ids[i], counts[i] // 128, counts[i] % 128)):
            labels = jnp.where((row == i) & (lane == at), value, labels)
    for u in range(len(positive)):
        labels = jnp.where((row == 0) & (lane == POSITIVE + u), positive[u], labels)
    embedding[:, width:] = labels.astype(F32).astype(BF16)


def bit(value, k):
    return (value >> k) & 1


def one_hot_turn(rows, home):
    to = lax.broadcasted_iota(jnp.int32, (rows, rows), 0)
    of = lax.broadcasted_iota(jnp.int32, (rows, rows), 1)
    return jnp.where(to == home(of), 1.0, 0.0).astype(BF16)


def loss_kernel(users_here, items_here, block, where, gain, *refs):
    piece_refs, emb_refs = refs[:4], refs[4:12]
    sums, user_grad, grads, emb_grads, riders, sems = refs[12:16], *refs[16:]
    x, y, z, core = where[0], where[1], where[2], where[3]
    group, full = emb_refs[0].shape
    width = full - LABELS
    items = 8 * group
    people = 16 * users_here
    stride, part = piece_refs[0].shape[0] // 4, piece_refs[0].shape[1]
    parts = width // part
    rode = parts * users_here
    copies = []
    for n in range(4):
        for b in range(4):
            copies.append(
                pltpu.make_async_copy(
                    piece_refs[n].at[pl.ds(b * stride + block, rode)],
                    riders.at[pl.ds((n * 4 + b) * rode, rode)],
                    sems.at[n * 4 + b],
                )
            )
    for copy in copies:
        copy.start()

    def item_home(s):
        one = s // items_here
        ax = x ^ bit(one, 0) ^ (3 * bit(one, 1))
        ay = y ^ bit(one, 2) ^ (3 * bit(one, 3))
        az = z ^ bit(one, 4) ^ (3 * bit(one, 5))
        ac = core ^ bit(one, 6)
        return (((ac * 4 + az) * 4 + ay) * 4 + ax) * items_here + s % items_here

    placed = jnp.concatenate([ref[...] for ref in emb_refs], axis=0)
    turned = dot(one_hot_turn(items, item_home), placed).astype(BF16)
    emb, labels = turned[:, :width], turned[:, width:]
    for copy in copies:
        copy.wait()
    def user_home(s):
        one = s // users_here
        ac, ay = core ^ bit(one, 3), (y // 2) ^ bit(one, 1)
        ax = x ^ bit(one, 2) ^ (3 * bit(one, 0))
        return ((ac * 2 + ay) * 4 + ax) * users_here + s % users_here

    wide = riders[...].astype(F32)
    placed = jnp.concatenate(
        [
            jnp.concatenate(
                [
                    wide[n * rode + j * users_here : n * rode + (j + 1) * users_here, :]
                    for n in range(16)
                ],
                axis=0,
            )
            for j in range(parts)
        ],
        axis=1,
    ).astype(BF16)
    users = dot(one_hot_turn(people, user_home), placed).astype(BF16)
    person = lax.broadcasted_iota(jnp.int32, (people, items), 0)
    at = lax.broadcasted_iota(jnp.int32, (people, items), 1)
    g = person // users_here
    g_y = jnp.where((g // 4) % 2 == y // 2, y, 3 - y)
    g_row = (((g // 8 * 4 + z) * 4 + g_y) * 4 + g % 4) * items_here
    positives = dot(jnp.where(at == g_row, 1.0, 0.0).astype(BF16), labels)
    lane = lax.broadcasted_iota(jnp.int32, (people, LABELS), 1)
    slot = lax.broadcasted_iota(jnp.int32, (people, LABELS), 0) % users_here
    positive = jnp.sum(jnp.where(lane == POSITIVE + slot, positives, 0.0), axis=1, keepdims=True)
    item_labels = contract_rows(labels, one_hot_turn(items, lambda s: s))
    ids = item_labels[0:1, :]
    log_counts = jnp.log(item_labels[1:2, :] * 128.0 + item_labels[2:3, :])
    item = lax.broadcasted_iota(jnp.int32, (1, items), 1)
    chip = item // items_here
    index = linear(chip % 4, (chip // 4) % 4, (chip // 16) % 4, chip // 64) * items_here
    index = (index + item % items_here).astype(F32)
    onehot = index == positive
    positive_id = jnp.sum(jnp.where(onehot, ids, 0.0), axis=1, keepdims=True)
    excluded = (ids == positive_id) & jnp.logical_not(onehot)
    scores = contract_last(users, emb)
    logits = jnp.where(excluded, MASKED_FILL, scores - log_counts)
    row_max = jnp.max(logits, axis=1, keepdims=True)
    weights = jnp.where(excluded, 0.0, jnp.exp(logits - row_max))
    row_total = jnp.sum(weights, axis=1, keepdims=True)
    picked = jnp.sum(jnp.where(onehot, logits, 0.0), axis=1, keepdims=True)
    losses = row_max + jnp.log(row_total) - picked
    grad = (weights / row_total - jnp.where(onehot, 1.0, 0.0)).astype(BF16)
    grads[...] = grad.astype(F32)
    all_grads = contract_rows(grad, users)
    emb_grads[...] = all_grads
    emb_float = emb.astype(F32)
    product = emb_float * all_grads
    mean = jnp.mean(product, axis=-1, keepdims=True)
    gain_sum = jnp.sum(product - emb_float * emb_float * mean, axis=0, keepdims=True)
    line = lax.broadcasted_iota(jnp.int32, (8 * items_here, 1), 0)
    loss = jnp.broadcast_to(jnp.sum(losses, axis=0, keepdims=True), (1, width))
    for q in range(4):
        az = z ^ OFFSETS[q]
        start = ((core * 4 + az) * 4 + (y // 2) * 2) * 4 * items_here
        rows = emb_grads[pl.ds(pl.multiple_of(start, 8 * items_here), 8 * items_here), :]
        for other in range(2):
            for i in range(items_here):
                chosen = line == (((y % 2) ^ other) * 4 + x) * items_here + i
                n = other * items_here + i
                sums[q][n : n + 1, :] = jnp.sum(
                    jnp.where(chosen, rows, 0.0), axis=0, keepdims=True
                )
        sums[q][2 * items_here : 2 * items_here + 1, :] = gain_sum
        sums[q][2 * items_here + 1 :, :] = jnp.broadcast_to(loss, (6 - 2 * items_here + 1, width))
    place = ((core * 2 + y // 2) * 4 + x) * users_here
    own = grads[pl.ds(pl.multiple_of(place, users_here), users_here), :]
    user_grad[...] = dot(own.astype(BF16), emb).astype(BF16)


def residual_kernel(people, where, lengths, stream, inverse, pooled, gain, *refs):
    own_sums, other_sums, residual_grad, keep, send, gain_grad, loss = refs
    tokens, width = stream.shape
    half = width // 2
    items = lengths.shape[0]
    length = tokens // items
    for i in range(items):
        mine = own_sums[i : i + 1, :] + other_sums[items + i : items + i + 1, :]
        pool = pooled[i : i + 1, :]
        scale = lax.rsqrt(jnp.mean(pool * pool, axis=-1, keepdims=True) + EPSILON)
        pool_grad = scale * mine - pool * scale * scale * scale * jnp.mean(
            pool * mine, axis=-1, keepdims=True
        )
        row = gain[...] * pool_grad / lengths[i].astype(F32)
        span = slice(i * length, (i + 1) * length)
        rows = stream[span, :]
        inv = inverse[span, :]
        position = lax.broadcasted_iota(jnp.int32, (length, 1), 0)
        kept = jnp.where(position < lengths[i], inv, 0.0)
        mean = jnp.mean(rows * row, axis=-1, keepdims=True)
        residual_grad[span, :] = (kept * row - rows * (kept * inv * inv * mean)).astype(BF16)
    keep[...] = residual_grad[:, pl.ds(pl.multiple_of(where[3] * half, half), half)]
    send[...] = residual_grad[:, pl.ds(pl.multiple_of((1 - where[3]) * half, half), half)]
    at = 2 * items
    gain_grad[...] = (own_sums[at : at + 1, :] + other_sums[at : at + 1, :]) / gain[...]
    at = at + 1
    loss[...] = (own_sums[at : at + 1, 0:1] + other_sums[at : at + 1, 0:1]) / people


def context_kernel(where, keep, send, *refs):
    context_grad = refs[12]
    half = keep.shape[1]
    block = context_grad.shape[1] // 8
    values = {}
    for p, (start, columns, orders) in enumerate(parts_of(half)):
        for k, order in enumerate(orders):
            product = sum(
                contract_last(
                    grad[:, start : start + columns], weight_rows(refs[side * 6 + p * 2 + k], block)
                )
                for side, grad in enumerate((keep, send))
            )
            for b, place in enumerate(order):
                piece = product[:, b * block : (b + 1) * block]
                values[place] = values[place] + piece if place in values else piece
    for (q, ry), value in values.items():
        home = block_home(where[0], where[1] // 2, q, ry)
        context_grad[:, pl.ds(pl.multiple_of(home * block, block), block)] = value.astype(BF16)


def blocks_kernel(first_blocks, second_blocks, where, own_context, peer_context, own_grad, peer_grad, *outs):
    part = own_grad.shape[1] // 2
    block = own_context.shape[1] // 8
    outs = list(outs)
    for at, blocks in ((0, first_blocks), (part, second_blocks)):
        if not blocks:
            continue
        value = contract_rows(
            blocks_of(own_context, where, blocks, block), own_grad[:, at : at + part]
        ) + contract_rows(blocks_of(peer_context, where, blocks, block), peer_grad[:, at : at + part])
        done = 0
        while done < value.shape[0]:
            out = outs.pop(0)
            out[...] = value[done : done + out.shape[0]].astype(out.dtype)
            done += out.shape[0]


def shaped(shape, dtype=F32):
    return jax.ShapeDtypeStruct(shape, dtype)


def added(kept, sent, swap, bits):
    return kept + swap(sent.astype(BF16), bits).astype(F32)


def folded(value, swap, bits):
    rows = value.shape[0] // 2
    return added(value[:rows], value[rows:], swap, bits)


def all_added(value, swap, bits):
    value = lax.reduce_precision(value, 8, 7)
    return added(value, value, swap, bits)


def on_device(
    context, residual, out_weight, norm_gain, user_vectors, positive, item_ids, item_counts, lengths
):
    tokens, head = context.shape
    width = residual.shape[1]
    items_here = lengths.shape[0]
    users_here = user_vectors.shape[0]
    dp, fsdp = lax.axis_index("dp"), lax.axis_index("fsdp")
    y_lo, z, core = dp // 8, (dp // 2) % 4, dp % 2
    y_hi, x = fsdp // 4, fsdp % 4
    y = y_hi * 2 + y_lo
    where = jnp.stack([x, y, z, core]).astype(jnp.int32)
    half, part = width // 2, width // 4
    rows = out_weight.shape[0]
    gain = norm_gain[None, :]

    columns = [part_columns for _, part_columns, _ in parts_of(half)]
    rode = users_here * (width // columns[2])
    travel = pl.pallas_call(
        pack_kernel,
        out_shape=(
            shaped((rows, columns[0]), BF16),
            shaped((rows, columns[1]), BF16),
            shaped((rows + rode, columns[2]), BF16),
        ),
        in_specs=[ANY] * 2,
        out_specs=(VMEM,) * 3,
        scratch_shapes=[
            pltpu.VMEM((users_here, width), BF16),
            pltpu.SemaphoreType.DMA((4,)),
        ],
        compiler_params=params(6),
        name="pack",
    )(out_weight, user_vectors)
    steps = ((swap_y, 3), (swap_x, 1), (swap_x, 3))
    for step in range(2):
        turns = [steps[step], steps[step + 1], steps[(step + 2) % 3]]
        travel = [jnp.concatenate([v, swap(v, n)], axis=0) for v, (swap, n) in zip(travel, turns)]
        travel = lax.optimization_barrier(travel)
    arrived = [swap_x(travel[0], 3), swap_y(travel[1], 3), swap_x(travel[2], 1)]
    arrived = lax.optimization_barrier(arrived)
    pieces = [piece for both in zip(travel, arrived) for piece in both]
    pieces = pieces + [swap_core(p) for p in pieces]
    ints, filled = 0, 0
    numbers = (where, lengths, item_ids, item_counts, positive)
    count = sum(v.shape[0] for v in numbers)
    for v in numbers:
        ints = ints + jnp.pad(v, (filled, count - filled - v.shape[0]))
        filled += v.shape[0]

    stream, inverse, pooled, emb = pl.pallas_call(
        functools.partial(forward_kernel, items_here),
        out_shape=(
            shaped((tokens, width)),
            shaped((tokens, 1)),
            shaped((items_here, width)),
            shaped((items_here, width + LABELS), BF16),
        ),
        in_specs=[SMEM, VMEM, HBM] + [VMEM] * 13,
        out_specs=(VMEM,) * 4,
        scratch_shapes=[pltpu.VMEM((tokens, width), BF16), pltpu.SemaphoreType.DMA],
        compiler_params=params(16),
        name="forward",
    )(ints, context, residual, gain, *pieces)

    emb = lax.optimization_barrier(jnp.concatenate(four(emb, swap_x), axis=0))
    peer_context = swap_core(after(context, emb))
    emb = lax.optimization_barrier(jnp.concatenate(four(emb, swap_y), axis=0))
    emb_pieces = four(emb, swap_z)
    emb_pieces = emb_pieces + [swap_core(p) for p in emb_pieces]

    items, people = 128 * items_here, 16 * users_here
    riding = pieces[4:6] + pieces[10:12]
    *sums, user_grad = pl.pallas_call(
        functools.partial(loss_kernel, users_here, items_here, rows),
        out_shape=(shaped((8, width)),) * 4 + (shaped((users_here, width), BF16),),
        in_specs=[SMEM, VMEM] + [ANY] * 4 + [VMEM] * 8,
        out_specs=(VMEM,) * 5,
        scratch_shapes=[
            pltpu.VMEM((people, items), F32),
            pltpu.VMEM((items, width), F32),
            pltpu.VMEM((16 * rode, columns[2]), BF16),
            pltpu.SemaphoreType.DMA((16,)),
        ],
        compiler_params=params(18),
        name="loss",
    )(where, gain, *riding, *emb_pieces)
    sums = [sums[0]] + [swap_z(sums[q], OFFSETS[q]) for q in (1, 2, 3)]
    sums = (sums[0] + sums[1]) + (sums[2] + sums[3])

    residual_grad, keep, send, gain_grad, loss = pl.pallas_call(
        functools.partial(residual_kernel, 8 * people),
        out_shape=(
            shaped((tokens, width), BF16),
            shaped((tokens, half), BF16),
            shaped((tokens, half), BF16),
            shaped((1, width)),
            shaped((1, 1)),
        ),
        in_specs=[SMEM, SMEM] + [VMEM] * 6,
        out_specs=(VMEM,) * 5,
        compiler_params=params(16),
        name="residual",
    )(where, lengths, stream, inverse, pooled, gain, sums, swap_y(sums, 1))
    peer_grad = swap_core(send)
    context_grad = pl.pallas_call(
        context_kernel,
        out_shape=shaped((tokens, head), BF16),
        in_specs=[SMEM] + [VMEM] * 14,
        out_specs=VMEM,
        compiler_params=params(14),
        name="context",
    )(where, keep, send, *pieces)

    def blocks(first_blocks, second_blocks, heights, dtype, operands, name):
        return pl.pallas_call(
            functools.partial(blocks_kernel, first_blocks, second_blocks),
            out_shape=tuple(shaped((height * rows, half // 2), dtype) for height in heights),
            in_specs=[SMEM] + [VMEM] * 4,
            out_specs=(VMEM,) * len(heights),
            compiler_params=params(14),
            name=name,
        )(where, *operands)

    def with_ry(ry):
        return [(q, ry) for q in range(4)]

    def with_q(*places):
        return [(q, ry) for q in places for ry in range(2)]

    operands = (context, peer_context, keep, peer_grad)
    (first_sent,) = blocks(with_ry(1), [], (4,), BF16, operands, "first_sent")
    first_sent, peer_grad = lax.optimization_barrier((first_sent, peer_grad))
    operands = (context, peer_context, keep, peer_grad)
    second_sent = blocks([], with_q(1, 2, 3), (2, 2, 2), BF16, operands, "second_sent")
    first, second = blocks(with_ry(0), with_q(0), (4, 2), F32, operands, "kept")
    arrived = [swap_y(first_sent, 3)] + [swap_x(second_sent[q - 1], OFFSETS[q]) for q in (1, 2, 3)]
    arrived, first, second, context_grad = lax.optimization_barrier(
        (arrived, first, second, context_grad)
    )
    first = first + arrived[0].astype(F32)
    for piece in arrived[1:]:
        second = second + piece.astype(F32)
    arrived = [swap_x(first[q * rows : (q + 1) * rows].astype(BF16), OFFSETS[q]) for q in (1, 2, 3)]
    second = folded(second, swap_y, 3)
    first = first[:rows]
    for piece in arrived:
        first = first + piece.astype(F32)
    first = all_added(first, swap_y, 1)
    second = all_added(second, swap_z, 1)
    first = all_added(first, swap_z, 1)
    second = all_added(second, swap_z, 3)
    first = all_added(first, swap_z, 3)
    second = all_added(second, swap_y, 1)
    own = jnp.concatenate([first, second], axis=1).astype(BF16)
    other = swap_core(own)
    weight_grad = jnp.where(
        core == 0, jnp.concatenate([own, other], axis=1), jnp.concatenate([other, own], axis=1)
    )
    return (loss[0, 0], residual_grad, context_grad, weight_grad, gain_grad[0], user_grad)


def solution(mesh):
    placed = (
        P(AXES, None),
        P(AXES, None),
        P("fsdp", None),
        P(),
        P(AXES, None),
        P(AXES),
        P(AXES),
        P(AXES),
        P(AXES),
    )
    return jax.shard_map(
        on_device,
        mesh=mesh,
        in_specs=placed,
        out_specs=(P(), P(AXES, None), P(AXES, None), P("fsdp", None), P(), P(AXES, None)),
        check_vma=False,
    )
```

```python
import functools

import jax
import jax.numpy as jnp
from jax import lax
from jax.experimental import pallas as pl
from jax.experimental.pallas import tpu as pltpu
from jax.sharding import PartitionSpec as P

EPSILON = 1e-06
MASKED_FILL = -1e30
AXES = ("dp", "fsdp")
F32 = jnp.float32
BF16 = jnp.bfloat16
VMEM = pl.BlockSpec(memory_space=pltpu.VMEM)
SMEM = pl.BlockSpec(memory_space=pltpu.SMEM)
HBM = pl.BlockSpec(memory_space=pltpu.HBM)
ANY = pl.BlockSpec(memory_space=pl.ANY)


def params(mebibytes):
    return pltpu.CompilerParams(vmem_limit_bytes=mebibytes * 1024 * 1024)


def after(value, other):
    return lax.optimization_barrier((value, other))[0]

LABELS = 128
POSITIVE = 8
OFFSETS = (0, 1, 3, 2)


def linear(x, y, z, c):
    return ((((y % 2) * 4 + z) * 2 + c) * 2 + y // 2) * 4 + x


def move(value, where):
    perm = []
    for x in range(4):
        for y in range(4):
            for z in range(4):
                for c in range(2):
                    perm.append((linear(x, y, z, c), linear(*where(x, y, z, c))))
    return lax.ppermute(value, AXES, perm)


def swap_core(value):
    return move(value, lambda x, y, z, c: (x, y, z, 1 - c))


def swap_x(value, bits):
    return move(value, lambda x, y, z, c: (x ^ bits, y, z, c))


def swap_y(value, bits):
    return move(value, lambda x, y, z, c: (x, y ^ bits, z, c))


def swap_z(value, bits):
    return move(value, lambda x, y, z, c: (x, y, z ^ bits, c))


def four(value, swap):
    return [value] + [swap(value, bits) for bits in OFFSETS[1:]]


def doubled(value, swap, bits):
    return lax.optimization_barrier(jnp.concatenate([value, swap(value, bits)], axis=0))


def dot(left, right):
    return jnp.dot(left, right, preferred_element_type=F32)


def contract_rows(left, right):
    return lax.dot_general(left, right, (((0,), (0,)), ((), ())), preferred_element_type=F32)


def contract_last(left, right):
    return lax.dot_general(left, right, (((1,), (1,)), ((), ())), preferred_element_type=F32)


def parts_of(half):
    wide = half * 3 // 8
    pair = range(2)
    return (
        (0, wide, [[(r3 * 2 + r1, ry) for r1 in pair for ry in pair] for r3 in pair]),
        (wide, wide, [[(q, ry) for q in range(4)] for ry in pair]),
        (
            2 * wide,
            half - 2 * wide,
            [[(r3 * 2 + r1, ry) for ry in pair for r3 in pair] for r1 in pair],
        ),
    )


def block_home(x, y_hi, q, ry):
    return (y_hi ^ ry) * 4 + (x ^ OFFSETS[q])


def blocks_of(ref, where, pairs, block):
    picked = []
    for q, ry in pairs:
        home = block_home(where[0], where[1] // 2, q, ry)
        picked.append(ref[:, pl.ds(pl.multiple_of(home * block, block), block)])
    return jnp.concatenate(picked, axis=1)


def weight_rows(ref, block):
    rows = ref.shape[0] // 4
    if rows == block:
        return ref[...]
    return jnp.concatenate([ref[q * rows : q * rows + block, :] for q in range(4)], axis=0)


def pack_kernel(weight, users, first, second, third, held, sems):
    rows, width = weight.shape
    half = width // 2
    mine = (lax.axis_index("dp") % 2) * half
    copies = [pltpu.make_async_copy(users, held, sems.at[3])]
    for n, ((start, columns, _), out) in enumerate(zip(parts_of(half), (first, second, third))):
        at = pl.multiple_of(mine + start, 128)
        copies.append(
            pltpu.make_async_copy(
                weight.at[:, pl.ds(at, columns)], out.at[pl.ds(0, rows)], sems.at[n]
            )
        )
    for copy in copies:
        copy.start()
    for copy in copies:
        copy.wait()
    part = third.shape[1]
    wide = held[...].astype(F32)
    riding = [wide[:, j * part : (j + 1) * part] for j in range(width // part)]
    third[rows:, :] = jnp.concatenate(riding, axis=0).astype(BF16)


def forward_kernel(items, ints, context, residual, gain, *refs):
    stream, inverse, pooled, embedding = refs[12:]
    where = [ints[i] for i in range(4)]
    lengths, ids, counts = ([ints[4 + j * items + i] for i in range(items)] for j in range(3))
    positive = [ints[i] for i in range(4 + 3 * items, ints.shape[0])]
    tokens, width = residual.shape
    half = width // 2
    block = context.shape[1] // 8
    length = tokens // items
    for p, (start, columns, orders) in enumerate(parts_of(half)):
        lanes = [blocks_of(context, where, order, block) for order in orders]
        for side in range(2):
            base = where[3] * half if side == 0 else (1 - where[3]) * half
            stream[:, pl.ds(pl.multiple_of(base + start, 128), columns)] = sum(
                dot(lanes[k], weight_rows(refs[side * 6 + p * 2 + k], block)) for k in range(2)
            )
    for i in range(items):
        span = slice(i * length, (i + 1) * length)
        rows = stream[span, :] + residual[span, :].astype(F32)
        stream[span, :] = rows
        inv = lax.rsqrt(jnp.mean(rows * rows, axis=-1, keepdims=True) + EPSILON)
        inverse[i * length : (i + 1) * length, :] = inv
        position = lax.broadcasted_iota(jnp.int32, (length, 1), 0)
        kept = jnp.where(position < lengths[i], inv, 0.0)
        total = jnp.sum(rows * kept, axis=0, keepdims=True)
        pooled[i : i + 1, :] = total * gain[...] / lengths[i].astype(F32)
    pool = pooled[...]
    scale = lax.rsqrt(jnp.mean(pool * pool, axis=-1, keepdims=True) + EPSILON)
    embedding[:, :width] = (pool * scale).astype(BF16)
    row = lax.broadcasted_iota(jnp.int32, (items, LABELS), 0)
    lane = lax.broadcasted_iota(jnp.int32, (items, LABELS), 1)
    labels = jnp.zeros((items, LABELS), jnp.int32)
    for i in range(items):
        for at, value in enumerate((ids[i], counts[i] // 128, counts[i] % 128)):
            labels = jnp.where((row == i) & (lane == at), value, labels)
    for u in range(len(positive)):
        labels = jnp.where((row == 0) & (lane == POSITIVE + u), positive[u], labels)
    embedding[:, width:] = labels.astype(F32).astype(BF16)


def bit(value, k):
    return (value >> k) & 1


def one_hot_turn(rows, home):
    to = lax.broadcasted_iota(jnp.int32, (rows, rows), 0)
    of = lax.broadcasted_iota(jnp.int32, (rows, rows), 1)
    return jnp.where(to == home(of), 1.0, 0.0).astype(BF16)


def hold_kernel(source, out, sem):
    copy = pltpu.make_async_copy(source, out, sem)
    copy.start()
    copy.wait()


def users_kernel(users_here, block, where, *refs):
    piece_refs, (out, riders, sems) = refs[:4], refs[4:]
    x, y, core = where[0], where[1], where[3]
    people, width = out.shape
    stride, part = piece_refs[0].shape[0] // 4, piece_refs[0].shape[1]
    parts = width // part
    rode = parts * users_here
    copies = []
    for n in range(4):
        for b in range(4):
            copies.append(
                pltpu.make_async_copy(
                    piece_refs[n].at[pl.ds(b * stride + block, rode)],
                    riders.at[pl.ds((n * 4 + b) * rode, rode)],
                    sems.at[n * 4 + b],
                )
            )
    for copy in copies:
        copy.start()
    for copy in copies:
        copy.wait()

    def user_home(s):
        one = s // users_here
        ac, ay = core ^ bit(one, 3), (y // 2) ^ bit(one, 1)
        ax = x ^ bit(one, 2) ^ (3 * bit(one, 0))
        return ((ac * 2 + ay) * 4 + ax) * users_here + s % users_here

    wide = riders[...].astype(F32)
    placed = jnp.concatenate(
        [
            jnp.concatenate(
                [
                    wide[n * rode + j * users_here : n * rode + (j + 1) * users_here, :]
                    for n in range(16)
                ],
                axis=0,
            )
            for j in range(parts)
        ],
        axis=1,
    ).astype(BF16)
    out[...] = dot(one_hot_turn(people, user_home), placed).astype(BF16)

def loss_kernel(users_here, items_here, where, gain, users_ref, *refs):
    emb_refs = refs[:8]
    sums, user_grad, grads, emb_grads = refs[8:12], *refs[12:]
    x, y, z, core = where[0], where[1], where[2], where[3]
    group, full = emb_refs[0].shape
    width = full - LABELS
    items = 8 * group
    people = users_ref.shape[0]

    def item_home(s):
        one = s // items_here
        ax = x ^ bit(one, 0) ^ (3 * bit(one, 1))
        ay = y ^ bit(one, 2) ^ (3 * bit(one, 3))
        az = z ^ bit(one, 4) ^ (3 * bit(one, 5))
        ac = core ^ bit(one, 6)
        return (((ac * 4 + az) * 4 + ay) * 4 + ax) * items_here + s % items_here

    placed = jnp.concatenate([ref[...] for ref in emb_refs], axis=0)
    turned = dot(one_hot_turn(items, item_home), placed).astype(BF16)
    emb, labels = turned[:, :width], turned[:, width:]
    users = users_ref[...]
    person = lax.broadcasted_iota(jnp.int32, (people, items), 0)
    at = lax.broadcasted_iota(jnp.int32, (people, items), 1)
    g = person // users_here
    g_y = jnp.where((g // 4) % 2 == y // 2, y, 3 - y)
    g_row = (((g // 8 * 4 + z) * 4 + g_y) * 4 + g % 4) * items_here
    positives = dot(jnp.where(at == g_row, 1.0, 0.0).astype(BF16), labels)
    lane = lax.broadcasted_iota(jnp.int32, (people, LABELS), 1)
    slot = lax.broadcasted_iota(jnp.int32, (people, LABELS), 0) % users_here
    positive = jnp.sum(jnp.where(lane == POSITIVE + slot, positives, 0.0), axis=1, keepdims=True)
    item_labels = contract_rows(labels, one_hot_turn(items, lambda s: s))
    ids = item_labels[0:1, :]
    log_counts = jnp.log(item_labels[1:2, :] * 128.0 + item_labels[2:3, :])
    item = lax.broadcasted_iota(jnp.int32, (1, items), 1)
    chip = item // items_here
    index = linear(chip % 4, (chip // 4) % 4, (chip // 16) % 4, chip // 64) * items_here
    index = (index + item % items_here).astype(F32)
    onehot = index == positive
    positive_id = jnp.sum(jnp.where(onehot, ids, 0.0), axis=1, keepdims=True)
    excluded = (ids == positive_id) & jnp.logical_not(onehot)
    scores = contract_last(users, emb)
    logits = jnp.where(excluded, MASKED_FILL, scores - log_counts)
    row_max = jnp.max(logits, axis=1, keepdims=True)
    weights = jnp.where(excluded, 0.0, jnp.exp(logits - row_max))
    row_total = jnp.sum(weights, axis=1, keepdims=True)
    picked = jnp.sum(jnp.where(onehot, logits, 0.0), axis=1, keepdims=True)
    losses = row_max + jnp.log(row_total) - picked
    grad = (weights / row_total - jnp.where(onehot, 1.0, 0.0)).astype(BF16)
    grads[...] = grad.astype(F32)
    all_grads = contract_rows(grad, users)
    emb_grads[...] = all_grads
    emb_float = emb.astype(F32)
    product = emb_float * all_grads
    mean = jnp.mean(product, axis=-1, keepdims=True)
    gain_sum = jnp.sum(product - emb_float * emb_float * mean, axis=0, keepdims=True)
    line = lax.broadcasted_iota(jnp.int32, (8 * items_here, 1), 0)
    loss = jnp.broadcast_to(jnp.sum(losses, axis=0, keepdims=True), (1, width))
    for q in range(4):
        az = z ^ OFFSETS[q]
        start = ((core * 4 + az) * 4 + (y // 2) * 2) * 4 * items_here
        rows = emb_grads[pl.ds(pl.multiple_of(start, 8 * items_here), 8 * items_here), :]
        for other in range(2):
            for i in range(items_here):
                chosen = line == (((y % 2) ^ other) * 4 + x) * items_here + i
                n = other * items_here + i
                sums[q][n : n + 1, :] = jnp.sum(
                    jnp.where(chosen, rows, 0.0), axis=0, keepdims=True
                )
        sums[q][2 * items_here : 2 * items_here + 1, :] = gain_sum
        sums[q][2 * items_here + 1 :, :] = jnp.broadcast_to(loss, (6 - 2 * items_here + 1, width))
    place = ((core * 2 + y // 2) * 4 + x) * users_here
    own = grads[pl.ds(pl.multiple_of(place, users_here), users_here), :]
    user_grad[...] = dot(own.astype(BF16), emb).astype(BF16)


def residual_kernel(people, where, lengths, stream, inverse, pooled, gain, *refs):
    own_sums, other_sums, residual_grad, keep, send, gain_grad, loss = refs
    tokens, width = stream.shape
    half = width // 2
    items = lengths.shape[0]
    length = tokens // items
    for i in range(items):
        mine = own_sums[i : i + 1, :] + other_sums[items + i : items + i + 1, :]
        pool = pooled[i : i + 1, :]
        scale = lax.rsqrt(jnp.mean(pool * pool, axis=-1, keepdims=True) + EPSILON)
        pool_grad = scale * mine - pool * scale * scale * scale * jnp.mean(
            pool * mine, axis=-1, keepdims=True
        )
        row = gain[...] * pool_grad / lengths[i].astype(F32)
        span = slice(i * length, (i + 1) * length)
        rows = stream[span, :]
        inv = inverse[span, :]
        position = lax.broadcasted_iota(jnp.int32, (length, 1), 0)
        kept = jnp.where(position < lengths[i], inv, 0.0)
        mean = jnp.mean(rows * row, axis=-1, keepdims=True)
        residual_grad[span, :] = (kept * row - rows * (kept * inv * inv * mean)).astype(BF16)
    keep[...] = residual_grad[:, pl.ds(pl.multiple_of(where[3] * half, half), half)]
    send[...] = residual_grad[:, pl.ds(pl.multiple_of((1 - where[3]) * half, half), half)]
    at = 2 * items
    gain_grad[...] = (own_sums[at : at + 1, :] + other_sums[at : at + 1, :]) / gain[...]
    at = at + 1
    loss[...] = (own_sums[at : at + 1, 0:1] + other_sums[at : at + 1, 0:1]) / people


def context_kernel(where, keep, send, *refs):
    context_grad = refs[12]
    half = keep.shape[1]
    block = context_grad.shape[1] // 8
    values = {}
    for p, (start, columns, orders) in enumerate(parts_of(half)):
        for k, order in enumerate(orders):
            product = sum(
                contract_last(
                    grad[:, start : start + columns], weight_rows(refs[side * 6 + p * 2 + k], block)
                )
                for side, grad in enumerate((keep, send))
            )
            for b, place in enumerate(order):
                piece = product[:, b * block : (b + 1) * block]
                values[place] = values[place] + piece if place in values else piece
    for (q, ry), value in values.items():
        home = block_home(where[0], where[1] // 2, q, ry)
        context_grad[:, pl.ds(pl.multiple_of(home * block, block), block)] = value.astype(BF16)


def blocks_kernel(first_blocks, second_blocks, where, own_context, peer_context, own_grad, peer_grad, *outs):
    part = own_grad.shape[1] // 2
    block = own_context.shape[1] // 8
    outs = list(outs)
    for at, blocks in ((0, first_blocks), (part, second_blocks)):
        if not blocks:
            continue
        value = contract_rows(
            blocks_of(own_context, where, blocks, block), own_grad[:, at : at + part]
        ) + contract_rows(blocks_of(peer_context, where, blocks, block), peer_grad[:, at : at + part])
        done = 0
        while done < value.shape[0]:
            out = outs.pop(0)
            out[...] = value[done : done + out.shape[0]].astype(out.dtype)
            done += out.shape[0]


def shaped(shape, dtype=F32):
    return jax.ShapeDtypeStruct(shape, dtype)


def added(kept, sent, swap, bits):
    return kept + swap(sent.astype(BF16), bits).astype(F32)


def folded(value, swap, bits):
    rows = value.shape[0] // 2
    return added(value[:rows], value[rows:], swap, bits)


def all_added(value, swap, bits):
    value = lax.reduce_precision(value, 8, 7)
    return added(value, value, swap, bits)


def on_device(
    context, residual, out_weight, norm_gain, user_vectors, positive, item_ids, item_counts, lengths
):
    tokens, head = context.shape
    width = residual.shape[1]
    items_here = lengths.shape[0]
    users_here = user_vectors.shape[0]
    dp, fsdp = lax.axis_index("dp"), lax.axis_index("fsdp")
    y_lo, z, core = dp // 8, (dp // 2) % 4, dp % 2
    y_hi, x = fsdp // 4, fsdp % 4
    y = y_hi * 2 + y_lo
    where = jnp.stack([x, y, z, core]).astype(jnp.int32)
    half, part = width // 2, width // 4
    rows = out_weight.shape[0]
    gain = norm_gain[None, :]

    columns = [part_columns for _, part_columns, _ in parts_of(half)]
    rode = users_here * (width // columns[2])
    travel = pl.pallas_call(
        pack_kernel,
        out_shape=(
            shaped((rows, columns[0]), BF16),
            shaped((rows, columns[1]), BF16),
            shaped((rows + rode, columns[2]), BF16),
        ),
        in_specs=[ANY] * 2,
        out_specs=(VMEM,) * 3,
        scratch_shapes=[
            pltpu.VMEM((users_here, width), BF16),
            pltpu.SemaphoreType.DMA((4,)),
        ],
        compiler_params=params(6),
        name="pack",
    )(out_weight, user_vectors)
    steps = ((swap_y, 3), (swap_x, 1), (swap_x, 3))
    for step in range(2):
        turns = [steps[step], steps[step + 1], steps[(step + 2) % 3]]
        travel = [jnp.concatenate([v, swap(v, n)], axis=0) for v, (swap, n) in zip(travel, turns)]
        travel = lax.optimization_barrier(travel)
    arrived = [swap_x(travel[0], 3), swap_y(travel[1], 3), swap_x(travel[2], 1)]
    held = pl.pallas_call(
        hold_kernel,
        out_shape=shaped((tokens, width), BF16),
        in_specs=[HBM],
        out_specs=VMEM,
        scratch_shapes=[pltpu.SemaphoreType.DMA],
        compiler_params=params(6),
        name="hold",
    )(residual)
    arrived, held = lax.optimization_barrier((arrived, held))
    pieces = [piece for both in zip(travel, arrived) for piece in both]
    pieces = pieces + [swap_core(p) for p in pieces]
    ints, filled = 0, 0
    numbers = (where, lengths, item_ids, item_counts, positive)
    count = sum(v.shape[0] for v in numbers)
    for v in numbers:
        ints = ints + jnp.pad(v, (filled, count - filled - v.shape[0]))
        filled += v.shape[0]

    stream, inverse, pooled, emb = pl.pallas_call(
        functools.partial(forward_kernel, items_here),
        out_shape=(
            shaped((tokens, width)),
            shaped((tokens, 1)),
            shaped((items_here, width)),
            shaped((items_here, width + LABELS), BF16),
        ),
        in_specs=[SMEM] + [VMEM] * 15,
        out_specs=(VMEM,) * 4,
        compiler_params=params(16),
        name="forward",
    )(ints, context, held, gain, *pieces)

    emb = lax.optimization_barrier(jnp.concatenate(four(emb, swap_x), axis=0))
    peer_context = swap_core(after(context, emb))
    riding = pieces[4:6] + pieces[10:12]
    users = pl.pallas_call(
        functools.partial(users_kernel, users_here, rows),
        out_shape=shaped((16 * users_here, width), BF16),
        in_specs=[SMEM] + [ANY] * 4,
        out_specs=VMEM,
        scratch_shapes=[
            pltpu.VMEM((16 * rode, columns[2]), BF16),
            pltpu.SemaphoreType.DMA((16,)),
        ],
        compiler_params=params(10),
        name="users",
    )(where, *riding)
    emb, users = lax.optimization_barrier((jnp.concatenate(four(emb, swap_y), axis=0), users))
    emb_pieces = four(emb, swap_z)
    emb_pieces = emb_pieces + [swap_core(p) for p in emb_pieces]

    items, people = 128 * items_here, 16 * users_here
    *sums, user_grad = pl.pallas_call(
        functools.partial(loss_kernel, users_here, items_here),
        out_shape=(shaped((8, width)),) * 4 + (shaped((users_here, width), BF16),),
        in_specs=[SMEM] + [VMEM] * 10,
        out_specs=(VMEM,) * 5,
        scratch_shapes=[
            pltpu.VMEM((people, items), F32),
            pltpu.VMEM((items, width), F32),
        ],
        compiler_params=params(18),
        name="loss",
    )(where, gain, users, *emb_pieces)
    sums = [sums[0]] + [swap_z(sums[q], OFFSETS[q]) for q in (1, 2, 3)]
    sums = (sums[0] + sums[1]) + (sums[2] + sums[3])

    residual_grad, keep, send, gain_grad, loss = pl.pallas_call(
        functools.partial(residual_kernel, 8 * people),
        out_shape=(
            shaped((tokens, width), BF16),
            shaped((tokens, half), BF16),
            shaped((tokens, half), BF16),
            shaped((1, width)),
            shaped((1, 1)),
        ),
        in_specs=[SMEM, SMEM] + [VMEM] * 6,
        out_specs=(VMEM,) * 5,
        compiler_params=params(16),
        name="residual",
    )(where, lengths, stream, inverse, pooled, gain, sums, swap_y(sums, 1))
    peer_grad = swap_core(send)
    context_grad = pl.pallas_call(
        context_kernel,
        out_shape=shaped((tokens, head), BF16),
        in_specs=[SMEM] + [VMEM] * 14,
        out_specs=VMEM,
        compiler_params=params(14),
        name="context",
    )(where, keep, send, *pieces)

    def blocks(first_blocks, second_blocks, heights, dtype, operands, name):
        return pl.pallas_call(
            functools.partial(blocks_kernel, first_blocks, second_blocks),
            out_shape=tuple(shaped((height * rows, half // 2), dtype) for height in heights),
            in_specs=[SMEM] + [VMEM] * 4,
            out_specs=(VMEM,) * len(heights),
            compiler_params=params(14),
            name=name,
        )(where, *operands)

    def with_ry(ry):
        return [(q, ry) for q in range(4)]

    def with_q(*places):
        return [(q, ry) for q in places for ry in range(2)]

    operands = (context, peer_context, keep, peer_grad)
    (first_sent,) = blocks(with_ry(1), [], (4,), BF16, operands, "first_sent")
    first_sent, peer_grad = lax.optimization_barrier((first_sent, peer_grad))
    operands = (context, peer_context, keep, peer_grad)
    second_sent = blocks([], with_q(1, 2, 3), (2, 2, 2), BF16, operands, "second_sent")
    first, second = blocks(with_ry(0), with_q(0), (4, 2), F32, operands, "kept")
    arrived = [swap_y(first_sent, 3)] + [swap_x(second_sent[q - 1], OFFSETS[q]) for q in (1, 2, 3)]
    arrived, first, second, context_grad = lax.optimization_barrier(
        (arrived, first, second, context_grad)
    )
    first = first + arrived[0].astype(F32)
    for piece in arrived[1:]:
        second = second + piece.astype(F32)
    arrived = [swap_x(first[q * rows : (q + 1) * rows].astype(BF16), OFFSETS[q]) for q in (1, 2, 3)]
    second = folded(second, swap_y, 3)
    first = first[:rows]
    for piece in arrived:
        first = first + piece.astype(F32)
    first = all_added(first, swap_y, 1)
    second = all_added(second, swap_z, 1)
    first = all_added(first, swap_z, 1)
    second = all_added(second, swap_z, 3)
    first = all_added(first, swap_z, 3)
    second = all_added(second, swap_y, 1)
    own = jnp.concatenate([first, second], axis=1).astype(BF16)
    other = swap_core(own)
    weight_grad = jnp.where(
        core == 0, jnp.concatenate([own, other], axis=1), jnp.concatenate([other, own], axis=1)
    )
    return (loss[0, 0], residual_grad, context_grad, weight_grad, gain_grad[0], user_grad)


def solution(mesh):
    placed = (
        P(AXES, None),
        P(AXES, None),
        P("fsdp", None),
        P(),
        P(AXES, None),
        P(AXES),
        P(AXES),
        P(AXES),
        P(AXES),
    )
    return jax.shard_map(
        on_device,
        mesh=mesh,
        in_specs=placed,
        out_specs=(P(), P(AXES, None), P(AXES, None), P("fsdp", None), P(), P(AXES, None)),
        check_vma=False,
    )
```

```python
import functools

import jax
import jax.numpy as jnp
from jax import lax
from jax.experimental import pallas as pl
from jax.experimental.pallas import tpu as pltpu
from jax.sharding import PartitionSpec as P

EPSILON = 1e-06
MASKED_FILL = -1e30
AXES = ("dp", "fsdp")
F32 = jnp.float32
BF16 = jnp.bfloat16
VMEM = pl.BlockSpec(memory_space=pltpu.VMEM)
SMEM = pl.BlockSpec(memory_space=pltpu.SMEM)
HBM = pl.BlockSpec(memory_space=pltpu.HBM)
ANY = pl.BlockSpec(memory_space=pl.ANY)


def params(mebibytes):
    return pltpu.CompilerParams(vmem_limit_bytes=mebibytes * 1024 * 1024)


def after(value, other):
    return lax.optimization_barrier((value, other))[0]

LABELS = 128
POSITIVE = 8
OFFSETS = (0, 1, 3, 2)


def linear(x, y, z, c):
    return ((((y % 2) * 4 + z) * 2 + c) * 2 + y // 2) * 4 + x


def move(value, where):
    perm = []
    for x in range(4):
        for y in range(4):
            for z in range(4):
                for c in range(2):
                    perm.append((linear(x, y, z, c), linear(*where(x, y, z, c))))
    return lax.ppermute(value, AXES, perm)


def swap_core(value):
    return move(value, lambda x, y, z, c: (x, y, z, 1 - c))


def swap_x(value, bits):
    return move(value, lambda x, y, z, c: (x ^ bits, y, z, c))


def swap_y(value, bits):
    return move(value, lambda x, y, z, c: (x, y ^ bits, z, c))


def swap_z(value, bits):
    return move(value, lambda x, y, z, c: (x, y, z ^ bits, c))


def four(value, swap):
    return [value] + [swap(value, bits) for bits in OFFSETS[1:]]


def doubled(value, swap, bits):
    return lax.optimization_barrier(jnp.concatenate([value, swap(value, bits)], axis=0))


def dot(left, right):
    return jnp.dot(left, right, preferred_element_type=F32)


def contract_rows(left, right):
    return lax.dot_general(left, right, (((0,), (0,)), ((), ())), preferred_element_type=F32)


def contract_last(left, right):
    return lax.dot_general(left, right, (((1,), (1,)), ((), ())), preferred_element_type=F32)


def parts_of(half):
    wide = half * 3 // 8
    pair = range(2)
    return (
        (0, wide, [[(r3 * 2 + r1, ry) for r1 in pair for ry in pair] for r3 in pair]),
        (wide, wide, [[(q, ry) for q in range(4)] for ry in pair]),
        (
            2 * wide,
            half - 2 * wide,
            [[(r3 * 2 + r1, ry) for ry in pair for r3 in pair] for r1 in pair],
        ),
    )


def block_home(x, y_hi, q, ry):
    return (y_hi ^ ry) * 4 + (x ^ OFFSETS[q])


def blocks_of(ref, where, pairs, block):
    picked = []
    for q, ry in pairs:
        home = block_home(where[0], where[1] // 2, q, ry)
        picked.append(ref[:, pl.ds(pl.multiple_of(home * block, block), block)])
    return jnp.concatenate(picked, axis=1)


def weight_rows(ref, block):
    rows = ref.shape[0] // 4
    if rows == block:
        return ref[...]
    return jnp.concatenate([ref[q * rows : q * rows + block, :] for q in range(4)], axis=0)


def pack_kernel(weight, users, first, second, third, held, sems):
    rows, width = weight.shape
    half = width // 2
    mine = (lax.axis_index("dp") % 2) * half
    copies = [pltpu.make_async_copy(users, held, sems.at[3])]
    for n, ((start, columns, _), out) in enumerate(zip(parts_of(half), (first, second, third))):
        at = pl.multiple_of(mine + start, 128)
        copies.append(
            pltpu.make_async_copy(
                weight.at[:, pl.ds(at, columns)], out.at[pl.ds(0, rows)], sems.at[n]
            )
        )
    for copy in copies:
        copy.start()
    for copy in copies:
        copy.wait()
    part = third.shape[1]
    wide = held[...].astype(F32)
    riding = [wide[:, j * part : (j + 1) * part] for j in range(width // part)]
    third[rows:, :] = jnp.concatenate(riding, axis=0).astype(BF16)


def forward_kernel(items, ints, context, residual, gain, *refs):
    stream, inverse, pooled, embedding = refs[12:]
    where = [ints[i] for i in range(4)]
    lengths, ids, counts = ([ints[4 + j * items + i] for i in range(items)] for j in range(3))
    positive = [ints[i] for i in range(4 + 3 * items, ints.shape[0])]
    tokens, width = residual.shape
    half = width // 2
    block = context.shape[1] // 8
    length = tokens // items
    for p, (start, columns, orders) in enumerate(parts_of(half)):
        lanes = [blocks_of(context, where, order, block) for order in orders]
        for side in range(2):
            base = where[3] * half if side == 0 else (1 - where[3]) * half
            stream[:, pl.ds(pl.multiple_of(base + start, 128), columns)] = sum(
                dot(lanes[k], weight_rows(refs[side * 6 + p * 2 + k], block)) for k in range(2)
            )
    for i in range(items):
        span = slice(i * length, (i + 1) * length)
        rows = stream[span, :] + residual[span, :].astype(F32)
        stream[span, :] = rows
        inv = lax.rsqrt(jnp.mean(rows * rows, axis=-1, keepdims=True) + EPSILON)
        inverse[i * length : (i + 1) * length, :] = inv
        position = lax.broadcasted_iota(jnp.int32, (length, 1), 0)
        kept = jnp.where(position < lengths[i], inv, 0.0)
        total = jnp.sum(rows * kept, axis=0, keepdims=True)
        pooled[i : i + 1, :] = total * gain[...] / lengths[i].astype(F32)
    pool = pooled[...]
    scale = lax.rsqrt(jnp.mean(pool * pool, axis=-1, keepdims=True) + EPSILON)
    embedding[:, :width] = (pool * scale).astype(BF16)
    row = lax.broadcasted_iota(jnp.int32, (items, LABELS), 0)
    lane = lax.broadcasted_iota(jnp.int32, (items, LABELS), 1)
    labels = jnp.zeros((items, LABELS), jnp.int32)
    for i in range(items):
        for at, value in enumerate((ids[i], counts[i] // 128, counts[i] % 128)):
            labels = jnp.where((row == i) & (lane == at), value, labels)
    for u in range(len(positive)):
        labels = jnp.where((row == 0) & (lane == POSITIVE + u), positive[u], labels)
    embedding[:, width:] = labels.astype(F32).astype(BF16)


def bit(value, k):
    return (value >> k) & 1


def one_hot_turn(rows, home):
    to = lax.broadcasted_iota(jnp.int32, (rows, rows), 0)
    of = lax.broadcasted_iota(jnp.int32, (rows, rows), 1)
    return jnp.where(to == home(of), 1.0, 0.0).astype(BF16)


def hold_kernel(source, out, sem):
    copy = pltpu.make_async_copy(source, out, sem)
    copy.start()
    copy.wait()


def users_kernel(users_here, block, where, *refs):
    piece_refs, (out, riders, sems) = refs[:4], refs[4:]
    x, y, core = where[0], where[1], where[3]
    people, width = out.shape
    stride, part = piece_refs[0].shape[0] // 4, piece_refs[0].shape[1]
    parts = width // part
    rode = parts * users_here
    copies = []
    for n in range(4):
        for b in range(4):
            copies.append(
                pltpu.make_async_copy(
                    piece_refs[n].at[pl.ds(b * stride + block, rode)],
                    riders.at[pl.ds((n * 4 + b) * rode, rode)],
                    sems.at[n * 4 + b],
                )
            )
    for copy in copies:
        copy.start()
    for copy in copies:
        copy.wait()

    def user_home(s):
        one = s // users_here
        ac, ay = core ^ bit(one, 3), (y // 2) ^ bit(one, 1)
        ax = x ^ bit(one, 2) ^ (3 * bit(one, 0))
        return ((ac * 2 + ay) * 4 + ax) * users_here + s % users_here

    wide = riders[...].astype(F32)
    placed = jnp.concatenate(
        [
            jnp.concatenate(
                [
                    wide[n * rode + j * users_here : n * rode + (j + 1) * users_here, :]
                    for n in range(16)
                ],
                axis=0,
            )
            for j in range(parts)
        ],
        axis=1,
    ).astype(BF16)
    out[...] = dot(one_hot_turn(people, user_home), placed).astype(BF16)

def loss_kernel(users_here, items_here, where, gain, users_ref, *refs):
    emb_refs = refs[:8]
    sums, user_grad, grads, emb_grads = refs[8:12], *refs[12:]
    x, y, z, core = where[0], where[1], where[2], where[3]
    group, full = emb_refs[0].shape
    width = full - LABELS
    items = 8 * group
    people = users_ref.shape[0]

    def item_home(s):
        one = s // items_here
        ax = x ^ bit(one, 0) ^ (3 * bit(one, 1))
        ay = y ^ bit(one, 2) ^ (3 * bit(one, 3))
        az = z ^ bit(one, 4) ^ (3 * bit(one, 5))
        ac = core ^ bit(one, 6)
        return (((ac * 4 + az) * 4 + ay) * 4 + ax) * items_here + s % items_here

    placed = jnp.concatenate([ref[...] for ref in emb_refs], axis=0)
    turned = dot(one_hot_turn(items, item_home), placed).astype(BF16)
    emb, labels = turned[:, :width], turned[:, width:]
    users = users_ref[...]
    person = lax.broadcasted_iota(jnp.int32, (people, items), 0)
    at = lax.broadcasted_iota(jnp.int32, (people, items), 1)
    g = person // users_here
    g_y = jnp.where((g // 4) % 2 == y // 2, y, 3 - y)
    g_row = (((g // 8 * 4 + z) * 4 + g_y) * 4 + g % 4) * items_here
    positives = dot(jnp.where(at == g_row, 1.0, 0.0).astype(BF16), labels)
    lane = lax.broadcasted_iota(jnp.int32, (people, LABELS), 1)
    slot = lax.broadcasted_iota(jnp.int32, (people, LABELS), 0) % users_here
    positive = jnp.sum(jnp.where(lane == POSITIVE + slot, positives, 0.0), axis=1, keepdims=True)
    item_labels = contract_rows(labels, one_hot_turn(items, lambda s: s))
    ids = item_labels[0:1, :]
    log_counts = jnp.log(item_labels[1:2, :] * 128.0 + item_labels[2:3, :])
    item = lax.broadcasted_iota(jnp.int32, (1, items), 1)
    chip = item // items_here
    index = linear(chip % 4, (chip // 4) % 4, (chip // 16) % 4, chip // 64) * items_here
    index = (index + item % items_here).astype(F32)
    onehot = index == positive
    positive_id = jnp.sum(jnp.where(onehot, ids, 0.0), axis=1, keepdims=True)
    excluded = (ids == positive_id) & jnp.logical_not(onehot)
    scores = contract_last(users, emb)
    logits = jnp.where(excluded, MASKED_FILL, scores - log_counts)
    row_max = jnp.max(logits, axis=1, keepdims=True)
    weights = jnp.where(excluded, 0.0, jnp.exp(logits - row_max))
    row_total = jnp.sum(weights, axis=1, keepdims=True)
    picked = jnp.sum(jnp.where(onehot, logits, 0.0), axis=1, keepdims=True)
    losses = row_max + jnp.log(row_total) - picked
    grad = (weights / row_total - jnp.where(onehot, 1.0, 0.0)).astype(BF16)
    grads[...] = grad.astype(F32)
    all_grads = contract_rows(grad, users)
    emb_grads[...] = all_grads
    emb_float = emb.astype(F32)
    product = emb_float * all_grads
    mean = jnp.mean(product, axis=-1, keepdims=True)
    gain_sum = jnp.sum(product - emb_float * emb_float * mean, axis=0, keepdims=True)
    line = lax.broadcasted_iota(jnp.int32, (8 * items_here, 1), 0)
    loss = jnp.broadcast_to(jnp.sum(losses, axis=0, keepdims=True), (1, width))
    for q in range(4):
        az = z ^ OFFSETS[q]
        start = ((core * 4 + az) * 4 + (y // 2) * 2) * 4 * items_here
        rows = emb_grads[pl.ds(pl.multiple_of(start, 8 * items_here), 8 * items_here), :]
        for other in range(2):
            for i in range(items_here):
                chosen = line == (((y % 2) ^ other) * 4 + x) * items_here + i
                n = other * items_here + i
                sums[q][n : n + 1, :] = jnp.sum(
                    jnp.where(chosen, rows, 0.0), axis=0, keepdims=True
                )
        sums[q][2 * items_here : 2 * items_here + 1, :] = gain_sum
        sums[q][2 * items_here + 1 :, :] = jnp.broadcast_to(loss, (6 - 2 * items_here + 1, width))
    place = ((core * 2 + y // 2) * 4 + x) * users_here
    own = grads[pl.ds(pl.multiple_of(place, users_here), users_here), :]
    user_grad[...] = dot(own.astype(BF16), emb).astype(BF16)


def residual_kernel(people, where, lengths, stream, inverse, pooled, gain, *refs):
    own_sums, other_sums, residual_grad, keep, send, gain_grad, loss = refs
    tokens, width = stream.shape
    half = width // 2
    items = lengths.shape[0]
    length = tokens // items
    for i in range(items):
        mine = own_sums[i : i + 1, :] + other_sums[items + i : items + i + 1, :]
        pool = pooled[i : i + 1, :]
        scale = lax.rsqrt(jnp.mean(pool * pool, axis=-1, keepdims=True) + EPSILON)
        pool_grad = scale * mine - pool * scale * scale * scale * jnp.mean(
            pool * mine, axis=-1, keepdims=True
        )
        row = gain[...] * pool_grad / lengths[i].astype(F32)
        span = slice(i * length, (i + 1) * length)
        rows = stream[span, :]
        inv = inverse[span, :]
        position = lax.broadcasted_iota(jnp.int32, (length, 1), 0)
        kept = jnp.where(position < lengths[i], inv, 0.0)
        mean = jnp.mean(rows * row, axis=-1, keepdims=True)
        residual_grad[span, :] = (kept * row - rows * (kept * inv * inv * mean)).astype(BF16)
    keep[...] = residual_grad[:, pl.ds(pl.multiple_of(where[3] * half, half), half)]
    send[...] = residual_grad[:, pl.ds(pl.multiple_of((1 - where[3]) * half, half), half)]
    at = 2 * items
    gain_grad[...] = (own_sums[at : at + 1, :] + other_sums[at : at + 1, :]) / gain[...]
    at = at + 1
    loss[...] = (own_sums[at : at + 1, 0:1] + other_sums[at : at + 1, 0:1]) / people


def context_kernel(where, keep, send, *refs):
    context_grad = refs[12]
    half = keep.shape[1]
    block = context_grad.shape[1] // 8
    values = {}
    for p, (start, columns, orders) in enumerate(parts_of(half)):
        for k, order in enumerate(orders):
            product = sum(
                contract_last(
                    grad[:, start : start + columns], weight_rows(refs[side * 6 + p * 2 + k], block)
                )
                for side, grad in enumerate((keep, send))
            )
            for b, place in enumerate(order):
                piece = product[:, b * block : (b + 1) * block]
                values[place] = values[place] + piece if place in values else piece
    for (q, ry), value in values.items():
        home = block_home(where[0], where[1] // 2, q, ry)
        context_grad[:, pl.ds(pl.multiple_of(home * block, block), block)] = value.astype(BF16)


def blocks_kernel(
    split, first_blocks, second_blocks, where, own_context, peer_context, own_grad, peer_grad, *outs
):
    half = own_grad.shape[1]
    block = own_context.shape[1] // 8
    outs = list(outs)
    for start, stop, blocks in ((0, split, first_blocks), (split, half, second_blocks)):
        if not blocks:
            continue
        value = contract_rows(
            blocks_of(own_context, where, blocks, block), own_grad[:, start:stop]
        ) + contract_rows(blocks_of(peer_context, where, blocks, block), peer_grad[:, start:stop])
        done = 0
        while done < value.shape[0]:
            out = outs.pop(0)
            out[...] = value[done : done + out.shape[0]].astype(out.dtype)
            done += out.shape[0]


def shaped(shape, dtype=F32):
    return jax.ShapeDtypeStruct(shape, dtype)


def added(kept, sent, swap, bits):
    return kept + swap(sent.astype(BF16), bits).astype(F32)


def folded(value, swap, bits):
    rows = value.shape[0] // 2
    return added(value[:rows], value[rows:], swap, bits)


def all_added(value, swap, bits):
    value = lax.reduce_precision(value, 8, 7)
    return added(value, value, swap, bits)


def on_device(
    context, residual, out_weight, norm_gain, user_vectors, positive, item_ids, item_counts, lengths
):
    tokens, head = context.shape
    width = residual.shape[1]
    items_here = lengths.shape[0]
    users_here = user_vectors.shape[0]
    dp, fsdp = lax.axis_index("dp"), lax.axis_index("fsdp")
    y_lo, z, core = dp // 8, (dp // 2) % 4, dp % 2
    y_hi, x = fsdp // 4, fsdp % 4
    y = y_hi * 2 + y_lo
    where = jnp.stack([x, y, z, core]).astype(jnp.int32)
    half, part = width // 2, width // 4
    rows = out_weight.shape[0]
    gain = norm_gain[None, :]

    columns = [part_columns for _, part_columns, _ in parts_of(half)]
    rode = users_here * (width // columns[2])
    travel = pl.pallas_call(
        pack_kernel,
        out_shape=(
            shaped((rows, columns[0]), BF16),
            shaped((rows, columns[1]), BF16),
            shaped((rows + rode, columns[2]), BF16),
        ),
        in_specs=[ANY] * 2,
        out_specs=(VMEM,) * 3,
        scratch_shapes=[
            pltpu.VMEM((users_here, width), BF16),
            pltpu.SemaphoreType.DMA((4,)),
        ],
        compiler_params=params(6),
        name="pack",
    )(out_weight, user_vectors)
    steps = ((swap_y, 3), (swap_x, 1), (swap_x, 3))
    for step in range(2):
        turns = [steps[step], steps[step + 1], steps[(step + 2) % 3]]
        travel = [jnp.concatenate([v, swap(v, n)], axis=0) for v, (swap, n) in zip(travel, turns)]
        travel = lax.optimization_barrier(travel)
    arrived = [swap_x(travel[0], 3), swap_y(travel[1], 3), swap_x(travel[2], 1)]
    held = pl.pallas_call(
        hold_kernel,
        out_shape=shaped((tokens, width), BF16),
        in_specs=[HBM],
        out_specs=VMEM,
        scratch_shapes=[pltpu.SemaphoreType.DMA],
        compiler_params=params(6),
        name="hold",
    )(residual)
    arrived, held = lax.optimization_barrier((arrived, held))
    pieces = [piece for both in zip(travel, arrived) for piece in both]
    pieces = pieces + [swap_core(p) for p in pieces]
    ints, filled = 0, 0
    numbers = (where, lengths, item_ids, item_counts, positive)
    count = sum(v.shape[0] for v in numbers)
    for v in numbers:
        ints = ints + jnp.pad(v, (filled, count - filled - v.shape[0]))
        filled += v.shape[0]

    stream, inverse, pooled, emb = pl.pallas_call(
        functools.partial(forward_kernel, items_here),
        out_shape=(
            shaped((tokens, width)),
            shaped((tokens, 1)),
            shaped((items_here, width)),
            shaped((items_here, width + LABELS), BF16),
        ),
        in_specs=[SMEM] + [VMEM] * 15,
        out_specs=(VMEM,) * 4,
        compiler_params=params(16),
        name="forward",
    )(ints, context, held, gain, *pieces)

    emb = lax.optimization_barrier(jnp.concatenate(four(emb, swap_x), axis=0))
    peer_context = swap_core(after(context, emb))
    riding = pieces[4:6] + pieces[10:12]
    users = pl.pallas_call(
        functools.partial(users_kernel, users_here, rows),
        out_shape=shaped((16 * users_here, width), BF16),
        in_specs=[SMEM] + [ANY] * 4,
        out_specs=VMEM,
        scratch_shapes=[
            pltpu.VMEM((16 * rode, columns[2]), BF16),
            pltpu.SemaphoreType.DMA((16,)),
        ],
        compiler_params=params(10),
        name="users",
    )(where, *riding)
    emb, users = lax.optimization_barrier((jnp.concatenate(four(emb, swap_y), axis=0), users))
    emb_pieces = four(emb, swap_z)
    emb_pieces = emb_pieces + [swap_core(p) for p in emb_pieces]

    items, people = 128 * items_here, 16 * users_here
    *sums, user_grad = pl.pallas_call(
        functools.partial(loss_kernel, users_here, items_here),
        out_shape=(shaped((8, width)),) * 4 + (shaped((users_here, width), BF16),),
        in_specs=[SMEM] + [VMEM] * 10,
        out_specs=(VMEM,) * 5,
        scratch_shapes=[
            pltpu.VMEM((people, items), F32),
            pltpu.VMEM((items, width), F32),
        ],
        compiler_params=params(18),
        name="loss",
    )(where, gain, users, *emb_pieces)
    sums = [sums[0]] + [swap_z(sums[q], OFFSETS[q]) for q in (1, 2, 3)]
    sums = (sums[0] + sums[1]) + (sums[2] + sums[3])

    residual_grad, keep, send, gain_grad, loss = pl.pallas_call(
        functools.partial(residual_kernel, 8 * people),
        out_shape=(
            shaped((tokens, width), BF16),
            shaped((tokens, half), BF16),
            shaped((tokens, half), BF16),
            shaped((1, width)),
            shaped((1, 1)),
        ),
        in_specs=[SMEM, SMEM] + [VMEM] * 6,
        out_specs=(VMEM,) * 5,
        compiler_params=params(16),
        name="residual",
    )(where, lengths, stream, inverse, pooled, gain, sums, swap_y(sums, 1))
    peer_grad = swap_core(send)
    context_grad = pl.pallas_call(
        context_kernel,
        out_shape=shaped((tokens, head), BF16),
        in_specs=[SMEM] + [VMEM] * 14,
        out_specs=VMEM,
        compiler_params=params(14),
        name="context",
    )(where, keep, send, *pieces)

    split = half * 5 // 8
    first_width, second_width = split, half - split

    def blocks(first_blocks, second_blocks, sizes, dtype, operands, name):
        return pl.pallas_call(
            functools.partial(blocks_kernel, split, first_blocks, second_blocks),
            out_shape=tuple(shaped((height * rows, across), dtype) for height, across in sizes),
            in_specs=[SMEM] + [VMEM] * 4,
            out_specs=(VMEM,) * len(sizes),
            compiler_params=params(14),
            name=name,
        )(where, *operands)

    def with_ry(ry):
        return [(q, ry) for q in range(4)]

    def with_q(*places):
        return [(q, ry) for q in places for ry in range(2)]

    operands = (context, peer_context, keep, peer_grad)
    (first_sent,) = blocks(with_ry(1), [], [(4, first_width)], BF16, operands, "first_sent")
    first_sent, peer_grad = lax.optimization_barrier((first_sent, peer_grad))
    operands = (context, peer_context, keep, peer_grad)
    second_sent = blocks(
        [], with_q(1, 2, 3), [(2, second_width)] * 3, BF16, operands, "second_sent"
    )
    first, second = blocks(
        with_ry(0), with_q(0), [(4, first_width), (2, second_width)], F32, operands, "kept"
    )
    arrived = [swap_y(first_sent, 3)] + [swap_x(second_sent[q - 1], OFFSETS[q]) for q in (1, 2, 3)]
    arrived, first, second, context_grad = lax.optimization_barrier(
        (arrived, first, second, context_grad)
    )
    first = first + arrived[0].astype(F32)
    for piece in arrived[1:]:
        second = second + piece.astype(F32)
    arrived = [swap_x(first[q * rows : (q + 1) * rows].astype(BF16), OFFSETS[q]) for q in (1, 2, 3)]
    second = folded(second, swap_y, 3)
    first = first[:rows]
    for piece in arrived:
        first = first + piece.astype(F32)
    second = jnp.concatenate([first[:, half // 2 :], second], axis=1)
    first = first[:, : half // 2]
    first = all_added(first, swap_y, 1)
    second = all_added(second, swap_z, 1)
    first = all_added(first, swap_z, 1)
    second = all_added(second, swap_z, 3)
    first = all_added(first, swap_z, 3)
    second = all_added(second, swap_y, 1)
    own = jnp.concatenate([first, second], axis=1).astype(BF16)
    other = swap_core(own)
    weight_grad = jnp.where(
        core == 0, jnp.concatenate([own, other], axis=1), jnp.concatenate([other, own], axis=1)
    )
    return (loss[0, 0], residual_grad, context_grad, weight_grad, gain_grad[0], user_grad)


def solution(mesh):
    placed = (
        P(AXES, None),
        P(AXES, None),
        P("fsdp", None),
        P(),
        P(AXES, None),
        P(AXES),
        P(AXES),
        P(AXES),
        P(AXES),
    )
    return jax.shard_map(
        on_device,
        mesh=mesh,
        in_specs=placed,
        out_specs=(P(), P(AXES, None), P(AXES, None), P("fsdp", None), P(), P(AXES, None)),
        check_vma=False,
    )
```

```python
import functools

import jax
import jax.numpy as jnp
from jax import lax
from jax.experimental import pallas as pl
from jax.experimental.pallas import tpu as pltpu
from jax.sharding import PartitionSpec as P

EPSILON = 1e-06
MASKED_FILL = -1e30
AXES = ("dp", "fsdp")
F32 = jnp.float32
BF16 = jnp.bfloat16
VMEM = pl.BlockSpec(memory_space=pltpu.VMEM)
SMEM = pl.BlockSpec(memory_space=pltpu.SMEM)
HBM = pl.BlockSpec(memory_space=pltpu.HBM)
ANY = pl.BlockSpec(memory_space=pl.ANY)


def params(mebibytes):
    return pltpu.CompilerParams(vmem_limit_bytes=mebibytes * 1024 * 1024)


def after(value, other):
    return lax.optimization_barrier((value, other))[0]

LABELS = 128
POSITIVE = 8
OFFSETS = (0, 1, 3, 2)


def linear(x, y, z, c):
    return ((((y % 2) * 4 + z) * 2 + c) * 2 + y // 2) * 4 + x


def move(value, where):
    perm = []
    for x in range(4):
        for y in range(4):
            for z in range(4):
                for c in range(2):
                    perm.append((linear(x, y, z, c), linear(*where(x, y, z, c))))
    return lax.ppermute(value, AXES, perm)


def swap_core(value):
    return move(value, lambda x, y, z, c: (x, y, z, 1 - c))


def swap_x(value, bits):
    return move(value, lambda x, y, z, c: (x ^ bits, y, z, c))


def swap_y(value, bits):
    return move(value, lambda x, y, z, c: (x, y ^ bits, z, c))


def swap_z(value, bits):
    return move(value, lambda x, y, z, c: (x, y, z ^ bits, c))


def four(value, swap):
    return [value] + [swap(value, bits) for bits in OFFSETS[1:]]


def doubled(value, swap, bits):
    return lax.optimization_barrier(jnp.concatenate([value, swap(value, bits)], axis=0))


def dot(left, right):
    return jnp.dot(left, right, preferred_element_type=F32)


def contract_rows(left, right):
    return lax.dot_general(left, right, (((0,), (0,)), ((), ())), preferred_element_type=F32)


def contract_last(left, right):
    return lax.dot_general(left, right, (((1,), (1,)), ((), ())), preferred_element_type=F32)


def parts_of(half):
    wide = half * 3 // 8
    pair = range(2)
    return (
        (0, wide, [[(r3 * 2 + r1, ry) for r1 in pair for ry in pair] for r3 in pair]),
        (wide, wide, [[(q, ry) for q in range(4)] for ry in pair]),
        (
            2 * wide,
            half - 2 * wide,
            [[(r3 * 2 + r1, ry) for ry in pair for r3 in pair] for r1 in pair],
        ),
    )


def block_home(x, y_hi, q, ry):
    return (y_hi ^ ry) * 4 + (x ^ OFFSETS[q])


def blocks_of(ref, where, pairs, block):
    picked = []
    for q, ry in pairs:
        home = block_home(where[0], where[1] // 2, q, ry)
        picked.append(ref[:, pl.ds(pl.multiple_of(home * block, block), block)])
    return jnp.concatenate(picked, axis=1)


def weight_rows(ref, block):
    rows = ref.shape[0] // 4
    if rows == block:
        return ref[...]
    return jnp.concatenate([ref[q * rows : q * rows + block, :] for q in range(4)], axis=0)


def pack_kernel(weight, users, first, second, third, held, sems):
    rows, width = weight.shape
    half = width // 2
    mine = (lax.axis_index("dp") % 2) * half
    copies = [pltpu.make_async_copy(users, held, sems.at[3])]
    for n, ((start, columns, _), out) in enumerate(zip(parts_of(half), (first, second, third))):
        at = pl.multiple_of(mine + start, 128)
        copies.append(
            pltpu.make_async_copy(
                weight.at[:, pl.ds(at, columns)], out.at[pl.ds(0, rows)], sems.at[n]
            )
        )
    for copy in copies:
        copy.start()
    for copy in copies:
        copy.wait()
    part = third.shape[1]
    wide = held[...].astype(F32)
    riding = [wide[:, j * part : (j + 1) * part] for j in range(width // part)]
    third[rows:, :] = jnp.concatenate(riding, axis=0).astype(BF16)


def forward_kernel(items, ints, context, residual, gain, *refs):
    stream, inverse, pooled, embedding = refs[12:]
    where = [ints[i] for i in range(4)]
    lengths, ids, counts = ([ints[4 + j * items + i] for i in range(items)] for j in range(3))
    positive = [ints[i] for i in range(4 + 3 * items, ints.shape[0])]
    tokens, width = residual.shape
    half = width // 2
    block = context.shape[1] // 8
    length = tokens // items
    for p, (start, columns, orders) in enumerate(parts_of(half)):
        lanes = [blocks_of(context, where, order, block) for order in orders]
        for side in range(2):
            base = where[3] * half if side == 0 else (1 - where[3]) * half
            stream[:, pl.ds(pl.multiple_of(base + start, 128), columns)] = sum(
                dot(lanes[k], weight_rows(refs[side * 6 + p * 2 + k], block)) for k in range(2)
            )
    for i in range(items):
        span = slice(i * length, (i + 1) * length)
        rows = stream[span, :] + residual[span, :].astype(F32)
        stream[span, :] = rows
        inv = lax.rsqrt(jnp.mean(rows * rows, axis=-1, keepdims=True) + EPSILON)
        inverse[i * length : (i + 1) * length, :] = inv
        position = lax.broadcasted_iota(jnp.int32, (length, 1), 0)
        kept = jnp.where(position < lengths[i], inv, 0.0)
        total = jnp.sum(rows * kept, axis=0, keepdims=True)
        pooled[i : i + 1, :] = total * gain[...] / lengths[i].astype(F32)
    pool = pooled[...]
    scale = lax.rsqrt(jnp.mean(pool * pool, axis=-1, keepdims=True) + EPSILON)
    embedding[:, :width] = (pool * scale).astype(BF16)
    row = lax.broadcasted_iota(jnp.int32, (items, LABELS), 0)
    lane = lax.broadcasted_iota(jnp.int32, (items, LABELS), 1)
    labels = jnp.zeros((items, LABELS), jnp.int32)
    for i in range(items):
        for at, value in enumerate((ids[i], counts[i] // 128, counts[i] % 128)):
            labels = jnp.where((row == i) & (lane == at), value, labels)
    for u in range(len(positive)):
        labels = jnp.where((row == 0) & (lane == POSITIVE + u), positive[u], labels)
    embedding[:, width:] = labels.astype(F32).astype(BF16)


def bit(value, k):
    return (value >> k) & 1


def one_hot_turn(rows, home):
    to = lax.broadcasted_iota(jnp.int32, (rows, rows), 0)
    of = lax.broadcasted_iota(jnp.int32, (rows, rows), 1)
    return jnp.where(to == home(of), 1.0, 0.0).astype(BF16)


def hold_kernel(source, out, sem):
    copy = pltpu.make_async_copy(source, out, sem)
    copy.start()
    copy.wait()


def users_kernel(users_here, block, where, *refs):
    piece_refs, (out, riders, sems) = refs[:4], refs[4:]
    x, y, core = where[0], where[1], where[3]
    people, width = out.shape
    stride, part = piece_refs[0].shape[0] // 4, piece_refs[0].shape[1]
    parts = width // part
    rode = parts * users_here
    copies = []
    for n in range(4):
        for b in range(4):
            copies.append(
                pltpu.make_async_copy(
                    piece_refs[n].at[pl.ds(b * stride + block, rode)],
                    riders.at[pl.ds((n * 4 + b) * rode, rode)],
                    sems.at[n * 4 + b],
                )
            )
    for copy in copies:
        copy.start()
    for copy in copies:
        copy.wait()

    def user_home(s):
        one = s // users_here
        ac, ay = core ^ bit(one, 3), (y // 2) ^ bit(one, 1)
        ax = x ^ bit(one, 2) ^ (3 * bit(one, 0))
        return ((ac * 2 + ay) * 4 + ax) * users_here + s % users_here

    wide = riders[...].astype(F32)
    placed = jnp.concatenate(
        [
            jnp.concatenate(
                [
                    wide[n * rode + j * users_here : n * rode + (j + 1) * users_here, :]
                    for n in range(16)
                ],
                axis=0,
            )
            for j in range(parts)
        ],
        axis=1,
    ).astype(BF16)
    out[...] = dot(one_hot_turn(people, user_home), placed).astype(BF16)

def loss_kernel(users_here, items_here, where, gain, users_ref, *refs):
    emb_refs = refs[:8]
    sums, user_grad, grads, emb_grads = refs[8:12], *refs[12:]
    x, y, z, core = where[0], where[1], where[2], where[3]
    group, full = emb_refs[0].shape
    width = full - LABELS
    items = 8 * group
    people = users_ref.shape[0]

    def item_home(s):
        one = s // items_here
        ax = x ^ bit(one, 0) ^ (3 * bit(one, 1))
        ay = y ^ bit(one, 2) ^ (3 * bit(one, 3))
        az = z ^ bit(one, 4) ^ (3 * bit(one, 5))
        ac = core ^ bit(one, 6)
        return (((ac * 4 + az) * 4 + ay) * 4 + ax) * items_here + s % items_here

    placed = jnp.concatenate([ref[...] for ref in emb_refs], axis=0)
    turned = dot(one_hot_turn(items, item_home), placed).astype(BF16)
    emb, labels = turned[:, :width], turned[:, width:]
    users = users_ref[...]
    person = lax.broadcasted_iota(jnp.int32, (people, items), 0)
    at = lax.broadcasted_iota(jnp.int32, (people, items), 1)
    g = person // users_here
    g_y = jnp.where((g // 4) % 2 == y // 2, y, 3 - y)
    g_row = (((g // 8 * 4 + z) * 4 + g_y) * 4 + g % 4) * items_here
    positives = dot(jnp.where(at == g_row, 1.0, 0.0).astype(BF16), labels)
    lane = lax.broadcasted_iota(jnp.int32, (people, LABELS), 1)
    slot = lax.broadcasted_iota(jnp.int32, (people, LABELS), 0) % users_here
    positive = jnp.sum(jnp.where(lane == POSITIVE + slot, positives, 0.0), axis=1, keepdims=True)
    item_labels = contract_rows(labels, one_hot_turn(items, lambda s: s))
    ids = item_labels[0:1, :]
    log_counts = jnp.log(item_labels[1:2, :] * 128.0 + item_labels[2:3, :])
    item = lax.broadcasted_iota(jnp.int32, (1, items), 1)
    chip = item // items_here
    index = linear(chip % 4, (chip // 4) % 4, (chip // 16) % 4, chip // 64) * items_here
    index = (index + item % items_here).astype(F32)
    onehot = index == positive
    positive_id = jnp.sum(jnp.where(onehot, ids, 0.0), axis=1, keepdims=True)
    excluded = (ids == positive_id) & jnp.logical_not(onehot)
    scores = contract_last(users, emb)
    logits = jnp.where(excluded, MASKED_FILL, scores - log_counts)
    row_max = jnp.max(logits, axis=1, keepdims=True)
    weights = jnp.where(excluded, 0.0, jnp.exp(logits - row_max))
    row_total = jnp.sum(weights, axis=1, keepdims=True)
    picked = jnp.sum(jnp.where(onehot, logits, 0.0), axis=1, keepdims=True)
    losses = row_max + jnp.log(row_total) - picked
    grad = (weights / row_total - jnp.where(onehot, 1.0, 0.0)).astype(BF16)
    grads[...] = grad.astype(F32)
    all_grads = contract_rows(grad, users)
    emb_grads[...] = all_grads
    emb_float = emb.astype(F32)
    product = emb_float * all_grads
    mean = jnp.mean(product, axis=-1, keepdims=True)
    gain_sum = jnp.sum(product - emb_float * emb_float * mean, axis=0, keepdims=True)
    line = lax.broadcasted_iota(jnp.int32, (8 * items_here, 1), 0)
    loss = jnp.broadcast_to(jnp.sum(losses, axis=0, keepdims=True), (1, width))
    for q in range(4):
        az = z ^ OFFSETS[q]
        start = ((core * 4 + az) * 4 + (y // 2) * 2) * 4 * items_here
        rows = emb_grads[pl.ds(pl.multiple_of(start, 8 * items_here), 8 * items_here), :]
        for other in range(2):
            for i in range(items_here):
                chosen = line == (((y % 2) ^ other) * 4 + x) * items_here + i
                n = other * items_here + i
                sums[q][n : n + 1, :] = jnp.sum(
                    jnp.where(chosen, rows, 0.0), axis=0, keepdims=True
                )
        sums[q][2 * items_here : 2 * items_here + 1, :] = gain_sum
        sums[q][2 * items_here + 1 :, :] = jnp.broadcast_to(loss, (6 - 2 * items_here + 1, width))
    place = ((core * 2 + y // 2) * 4 + x) * users_here
    own = grads[pl.ds(pl.multiple_of(place, users_here), users_here), :]
    user_grad[...] = dot(own.astype(BF16), emb).astype(BF16)


def residual_kernel(people, where, lengths, stream, inverse, pooled, gain, *refs):
    own_sums, other_sums, residual_grad, keep, send, gain_grad, loss = refs
    tokens, width = stream.shape
    half = width // 2
    items = lengths.shape[0]
    length = tokens // items
    for i in range(items):
        mine = own_sums[i : i + 1, :] + other_sums[items + i : items + i + 1, :]
        pool = pooled[i : i + 1, :]
        scale = lax.rsqrt(jnp.mean(pool * pool, axis=-1, keepdims=True) + EPSILON)
        pool_grad = scale * mine - pool * scale * scale * scale * jnp.mean(
            pool * mine, axis=-1, keepdims=True
        )
        row = gain[...] * pool_grad / lengths[i].astype(F32)
        span = slice(i * length, (i + 1) * length)
        rows = stream[span, :]
        inv = inverse[span, :]
        position = lax.broadcasted_iota(jnp.int32, (length, 1), 0)
        kept = jnp.where(position < lengths[i], inv, 0.0)
        mean = jnp.mean(rows * row, axis=-1, keepdims=True)
        residual_grad[span, :] = (kept * row - rows * (kept * inv * inv * mean)).astype(BF16)
    keep[...] = residual_grad[:, pl.ds(pl.multiple_of(where[3] * half, half), half)]
    send[...] = residual_grad[:, pl.ds(pl.multiple_of((1 - where[3]) * half, half), half)]
    at = 2 * items
    gain_grad[...] = (own_sums[at : at + 1, :] + other_sums[at : at + 1, :]) / gain[...]
    at = at + 1
    loss[...] = (own_sums[at : at + 1, 0:1] + other_sums[at : at + 1, 0:1]) / people


def context_kernel(where, keep, send, *refs):
    context_grad = refs[12]
    half = keep.shape[1]
    block = context_grad.shape[1] // 8
    values = {}
    for p, (start, columns, orders) in enumerate(parts_of(half)):
        for k, order in enumerate(orders):
            product = sum(
                contract_last(
                    grad[:, start : start + columns], weight_rows(refs[side * 6 + p * 2 + k], block)
                )
                for side, grad in enumerate((keep, send))
            )
            for b, place in enumerate(order):
                piece = product[:, b * block : (b + 1) * block]
                values[place] = values[place] + piece if place in values else piece
    for (q, ry), value in values.items():
        home = block_home(where[0], where[1] // 2, q, ry)
        context_grad[:, pl.ds(pl.multiple_of(home * block, block), block)] = value.astype(BF16)


def blocks_kernel(first_blocks, second_blocks, where, own_context, peer_context, own_grad, peer_grad, *outs):
    part = own_grad.shape[1] // 2
    block = own_context.shape[1] // 8
    outs = list(outs)
    for at, blocks in ((0, first_blocks), (part, second_blocks)):
        if not blocks:
            continue
        value = contract_rows(
            blocks_of(own_context, where, blocks, block), own_grad[:, at : at + part]
        ) + contract_rows(blocks_of(peer_context, where, blocks, block), peer_grad[:, at : at + part])
        done = 0
        while done < value.shape[0]:
            out = outs.pop(0)
            out[...] = value[done : done + out.shape[0]].astype(out.dtype)
            done += out.shape[0]


def shaped(shape, dtype=F32):
    return jax.ShapeDtypeStruct(shape, dtype)


def added(kept, sent, swap, bits):
    return kept + swap(sent.astype(BF16), bits).astype(F32)


def folded(value, swap, bits):
    rows = value.shape[0] // 2
    return added(value[:rows], value[rows:], swap, bits)


def all_added(value, swap, bits):
    value = lax.reduce_precision(value, 8, 7)
    return added(value, value, swap, bits)


def on_device(
    context, residual, out_weight, norm_gain, user_vectors, positive, item_ids, item_counts, lengths
):
    tokens, head = context.shape
    width = residual.shape[1]
    items_here = lengths.shape[0]
    users_here = user_vectors.shape[0]
    dp, fsdp = lax.axis_index("dp"), lax.axis_index("fsdp")
    y_lo, z, core = dp // 8, (dp // 2) % 4, dp % 2
    y_hi, x = fsdp // 4, fsdp % 4
    y = y_hi * 2 + y_lo
    where = jnp.stack([x, y, z, core]).astype(jnp.int32)
    half, part = width // 2, width // 4
    rows = out_weight.shape[0]
    gain = norm_gain[None, :]

    columns = [part_columns for _, part_columns, _ in parts_of(half)]
    rode = users_here * (width // columns[2])
    travel = pl.pallas_call(
        pack_kernel,
        out_shape=(
            shaped((rows, columns[0]), BF16),
            shaped((rows, columns[1]), BF16),
            shaped((rows + rode, columns[2]), BF16),
        ),
        in_specs=[ANY] * 2,
        out_specs=(VMEM,) * 3,
        scratch_shapes=[
            pltpu.VMEM((users_here, width), BF16),
            pltpu.SemaphoreType.DMA((4,)),
        ],
        compiler_params=params(6),
        name="pack",
    )(out_weight, user_vectors)
    steps = ((swap_y, 3), (swap_x, 1), (swap_x, 3))
    for step in range(2):
        turns = [steps[step], steps[step + 1], steps[(step + 2) % 3]]
        travel = [jnp.concatenate([v, swap(v, n)], axis=0) for v, (swap, n) in zip(travel, turns)]
        travel = lax.optimization_barrier(travel)
    arrived = [swap_x(travel[0], 3), swap_y(travel[1], 3), swap_x(travel[2], 1)]
    held = pl.pallas_call(
        hold_kernel,
        out_shape=shaped((tokens, width), BF16),
        in_specs=[HBM],
        out_specs=VMEM,
        scratch_shapes=[pltpu.SemaphoreType.DMA],
        compiler_params=params(6),
        name="hold",
    )(residual)
    arrived, held = lax.optimization_barrier((arrived, held))
    pieces = [piece for both in zip(travel, arrived) for piece in both]
    pieces = pieces + [swap_core(p) for p in pieces]
    ints, filled = 0, 0
    numbers = (where, lengths, item_ids, item_counts, positive)
    count = sum(v.shape[0] for v in numbers)
    for v in numbers:
        ints = ints + jnp.pad(v, (filled, count - filled - v.shape[0]))
        filled += v.shape[0]

    stream, inverse, pooled, emb = pl.pallas_call(
        functools.partial(forward_kernel, items_here),
        out_shape=(
            shaped((tokens, width)),
            shaped((tokens, 1)),
            shaped((items_here, width)),
            shaped((items_here, width + LABELS), BF16),
        ),
        in_specs=[SMEM] + [VMEM] * 15,
        out_specs=(VMEM,) * 4,
        compiler_params=params(16),
        name="forward",
    )(ints, context, held, gain, *pieces)

    emb = lax.optimization_barrier(jnp.concatenate(four(emb, swap_x), axis=0))
    peer_context = swap_core(after(context, emb))
    riding = pieces[4:6] + pieces[10:12]
    users = pl.pallas_call(
        functools.partial(users_kernel, users_here, rows),
        out_shape=shaped((16 * users_here, width), BF16),
        in_specs=[SMEM] + [ANY] * 4,
        out_specs=VMEM,
        scratch_shapes=[
            pltpu.VMEM((16 * rode, columns[2]), BF16),
            pltpu.SemaphoreType.DMA((16,)),
        ],
        compiler_params=params(10),
        name="users",
    )(where, *riding)
    emb = lax.optimization_barrier(jnp.concatenate(four(emb, swap_y), axis=0))
    emb_pieces = four(emb, swap_z)
    arrived, users = lax.optimization_barrier((emb_pieces[1:], users))
    emb_pieces = emb_pieces[:1] + arrived
    emb_pieces = emb_pieces + [swap_core(p) for p in emb_pieces]

    items, people = 128 * items_here, 16 * users_here
    *sums, user_grad = pl.pallas_call(
        functools.partial(loss_kernel, users_here, items_here),
        out_shape=(shaped((8, width)),) * 4 + (shaped((users_here, width), BF16),),
        in_specs=[SMEM] + [VMEM] * 10,
        out_specs=(VMEM,) * 5,
        scratch_shapes=[
            pltpu.VMEM((people, items), F32),
            pltpu.VMEM((items, width), F32),
        ],
        compiler_params=params(18),
        name="loss",
    )(where, gain, users, *emb_pieces)
    sums = [sums[0]] + [swap_z(sums[q], OFFSETS[q]) for q in (1, 2, 3)]
    sums = (sums[0] + sums[1]) + (sums[2] + sums[3])

    residual_grad, keep, send, gain_grad, loss = pl.pallas_call(
        functools.partial(residual_kernel, 8 * people),
        out_shape=(
            shaped((tokens, width), BF16),
            shaped((tokens, half), BF16),
            shaped((tokens, half), BF16),
            shaped((1, width)),
            shaped((1, 1)),
        ),
        in_specs=[SMEM, SMEM] + [VMEM] * 6,
        out_specs=(VMEM,) * 5,
        compiler_params=params(16),
        name="residual",
    )(where, lengths, stream, inverse, pooled, gain, sums, swap_y(sums, 1))
    peer_grad = swap_core(send)
    context_grad = pl.pallas_call(
        context_kernel,
        out_shape=shaped((tokens, head), BF16),
        in_specs=[SMEM] + [VMEM] * 14,
        out_specs=VMEM,
        compiler_params=params(14),
        name="context",
    )(where, keep, send, *pieces)

    def blocks(first_blocks, second_blocks, heights, dtype, operands, name):
        return pl.pallas_call(
            functools.partial(blocks_kernel, first_blocks, second_blocks),
            out_shape=tuple(shaped((height * rows, half // 2), dtype) for height in heights),
            in_specs=[SMEM] + [VMEM] * 4,
            out_specs=(VMEM,) * len(heights),
            compiler_params=params(14),
            name=name,
        )(where, *operands)

    def with_ry(ry):
        return [(q, ry) for q in range(4)]

    def with_q(*places):
        return [(q, ry) for q in places for ry in range(2)]

    operands = (context, peer_context, keep, peer_grad)
    (first_sent,) = blocks(with_ry(1), [], (4,), BF16, operands, "first_sent")
    first_sent, peer_grad = lax.optimization_barrier((first_sent, peer_grad))
    operands = (context, peer_context, keep, peer_grad)
    second_sent = blocks([], with_q(1, 2, 3), (2, 2, 2), BF16, operands, "second_sent")
    first, second = blocks(with_ry(0), with_q(0), (4, 2), F32, operands, "kept")
    arrived = [swap_y(first_sent, 3)] + [swap_x(second_sent[q - 1], OFFSETS[q]) for q in (1, 2, 3)]
    arrived, first, second, context_grad = lax.optimization_barrier(
        (arrived, first, second, context_grad)
    )
    first = first + arrived[0].astype(F32)
    for piece in arrived[1:]:
        second = second + piece.astype(F32)
    arrived = [swap_x(first[q * rows : (q + 1) * rows].astype(BF16), OFFSETS[q]) for q in (1, 2, 3)]
    second = folded(second, swap_y, 3)
    first = first[:rows]
    for piece in arrived:
        first = first + piece.astype(F32)
    first = all_added(first, swap_y, 1)
    second = all_added(second, swap_z, 1)
    first = all_added(first, swap_z, 1)
    second = all_added(second, swap_z, 3)
    first = all_added(first, swap_z, 3)
    second = all_added(second, swap_y, 1)
    own = jnp.concatenate([first, second], axis=1).astype(BF16)
    other = swap_core(own)
    weight_grad = jnp.where(
        core == 0, jnp.concatenate([own, other], axis=1), jnp.concatenate([other, own], axis=1)
    )
    return (loss[0, 0], residual_grad, context_grad, weight_grad, gain_grad[0], user_grad)


def solution(mesh):
    placed = (
        P(AXES, None),
        P(AXES, None),
        P("fsdp", None),
        P(),
        P(AXES, None),
        P(AXES),
        P(AXES),
        P(AXES),
        P(AXES),
    )
    return jax.shard_map(
        on_device,
        mesh=mesh,
        in_specs=placed,
        out_specs=(P(), P(AXES, None), P(AXES, None), P("fsdp", None), P(), P(AXES, None)),
        check_vma=False,
    )
```

```python
import functools

import jax
import jax.numpy as jnp
from jax import lax
from jax.experimental import pallas as pl
from jax.experimental.pallas import tpu as pltpu
from jax.sharding import PartitionSpec as P

EPSILON = 1e-06
MASKED_FILL = -1e30
AXES = ("dp", "fsdp")
F32 = jnp.float32
BF16 = jnp.bfloat16
VMEM = pl.BlockSpec(memory_space=pltpu.VMEM)
SMEM = pl.BlockSpec(memory_space=pltpu.SMEM)
HBM = pl.BlockSpec(memory_space=pltpu.HBM)
ANY = pl.BlockSpec(memory_space=pl.ANY)


def params(mebibytes):
    return pltpu.CompilerParams(vmem_limit_bytes=mebibytes * 1024 * 1024)


def after(value, other):
    return lax.optimization_barrier((value, other))[0]

LABELS = 128
POSITIVE = 8
OFFSETS = (0, 1, 3, 2)


def linear(x, y, z, c):
    return ((((y % 2) * 4 + z) * 2 + c) * 2 + y // 2) * 4 + x


def move(value, where):
    perm = []
    for x in range(4):
        for y in range(4):
            for z in range(4):
                for c in range(2):
                    perm.append((linear(x, y, z, c), linear(*where(x, y, z, c))))
    return lax.ppermute(value, AXES, perm)


def swap_core(value):
    return move(value, lambda x, y, z, c: (x, y, z, 1 - c))


def swap_x(value, bits):
    return move(value, lambda x, y, z, c: (x ^ bits, y, z, c))


def swap_y(value, bits):
    return move(value, lambda x, y, z, c: (x, y ^ bits, z, c))


def swap_z(value, bits):
    return move(value, lambda x, y, z, c: (x, y, z ^ bits, c))


def four(value, swap):
    return [value] + [swap(value, bits) for bits in OFFSETS[1:]]


def doubled(value, swap, bits):
    return lax.optimization_barrier(jnp.concatenate([value, swap(value, bits)], axis=0))


def dot(left, right):
    return jnp.dot(left, right, preferred_element_type=F32)


def contract_rows(left, right):
    return lax.dot_general(left, right, (((0,), (0,)), ((), ())), preferred_element_type=F32)


def contract_last(left, right):
    return lax.dot_general(left, right, (((1,), (1,)), ((), ())), preferred_element_type=F32)


def parts_of(half):
    wide = half * 3 // 8
    pair = range(2)
    return (
        (0, wide, [[(r3 * 2 + r1, ry) for r1 in pair for ry in pair] for r3 in pair]),
        (wide, wide, [[(q, ry) for q in range(4)] for ry in pair]),
        (
            2 * wide,
            half - 2 * wide,
            [[(r3 * 2 + r1, ry) for ry in pair for r3 in pair] for r1 in pair],
        ),
    )


def block_home(x, y_hi, q, ry):
    return (y_hi ^ ry) * 4 + (x ^ OFFSETS[q])


def blocks_of(ref, where, pairs, block):
    picked = []
    for q, ry in pairs:
        home = block_home(where[0], where[1] // 2, q, ry)
        picked.append(ref[:, pl.ds(pl.multiple_of(home * block, block), block)])
    return jnp.concatenate(picked, axis=1)


def weight_rows(ref, block):
    rows = ref.shape[0] // 4
    if rows == block:
        return ref[...]
    return jnp.concatenate([ref[q * rows : q * rows + block, :] for q in range(4)], axis=0)


def pack_kernel(weight, users, first, second, third, held, sems):
    rows, width = weight.shape
    half = width // 2
    mine = (lax.axis_index("dp") % 2) * half
    copies = [pltpu.make_async_copy(users, held, sems.at[3])]
    for n, ((start, columns, _), out) in enumerate(zip(parts_of(half), (first, second, third))):
        at = pl.multiple_of(mine + start, 128)
        copies.append(
            pltpu.make_async_copy(
                weight.at[:, pl.ds(at, columns)], out.at[pl.ds(0, rows)], sems.at[n]
            )
        )
    for copy in copies:
        copy.start()
    for copy in copies:
        copy.wait()
    part = third.shape[1]
    wide = held[...].astype(F32)
    riding = [wide[:, j * part : (j + 1) * part] for j in range(width // part)]
    third[rows:, :] = jnp.concatenate(riding, axis=0).astype(BF16)


def forward_kernel(items, ints, context, residual, gain, *refs):
    stream, inverse, pooled, embedding = refs[12:]
    where = [ints[i] for i in range(4)]
    lengths, ids, counts = ([ints[4 + j * items + i] for i in range(items)] for j in range(3))
    positive = [ints[i] for i in range(4 + 3 * items, ints.shape[0])]
    tokens, width = residual.shape
    half = width // 2
    block = context.shape[1] // 8
    length = tokens // items
    for p, (start, columns, orders) in enumerate(parts_of(half)):
        lanes = [blocks_of(context, where, order, block) for order in orders]
        for side in range(2):
            base = where[3] * half if side == 0 else (1 - where[3]) * half
            stream[:, pl.ds(pl.multiple_of(base + start, 128), columns)] = sum(
                dot(lanes[k], weight_rows(refs[side * 6 + p * 2 + k], block)) for k in range(2)
            )
    for i in range(items):
        span = slice(i * length, (i + 1) * length)
        rows = stream[span, :] + residual[span, :].astype(F32)
        stream[span, :] = rows
        inv = lax.rsqrt(jnp.mean(rows * rows, axis=-1, keepdims=True) + EPSILON)
        inverse[i * length : (i + 1) * length, :] = inv
        position = lax.broadcasted_iota(jnp.int32, (length, 1), 0)
        kept = jnp.where(position < lengths[i], inv, 0.0)
        total = jnp.sum(rows * kept, axis=0, keepdims=True)
        pooled[i : i + 1, :] = total * gain[...] / lengths[i].astype(F32)
    pool = pooled[...]
    scale = lax.rsqrt(jnp.mean(pool * pool, axis=-1, keepdims=True) + EPSILON)
    embedding[:, :width] = (pool * scale).astype(BF16)
    row = lax.broadcasted_iota(jnp.int32, (items, LABELS), 0)
    lane = lax.broadcasted_iota(jnp.int32, (items, LABELS), 1)
    labels = jnp.zeros((items, LABELS), jnp.int32)
    for i in range(items):
        for at, value in enumerate((ids[i], counts[i] // 128, counts[i] % 128)):
            labels = jnp.where((row == i) & (lane == at), value, labels)
    for u in range(len(positive)):
        labels = jnp.where((row == 0) & (lane == POSITIVE + u), positive[u], labels)
    embedding[:, width:] = labels.astype(F32).astype(BF16)


def bit(value, k):
    return (value >> k) & 1


def one_hot_turn(rows, home):
    to = lax.broadcasted_iota(jnp.int32, (rows, rows), 0)
    of = lax.broadcasted_iota(jnp.int32, (rows, rows), 1)
    return jnp.where(to == home(of), 1.0, 0.0).astype(BF16)


def hold_kernel(source, out, sem):
    copy = pltpu.make_async_copy(source, out, sem)
    copy.start()
    copy.wait()


def users_kernel(users_here, block, where, *refs):
    piece_refs, (out, riders, sems) = refs[:4], refs[4:]
    x, y, core = where[0], where[1], where[3]
    people, width = out.shape
    stride, part = piece_refs[0].shape[0] // 4, piece_refs[0].shape[1]
    parts = width // part
    rode = parts * users_here
    copies = []
    for n in range(4):
        for b in range(4):
            copies.append(
                pltpu.make_async_copy(
                    piece_refs[n].at[pl.ds(b * stride + block, rode)],
                    riders.at[pl.ds((n * 4 + b) * rode, rode)],
                    sems.at[n * 4 + b],
                )
            )
    for copy in copies:
        copy.start()
    for copy in copies:
        copy.wait()

    def user_home(s):
        one = s // users_here
        ac, ay = core ^ bit(one, 3), (y // 2) ^ bit(one, 1)
        ax = x ^ bit(one, 2) ^ (3 * bit(one, 0))
        return ((ac * 2 + ay) * 4 + ax) * users_here + s % users_here

    wide = riders[...].astype(F32)
    placed = jnp.concatenate(
        [
            jnp.concatenate(
                [
                    wide[n * rode + j * users_here : n * rode + (j + 1) * users_here, :]
                    for n in range(16)
                ],
                axis=0,
            )
            for j in range(parts)
        ],
        axis=1,
    ).astype(BF16)
    out[...] = dot(one_hot_turn(people, user_home), placed).astype(BF16)

def loss_kernel(users_here, items_here, where, gain, users_ref, *refs):
    emb_refs = refs[:8]
    sums, user_grad, grads, emb_grads = refs[8:12], *refs[12:]
    x, y, z, core = where[0], where[1], where[2], where[3]
    group, full = emb_refs[0].shape
    width = full - LABELS
    items = 8 * group
    people = users_ref.shape[0]

    def item_home(s):
        one = s // items_here
        ax = x ^ bit(one, 0) ^ (3 * bit(one, 1))
        ay = y ^ bit(one, 2) ^ (3 * bit(one, 3))
        az = z ^ bit(one, 4) ^ (3 * bit(one, 5))
        ac = core ^ bit(one, 6)
        return (((ac * 4 + az) * 4 + ay) * 4 + ax) * items_here + s % items_here

    placed = jnp.concatenate([ref[...] for ref in emb_refs], axis=0)
    turned = dot(one_hot_turn(items, item_home), placed).astype(BF16)
    emb, labels = turned[:, :width], turned[:, width:]
    users = users_ref[...]
    person = lax.broadcasted_iota(jnp.int32, (people, items), 0)
    at = lax.broadcasted_iota(jnp.int32, (people, items), 1)
    g = person // users_here
    g_y = jnp.where((g // 4) % 2 == y // 2, y, 3 - y)
    g_row = (((g // 8 * 4 + z) * 4 + g_y) * 4 + g % 4) * items_here
    positives = dot(jnp.where(at == g_row, 1.0, 0.0).astype(BF16), labels)
    lane = lax.broadcasted_iota(jnp.int32, (people, LABELS), 1)
    slot = lax.broadcasted_iota(jnp.int32, (people, LABELS), 0) % users_here
    positive = jnp.sum(jnp.where(lane == POSITIVE + slot, positives, 0.0), axis=1, keepdims=True)
    item_labels = contract_rows(labels, one_hot_turn(items, lambda s: s))
    ids = item_labels[0:1, :]
    log_counts = jnp.log(item_labels[1:2, :] * 128.0 + item_labels[2:3, :])
    item = lax.broadcasted_iota(jnp.int32, (1, items), 1)
    chip = item // items_here
    index = linear(chip % 4, (chip // 4) % 4, (chip // 16) % 4, chip // 64) * items_here
    index = (index + item % items_here).astype(F32)
    onehot = index == positive
    positive_id = jnp.sum(jnp.where(onehot, ids, 0.0), axis=1, keepdims=True)
    excluded = (ids == positive_id) & jnp.logical_not(onehot)
    scores = contract_last(users, emb)
    logits = jnp.where(excluded, MASKED_FILL, scores - log_counts)
    row_max = jnp.max(logits, axis=1, keepdims=True)
    weights = jnp.where(excluded, 0.0, jnp.exp(logits - row_max))
    row_total = jnp.sum(weights, axis=1, keepdims=True)
    picked = jnp.sum(jnp.where(onehot, logits, 0.0), axis=1, keepdims=True)
    losses = row_max + jnp.log(row_total) - picked
    grad = (weights / row_total - jnp.where(onehot, 1.0, 0.0)).astype(BF16)
    grads[...] = grad.astype(F32)
    all_grads = contract_rows(grad, users)
    emb_grads[...] = all_grads
    emb_float = emb.astype(F32)
    product = emb_float * all_grads
    mean = jnp.mean(product, axis=-1, keepdims=True)
    gain_sum = jnp.sum(product - emb_float * emb_float * mean, axis=0, keepdims=True)
    line = lax.broadcasted_iota(jnp.int32, (8 * items_here, 1), 0)
    loss = jnp.broadcast_to(jnp.sum(losses, axis=0, keepdims=True), (1, width))
    for q in range(4):
        az = z ^ OFFSETS[q]
        start = ((core * 4 + az) * 4 + (y // 2) * 2) * 4 * items_here
        rows = emb_grads[pl.ds(pl.multiple_of(start, 8 * items_here), 8 * items_here), :]
        for other in range(2):
            for i in range(items_here):
                chosen = line == (((y % 2) ^ other) * 4 + x) * items_here + i
                n = other * items_here + i
                sums[q][n : n + 1, :] = jnp.sum(
                    jnp.where(chosen, rows, 0.0), axis=0, keepdims=True
                )
        sums[q][2 * items_here : 2 * items_here + 1, :] = gain_sum
        sums[q][2 * items_here + 1 :, :] = jnp.broadcast_to(loss, (6 - 2 * items_here + 1, width))
    place = ((core * 2 + y // 2) * 4 + x) * users_here
    own = grads[pl.ds(pl.multiple_of(place, users_here), users_here), :]
    user_grad[...] = dot(own.astype(BF16), emb).astype(BF16)


def residual_kernel(people, where, lengths, stream, inverse, pooled, gain, *refs):
    own_sums, other_sums, residual_grad, keep, send, gain_grad, loss = refs
    tokens, width = stream.shape
    half = width // 2
    items = lengths.shape[0]
    length = tokens // items
    for i in range(items):
        mine = own_sums[i : i + 1, :] + other_sums[items + i : items + i + 1, :]
        pool = pooled[i : i + 1, :]
        scale = lax.rsqrt(jnp.mean(pool * pool, axis=-1, keepdims=True) + EPSILON)
        pool_grad = scale * mine - pool * scale * scale * scale * jnp.mean(
            pool * mine, axis=-1, keepdims=True
        )
        row = gain[...] * pool_grad / lengths[i].astype(F32)
        span = slice(i * length, (i + 1) * length)
        rows = stream[span, :]
        inv = inverse[span, :]
        position = lax.broadcasted_iota(jnp.int32, (length, 1), 0)
        kept = jnp.where(position < lengths[i], inv, 0.0)
        mean = jnp.mean(rows * row, axis=-1, keepdims=True)
        residual_grad[span, :] = (kept * row - rows * (kept * inv * inv * mean)).astype(BF16)
    keep[...] = residual_grad[:, pl.ds(pl.multiple_of(where[3] * half, half), half)]
    send[...] = residual_grad[:, pl.ds(pl.multiple_of((1 - where[3]) * half, half), half)]
    at = 2 * items
    gain_grad[...] = (own_sums[at : at + 1, :] + other_sums[at : at + 1, :]) / gain[...]
    at = at + 1
    loss[...] = (own_sums[at : at + 1, 0:1] + other_sums[at : at + 1, 0:1]) / people


def context_kernel(where, keep, send, *refs):
    context_grad = refs[12]
    half = keep.shape[1]
    block = context_grad.shape[1] // 8
    values = {}
    for p, (start, columns, orders) in enumerate(parts_of(half)):
        for k, order in enumerate(orders):
            product = sum(
                contract_last(
                    grad[:, start : start + columns], weight_rows(refs[side * 6 + p * 2 + k], block)
                )
                for side, grad in enumerate((keep, send))
            )
            for b, place in enumerate(order):
                piece = product[:, b * block : (b + 1) * block]
                values[place] = values[place] + piece if place in values else piece
    for (q, ry), value in values.items():
        home = block_home(where[0], where[1] // 2, q, ry)
        context_grad[:, pl.ds(pl.multiple_of(home * block, block), block)] = value.astype(BF16)


def blocks_kernel(first_blocks, second_blocks, where, own_context, peer_context, own_grad, peer_grad, *outs):
    part = own_grad.shape[1] // 2
    block = own_context.shape[1] // 8
    outs = list(outs)
    for at, blocks in ((0, first_blocks), (part, second_blocks)):
        if not blocks:
            continue
        value = contract_rows(
            blocks_of(own_context, where, blocks, block), own_grad[:, at : at + part]
        ) + contract_rows(blocks_of(peer_context, where, blocks, block), peer_grad[:, at : at + part])
        done = 0
        while done < value.shape[0]:
            out = outs.pop(0)
            out[...] = value[done : done + out.shape[0]].astype(out.dtype)
            done += out.shape[0]


def shaped(shape, dtype=F32):
    return jax.ShapeDtypeStruct(shape, dtype)


def added(kept, sent, swap, bits):
    return kept + swap(sent.astype(BF16), bits).astype(F32)


def folded(value, swap, bits):
    rows = value.shape[0] // 2
    return added(value[:rows], value[rows:], swap, bits)


def all_added(value, swap, bits):
    value = lax.reduce_precision(value, 8, 7)
    return added(value, value, swap, bits)


def on_device(
    context, residual, out_weight, norm_gain, user_vectors, positive, item_ids, item_counts, lengths
):
    tokens, head = context.shape
    width = residual.shape[1]
    items_here = lengths.shape[0]
    users_here = user_vectors.shape[0]
    dp, fsdp = lax.axis_index("dp"), lax.axis_index("fsdp")
    y_lo, z, core = dp // 8, (dp // 2) % 4, dp % 2
    y_hi, x = fsdp // 4, fsdp % 4
    y = y_hi * 2 + y_lo
    where = jnp.stack([x, y, z, core]).astype(jnp.int32)
    half, part = width // 2, width // 4
    rows = out_weight.shape[0]
    gain = norm_gain[None, :]

    columns = [part_columns for _, part_columns, _ in parts_of(half)]
    rode = users_here * (width // columns[2])
    travel = pl.pallas_call(
        pack_kernel,
        out_shape=(
            shaped((rows, columns[0]), BF16),
            shaped((rows, columns[1]), BF16),
            shaped((rows + rode, columns[2]), BF16),
        ),
        in_specs=[ANY] * 2,
        out_specs=(VMEM,) * 3,
        scratch_shapes=[
            pltpu.VMEM((users_here, width), BF16),
            pltpu.SemaphoreType.DMA((4,)),
        ],
        compiler_params=params(6),
        name="pack",
    )(out_weight, user_vectors)
    steps = ((swap_y, 3), (swap_x, 1), (swap_x, 3))
    for step in range(2):
        turns = [steps[step], steps[step + 1], steps[(step + 2) % 3]]
        travel = [jnp.concatenate([v, swap(v, n)], axis=0) for v, (swap, n) in zip(travel, turns)]
        travel = lax.optimization_barrier(travel)
    arrived = [swap_x(travel[0], 3), swap_y(travel[1], 3), swap_x(travel[2], 1)]
    held = pl.pallas_call(
        hold_kernel,
        out_shape=shaped((tokens, width), BF16),
        in_specs=[HBM],
        out_specs=VMEM,
        scratch_shapes=[pltpu.SemaphoreType.DMA],
        compiler_params=params(6),
        name="hold",
    )(residual)
    arrived, held = lax.optimization_barrier((arrived, held))
    pieces = [piece for both in zip(travel, arrived) for piece in both]
    pieces = pieces + [swap_core(p) for p in pieces]
    ints, filled = 0, 0
    numbers = (where, lengths, item_ids, item_counts, positive)
    count = sum(v.shape[0] for v in numbers)
    for v in numbers:
        ints = ints + jnp.pad(v, (filled, count - filled - v.shape[0]))
        filled += v.shape[0]

    stream, inverse, pooled, emb = pl.pallas_call(
        functools.partial(forward_kernel, items_here),
        out_shape=(
            shaped((tokens, width)),
            shaped((tokens, 1)),
            shaped((items_here, width)),
            shaped((items_here, width + LABELS), BF16),
        ),
        in_specs=[SMEM] + [VMEM] * 15,
        out_specs=(VMEM,) * 4,
        compiler_params=params(16),
        name="forward",
    )(ints, context, held, gain, *pieces)

    emb = lax.optimization_barrier(jnp.concatenate(four(emb, swap_x), axis=0))
    peer_context = swap_core(after(context, emb))
    riding = pieces[4:6] + pieces[10:12]
    users = pl.pallas_call(
        functools.partial(users_kernel, users_here, rows),
        out_shape=shaped((16 * users_here, width), BF16),
        in_specs=[SMEM] + [ANY] * 4,
        out_specs=VMEM,
        scratch_shapes=[
            pltpu.VMEM((16 * rode, columns[2]), BF16),
            pltpu.SemaphoreType.DMA((16,)),
        ],
        compiler_params=params(10),
        name="users",
    )(where, *riding)
    emb, users = lax.optimization_barrier((jnp.concatenate(four(emb, swap_y), axis=0), users))
    emb_pieces = four(emb, swap_z)
    emb_pieces = emb_pieces + [swap_core(p) for p in emb_pieces]

    items, people = 128 * items_here, 16 * users_here
    *sums, user_grad = pl.pallas_call(
        functools.partial(loss_kernel, users_here, items_here),
        out_shape=(shaped((8, width)),) * 4 + (shaped((users_here, width), BF16),),
        in_specs=[SMEM] + [VMEM] * 10,
        out_specs=(VMEM,) * 5,
        scratch_shapes=[
            pltpu.VMEM((people, items), F32),
            pltpu.VMEM((items, width), F32),
        ],
        compiler_params=params(18),
        name="loss",
    )(where, gain, users, *emb_pieces)
    sums = [sums[0]] + [swap_z(sums[q], OFFSETS[q]) for q in (1, 2, 3)]
    sums = (sums[0] + sums[1]) + (sums[2] + sums[3])

    residual_grad, keep, send, gain_grad, loss = pl.pallas_call(
        functools.partial(residual_kernel, 8 * people),
        out_shape=(
            shaped((tokens, width), BF16),
            shaped((tokens, half), BF16),
            shaped((tokens, half), BF16),
            shaped((1, width)),
            shaped((1, 1)),
        ),
        in_specs=[SMEM, SMEM] + [VMEM] * 6,
        out_specs=(VMEM,) * 5,
        compiler_params=params(16),
        name="residual",
    )(where, lengths, stream, inverse, pooled, gain, sums, swap_y(sums, 1))
    peer_grad = swap_core(send)
    context_grad = pl.pallas_call(
        context_kernel,
        out_shape=shaped((tokens, head), BF16),
        in_specs=[SMEM] + [VMEM] * 14,
        out_specs=VMEM,
        compiler_params=params(14),
        name="context",
    )(where, keep, send, *pieces)

    def blocks(first_blocks, second_blocks, heights, dtype, operands, name):
        return pl.pallas_call(
            functools.partial(blocks_kernel, first_blocks, second_blocks),
            out_shape=tuple(shaped((height * rows, half // 2), dtype) for height in heights),
            in_specs=[SMEM] + [VMEM] * 4,
            out_specs=(VMEM,) * len(heights),
            compiler_params=params(14),
            name=name,
        )(where, *operands)

    def with_ry(ry):
        return [(q, ry) for q in range(4)]

    def with_q(*places):
        return [(q, ry) for q in places for ry in range(2)]

    operands = (context, peer_context, keep, peer_grad)
    (first_sent,) = blocks(with_ry(1), [], (4,), BF16, operands, "first_sent")
    first_sent, peer_grad = lax.optimization_barrier((first_sent, peer_grad))
    operands = (context, peer_context, keep, peer_grad)
    second_sent = blocks([], with_q(1, 2, 3), (2, 2, 2), BF16, operands, "second_sent")
    first, second = blocks(with_ry(0), with_q(0), (4, 2), F32, operands, "kept")
    arrived = [swap_y(first_sent, 3)] + [swap_x(second_sent[q - 1], OFFSETS[q]) for q in (1, 2, 3)]
    arrived, first, second, context_grad = lax.optimization_barrier(
        (arrived, first, second, context_grad)
    )
    first = first + arrived[0].astype(F32)
    for piece in arrived[1:]:
        second = second + piece.astype(F32)
    arrived = [swap_x(first[q * rows : (q + 1) * rows].astype(BF16), OFFSETS[q]) for q in (1, 2, 3)]
    second = folded(second, swap_y, 3)
    first = first[:rows]
    for piece in arrived:
        first = first + piece.astype(F32)
    first = all_added(first, swap_y, 1)
    second = all_added(second, swap_z, 1)
    first = all_added(first, swap_z, 1)
    second = all_added(second, swap_z, 3)
    first = all_added(first, swap_z, 3)
    second = all_added(second, swap_y, 1)
    halves = [first.astype(BF16), second.astype(BF16)]
    others = [swap_core(v) for v in halves]
    weight_grad = jnp.where(
        core == 0,
        jnp.concatenate(halves + others, axis=1),
        jnp.concatenate(others + halves, axis=1),
    )
    return (loss[0, 0], residual_grad, context_grad, weight_grad, gain_grad[0], user_grad)


def solution(mesh):
    placed = (
        P(AXES, None),
        P(AXES, None),
        P("fsdp", None),
        P(),
        P(AXES, None),
        P(AXES),
        P(AXES),
        P(AXES),
        P(AXES),
    )
    return jax.shard_map(
        on_device,
        mesh=mesh,
        in_specs=placed,
        out_specs=(P(), P(AXES, None), P(AXES, None), P("fsdp", None), P(), P(AXES, None)),
        check_vma=False,
    )
```
